32 devices in a mesh: grp: 2 (over x), lon: 16 (over z, y, core), lat: 1.
Axes of the slice: x: 2, y: 2, z: 4, core: 2. Of those that a mesh axis runs over, the one named last changes fastest.
Arguments:
- tokens: bfloat16 [4, 8, 128, 1536], P('grp', 'lat', 'lon'), parts along dimension 0, may hold values from -6 to 6
- land: int32 [16, 128], P(('grp', 'lat'), 'lon'), parts along dimension 0, may hold values 0 or 1
- surface: float32 [2, 1536], replicated, may hold values from -4 to 4
- gain: float32 [1536], replicated, may hold values from 0.25 to 1.75
- weights: bfloat16 [1536, 3072], P('lon'), may hold values from -0.15625 to 0.15625
- shifts: int32 [2, 2], replicated, may hold values from 1 to 7, as said below
- index_table: int32 [64, 64], replicated, may hold values from 0 to 224
- bias_table: float32 [2, 225, 12], P('lat'), as said below
- cotangent: bfloat16 [4, 8, 128, 1536], P('grp', 'lat', 'lon'), parts along dimension 0, may hold values from -6 to 6
Outputs:
- output: bfloat16 [4, 8, 128, 1536], P('grp', 'lat', 'lon'), parts along dimension 0
- grad_tokens: bfloat16 [4, 8, 128, 1536], P('grp', 'lat', 'lon'), parts along dimension 0
- grad_weights: float32 [3072, 3072], P(('grp', 'lon')), parts along dimension 0
The draws below stay inside these ranges and needn't reach their ends.
There are 2 independent parts, one for each index of `grp`. The reference program is written for one: setup_inputs(seed, part) draws one part's arguments, and reference() takes and returns one part's arrays. A program takes and returns all parts, laid end to end along the dimension named above; an argument that names none is the same for every part. Nothing has to cross between parts.
Inputs may be any that keep to these rules, and one draw needn't show every extreme that they name: `shifts`: row l holds level l's offsets along latitude and longitude; taken together the entries include 1 and 7. `bias_table`: every entry is finite.
All inputs are finite; a program needn't handle non-finite values. No bound on the sum of `land` on one device may be relied on, other than what follows from the above.
Results may differ from the reference program's by a relative error of at most 0.023.
Values may be sent and summed in bfloat16 or wider, within the bound.
No kernel may reach another device: no remote copies, remote signals or barrier semaphores. Data moves between devices by JAX's collectives and lax.ppermute only.
A program may use at most 128 MiB of HBM per device.

```python
import math
import jax
import jax.numpy as jnp
from jax import lax

D = 1536
HEADS = 12
HDIM = 64
WIN = 8
LVL = 2
CLON = 8
HD = 768
NREL = 225
NLAT = 8
NLON = 128
BANDS = 2
N_LON = 16
N_LAT = 1


def draw_shifts(key, part):
    count = 2 * LVL
    key_vals, key_order = jax.random.split(jax.random.fold_in(key, 5), 2)
    values = jax.random.randint(key_vals, (count,), 1, WIN)
    order = jax.random.permutation(key_order, count)
    values = values.at[order[0]].set(1)
    values = values.at[order[1]].set(WIN - 1)
    return values.reshape(LVL, 2).astype(jnp.int32)


def draw_bias_table(key, part):
    shape = (BANDS, NREL, HEADS)
    key_base = jax.random.fold_in(jax.random.fold_in(key, 11), 0)
    return jnp.clip(jax.random.normal(key_base, shape, jnp.float32), -4.0, 4.0)


def place_ends(drawn, stream_key, low, high):
    place = [jax.random.randint(jax.random.fold_in(stream_key, axis), (), 0, length) for axis, length in enumerate(drawn.shape)]
    widest = drawn.shape.index(max(drawn.shape))
    next_to = place[:widest] + [(place[widest] + 1) % drawn.shape[widest]] + place[widest + 1:]
    return drawn.at[tuple(place)].set(low).at[tuple(next_to)].set(high)


def block_levels(stream_key, extent, cuts, least, largest):
    level, own = 1.0, jax.random.fold_in(stream_key, 6)
    for dim, shards_of in cuts:
        draws = jnp.exp(jax.random.uniform(jax.random.fold_in(own, dim), (shards_of,), jnp.float32, least / len(cuts), largest / len(cuts)))
        level = level * jnp.repeat(draws, extent[dim] // shards_of).reshape([-1 if axis == dim else 1 for axis in range(len(extent))])
    return level


def normal_values(stream_key, shape, deviation, bound, cuts=(), held_as=jnp.bfloat16):
    entries = deviation * jax.random.normal(stream_key, shape, jnp.float32)
    if cuts:
        entries = entries * block_levels(stream_key, shape, cuts, -0.22, 0.18)
    return jnp.clip(entries, -bound, bound).astype(held_as)


def setup_inputs(seed: int = 0, part: int = 0) -> dict:
    key_list = jax.random.split(jax.random.key(seed), 10)
    part_splits = jax.random.split(jax.random.fold_in(key_list[9], part), 10)
    return {
        "tokens": normal_values(part_splits[0], (LVL, NLAT, NLON, D), 1.0, 6.0, ((2, 16),)),
        "land": place_ends((jax.random.randint(part_splits[1], (NLAT, NLON), 0, 10) < 3).astype(jnp.int32), jax.random.fold_in(part_splits[1], 1), 0, 1),
        "surface": normal_values(key_list[2], (2, D), 0.7, 4.0, (), jnp.float32),
        "gain": jnp.clip(1.0 + 0.15 * jax.random.normal(key_list[3], (D,), jnp.float32), 0.25, 1.75),
        "weights": normal_values(key_list[4], (D, 4 * HD), D ** -0.5, 0.15625, ((0, 16),)),
        "shifts": draw_shifts(jax.random.fold_in(key_list[9], 71), part),
        "index_table": place_ends(jax.random.randint(key_list[6], (WIN * WIN, WIN * WIN), 0, NREL), jax.random.fold_in(key_list[6], 1), 0, NREL - 1).astype(jnp.int32),
        "bias_table": draw_bias_table(jax.random.fold_in(key_list[9], 71), part),
        "cotangent": normal_values(part_splits[8], (LVL, NLAT, NLON, D), 1.0, 6.0, ((2, 16),)),
    }


epsilon = 1e-05

def rounded(values):
    return lax.optimization_barrier(values.astype(jnp.bfloat16)).astype(jnp.float32)

def normalize(stream, gain):
    values = stream.astype(jnp.float32)
    center = values - lax.optimization_barrier(jnp.mean(values, axis=-1, keepdims=True))
    spread = lax.rsqrt(lax.optimization_barrier(jnp.mean(center * center, axis=-1, keepdims=True)) + epsilon)
    return (center * spread * gain).astype(jnp.bfloat16)

def normalize_back(stream, gain, grad_normed):
    values = stream.astype(jnp.float32)
    center = values - lax.optimization_barrier(jnp.mean(values, axis=-1, keepdims=True))
    spread = lax.rsqrt(lax.optimization_barrier(jnp.mean(center * center, axis=-1, keepdims=True)) + epsilon)
    scaled = center * spread
    upstream = grad_normed.astype(jnp.float32) * gain
    return spread * (upstream - lax.optimization_barrier(jnp.mean(upstream, axis=-1, keepdims=True)) - scaled * lax.optimization_barrier(jnp.mean(upstream * scaled, axis=-1, keepdims=True)))

def roll_grid(field, shifts, sign):
    planes = []
    for level in range(field.shape[0]):
        planes.append(jnp.roll(field[level], (-sign * shifts[level, 0], -sign * shifts[level, 1]), axis=(0, 1)))
    return jnp.stack(planes)

def reference(tokens, land, surface, gain, weights, shifts, index_table, bias_table, cotangent):
    width = HEADS * HDIM
    area = WIN * WIN
    columns = NLON // WIN
    scale = 1.0 / math.sqrt(HDIM)
    surface_term = jnp.where(land[None, :, :, None] == 1, surface[1], surface[0])
    stream = (tokens.astype(jnp.float32) + surface_term).astype(jnp.bfloat16)
    normed = normalize(stream, gain)
    rolled = roll_grid(normed, shifts, 1)
    rolled_cot = roll_grid(cotangent, shifts, 1)
    w_qkv = weights[:, :3 * width]
    w_out = weights[:, 3 * width:]
    qkv = jnp.dot(rolled.reshape(-1, D), w_qkv, preferred_element_type=jnp.float32)
    view = rounded(qkv).reshape(LVL, N_LAT, WIN, columns, WIN, 3, HEADS, HDIM)
    query = view[:, :, :, :, :, 0]
    keys = view[:, :, :, :, :, 1]
    values = view[:, :, :, :, :, 2]
    six = (LVL, N_LAT, columns, HEADS, area, area)
    seven = (LVL, N_LAT, columns, HEADS, WIN, WIN, WIN, WIN)
    scores = jnp.einsum('liawbhd,licwehd->liwhabce', query, keys).reshape(six)
    onehot = (index_table[:, :, None] == jnp.arange(NREL, dtype=jnp.int32)).astype(jnp.float32)
    bias = jnp.einsum('qkr,srh->shqk', onehot, bias_table, precision=lax.Precision.HIGHEST)
    bias = bias.reshape(N_LAT, LVL, HEADS, area, area).transpose(1, 0, 2, 3, 4)
    rows = jnp.arange(NLAT, dtype=jnp.int32)
    group = rows[None, :] >= (NLAT - shifts[:, 0])[:, None]
    group = jnp.repeat(group.reshape(LVL, N_LAT, WIN), WIN, axis=2)
    allowed = group[:, :, :, None] == group[:, :, None, :]
    scores = scores * scale + bias[:, :, None]
    scores = jnp.where(allowed[:, :, None, None], scores, -1e+30)
    top = lax.optimization_barrier(jnp.max(scores, axis=-1, keepdims=True))
    expo = jnp.exp(scores - top)
    probs = expo / lax.optimization_barrier(jnp.sum(expo, axis=-1, keepdims=True))
    probs_b = rounded(probs).reshape(seven)
    mixed = jnp.einsum('liwhabce,licwehd->liawbhd', probs_b, values).astype(jnp.bfloat16)
    mixed_flat = mixed.reshape(-1, width)
    attended = jnp.dot(mixed_flat, w_out.T, preferred_element_type=jnp.float32).astype(jnp.bfloat16)
    attended = attended.reshape(LVL, NLAT, NLON, D)
    output = (stream.astype(jnp.float32) + roll_grid(attended, shifts, -1).astype(jnp.float32)).astype(jnp.bfloat16)
    cot_flat = rolled_cot.reshape(-1, D)
    grad_mixed = jnp.dot(cot_flat, w_out, preferred_element_type=jnp.float32)
    grad_mixed = rounded(grad_mixed).reshape(LVL, N_LAT, WIN, columns, WIN, HEADS, HDIM)
    grad_probs = jnp.einsum('liawbhd,licwehd->liwhabce', grad_mixed, values).reshape(six)
    grad_values = jnp.einsum('liwhabce,liawbhd->licwehd', probs_b, grad_mixed).astype(jnp.bfloat16)
    grad_scores = probs * (grad_probs - lax.optimization_barrier(jnp.sum(probs * grad_probs, axis=-1, keepdims=True)))
    grad_scores = rounded(grad_scores * scale).reshape(seven)
    grad_query = jnp.einsum('liwhabce,licwehd->liawbhd', grad_scores, keys).astype(jnp.bfloat16)
    grad_keys = jnp.einsum('liwhabce,liawbhd->licwehd', grad_scores, query).astype(jnp.bfloat16)
    grad_qkv = jnp.stack([grad_query, grad_keys, grad_values], axis=5).reshape(-1, 3 * width)
    grad_normed = jnp.dot(grad_qkv, w_qkv.T, preferred_element_type=jnp.float32).astype(jnp.bfloat16)
    grad_normed = roll_grid(grad_normed.reshape(LVL, NLAT, NLON, D), shifts, -1)
    grad_stream = normalize_back(stream, gain, grad_normed)
    grad_tokens = (cotangent.astype(jnp.float32) + grad_stream).astype(jnp.bfloat16)

    def split_tiles(field):
        return jnp.moveaxis(field.reshape(LVL, N_LAT, WIN, N_LON, CLON, -1), 3, 0)
    in_tiles = split_tiles(rolled)
    cot_tiles = split_tiles(rolled_cot)
    qkv_tiles = split_tiles(grad_qkv.reshape(LVL, NLAT, NLON, 3 * width))
    mixed_tiles = split_tiles(mixed_flat.reshape(LVL, NLAT, NLON, width))

    def add_tile(total, pieces):
        in_tile, cot_tile, qkv_tile, mixed_tile = pieces
        first = jnp.einsum('liacx,liacy->ixy', in_tile.astype(jnp.float32), qkv_tile.astype(jnp.float32))
        second = jnp.einsum('liacx,liacy->ixy', cot_tile.astype(jnp.float32), mixed_tile.astype(jnp.float32))
        part = rounded(jnp.concatenate([first, second], axis=2))
        return (total + lax.optimization_barrier(jnp.sum(part, axis=0)), None)
    total, _ = lax.scan(add_tile, jnp.zeros((D, 4 * width), jnp.float32), (in_tiles, cot_tiles, qkv_tiles, mixed_tiles))
    grad_weights = total * (1.0 / math.sqrt(LVL * NLAT * NLON))
    return (output, grad_tokens, grad_weights)
```

```python
import functools
import math

import jax
import jax.numpy as jnp
from jax import lax
from jax.experimental import pallas as pl
from jax.experimental.pallas import tpu as pltpu
from jax.sharding import Mesh
from jax.sharding import PartitionSpec as P

epsilon = 1e-05
LON = ("chip", "core")


def along_lon(shard, by):
    chips, cores = lax.axis_size("chip"), lax.axis_size("core")
    count = chips * cores
    return lax.ppermute(shard, LON, [(i, (i + by) % count) for i in range(count)])


def along_lat(shard, by):
    count = lax.axis_size("lat")
    return lax.ppermute(shard, "lat", [(i, (i + by) % count) for i in range(count)])


def swap_cores(shard):
    return lax.ppermute(shard, "core", [(0, 1), (1, 0)])


def pick(rows, cols, levels, side, over_rows):
    tile = levels * side * side
    shape = (tile, 2 * tile)
    target = lax.broadcasted_iota(jnp.int32, shape, 0)
    source = lax.broadcasted_iota(jnp.int32, shape, 1)
    level = target // (side * side)
    row = target // side % side
    col = target % side
    from_row = jnp.full_like(row, rows[levels - 1])
    from_col = jnp.full_like(col, cols[levels - 1])
    for l in range(levels - 1):
        from_row = jnp.where(level == l, rows[l], from_row)
        from_col = jnp.where(level == l, cols[l], from_col)
    from_row = row + from_row
    from_col = col + from_col
    which = (from_row if over_rows else from_col) // side
    wanted = which * tile + level * side * side + from_row % side * side + from_col % side
    return (source == wanted).astype(jnp.bfloat16)


def picked(onehot, first, second):
    both = jnp.concatenate([first, second], axis=0)
    return jnp.dot(onehot, both, preferred_element_type=jnp.float32).astype(jnp.bfloat16)


def roll_forward(field, shifts, levels, side):
    zeros = jnp.zeros_like(shifts[:, 0])
    rows = shifts[:, 0]
    if lax.axis_size("lat") > 1:
        field = picked(pick(rows, zeros, levels, side, True), field, along_lat(field, -1))
        rows = zeros
    return picked(pick(rows, shifts[:, 1], levels, side, False), field, along_lon(field, -1))


def roll_back(field, shifts, levels, side):
    zeros = jnp.zeros_like(shifts[:, 0])
    rows = side - shifts[:, 0]
    more = lax.axis_size("lat") > 1
    field = picked(
        pick(zeros if more else rows, side - shifts[:, 1], levels, side, False),
        along_lon(field, 1),
        field,
    )
    if more:
        field = picked(pick(rows, zeros, levels, side, True), along_lat(field, 1), field)
    return field


def middle_kernel(area, head, own_ref, other_ref, turned_ref, w_ref, bias_ref, gw_ref, mixed_ref, grad_ref, qkv_ref, gm_ref):
    tile, both = own_ref.shape
    width = both // 2
    part = w_ref.shape[1] // 4
    levels, pairs = bias_ref.shape[:2]
    scale = 1.0 / math.sqrt(head)
    for t, x_ref in enumerate((own_ref, other_ref)):
        rows = pl.ds(t * tile, tile)
        for n in range(3):
            cols = pl.ds(n * part, part)
            qkv_ref[rows, cols] = jnp.dot(
                x_ref[:, :width], w_ref[:, cols], preferred_element_type=jnp.float32
            ).astype(jnp.bfloat16)
        gm_ref[rows, :] = jnp.dot(
            x_ref[:, width:], w_ref[:, 3 * part :], preferred_element_type=jnp.float32
        ).astype(jnp.bfloat16)
    lane = lax.broadcasted_iota(jnp.int32, (area, 2 * head), 1)
    left = lane < head

    def stacked(pair):
        zero = jnp.zeros_like(pair)
        return jnp.concatenate([jnp.where(left, pair, zero), jnp.where(left, zero, pair)], axis=0)

    def unstacked(product):
        return jnp.where(left, product[:area], product[area:]).astype(jnp.bfloat16)

    def across(a, b):
        return lax.dot_general(a, b, (((1,), (1,)), ((), ())), preferred_element_type=jnp.float32)

    def down(a, b):
        return lax.dot_general(a, b, (((0,), (0,)), ((), ())), preferred_element_type=jnp.float32)

    for w in range(2 * tile // area):
        rows = pl.ds(w * area, area)
        for p in range(pairs):
            at = p * 2 * head
            q_cols, k_cols, v_cols = (pl.ds(n * part + at, 2 * head) for n in range(3))
            query = stacked(qkv_ref[rows, q_cols])
            keys = qkv_ref[rows, k_cols]
            values = qkv_ref[rows, v_cols]
            upstream = stacked(gm_ref[rows, q_cols])
            scores = across(query, keys) * scale + bias_ref[w % levels, p]
            expo = jnp.exp(scores - jnp.max(scores, axis=-1, keepdims=True))
            probs = expo / jnp.sum(expo, axis=-1, keepdims=True)
            probs_b = probs.astype(jnp.bfloat16)
            mixed_ref[rows, q_cols] = unstacked(
                jnp.dot(probs_b, values, preferred_element_type=jnp.float32)
            )
            grad_probs = across(upstream, values)
            grad_ref[rows, v_cols] = down(probs_b, upstream).astype(jnp.bfloat16)
            inner = jnp.sum(probs * grad_probs, axis=-1, keepdims=True)
            grad_scores = (probs * (grad_probs - inner) * scale).astype(jnp.bfloat16)
            grad_ref[rows, q_cols] = unstacked(
                jnp.dot(grad_scores, keys, preferred_element_type=jnp.float32)
            )
            grad_ref[rows, k_cols] = down(grad_scores, query).astype(jnp.bfloat16)
    for m in range(2):
        rows = pl.ds(m * (width // 2), width // 2)
        for n in range(3):
            cols = pl.ds(n * part, part)
            gw_ref[rows, cols] = jnp.dot(
                turned_ref[rows, :], grad_ref[:, cols], preferred_element_type=jnp.float32
            ).astype(jnp.bfloat16)
        lower = pl.ds(width + m * (width // 2), width // 2)
        gw_ref[rows, 3 * part :] = jnp.dot(
            turned_ref[lower, :], mixed_ref[...], preferred_element_type=jnp.float32
        ).astype(jnp.bfloat16)


def outer_kernel(mixed_ref, grad_ref, w_ref, own_ref, other_ref):
    tile = own_ref.shape[0]
    width = w_ref.shape[0]
    part = w_ref.shape[1] // 4
    step = width // 4
    for n in range(4):
        rows = pl.ds(n * step, step)
        for k, (x_ref, w_cols) in enumerate(((mixed_ref, pl.ds(3 * part, part)), (grad_ref, pl.ds(0, 3 * part)))):
            product = lax.dot_general(
                x_ref[...], w_ref[rows, w_cols], (((1,), (1,)), ((), ())), preferred_element_type=jnp.float32
            )
            cols = pl.ds(k * width + n * step, step)
            own_ref[:, cols] = product[:tile]
            other_ref[:, cols] = product[tile:].astype(jnp.bfloat16)


def on_device(tokens, land, surface, gain, weights, shifts, index_table, bias_table, cotangent):
    levels, side, _, width = tokens.shape
    area = side * side
    tile = levels * area
    heads = bias_table.shape[2]
    entries = bias_table.shape[1]
    own_rows = weights.shape[0]
    cores = lax.axis_size("core")
    part = weights.shape[1] // 4 // cores
    head = weights.shape[1] // 4 // heads
    own_heads = heads // cores
    core = lax.axis_index("core")
    first_core = core == 0

    halves = weights.reshape(own_rows, 4, cores, part)
    low = halves[:, :, 0].reshape(own_rows, 4 * part)
    high = halves[:, :, 1].reshape(own_rows, 4 * part)
    kept = jnp.where(first_core, low, high)
    came = swap_cores(jnp.where(first_core, high, low))
    chip_rows = jnp.concatenate(
        [jnp.where(first_core, kept, came), jnp.where(first_core, came, kept)], axis=0
    )
    w_own = lax.all_gather(chip_rows, "chip", axis=0, tiled=True)

    surface_term = jnp.where(land[None, :, :, None] == 1, surface[1], surface[0])
    stream = (tokens.astype(jnp.float32) + surface_term).astype(jnp.bfloat16).reshape(tile, width)
    flat_cot = cotangent.reshape(tile, width)
    values = stream.astype(jnp.float32)
    center = values - jnp.mean(values, axis=-1, keepdims=True)
    spread = lax.rsqrt(jnp.mean(center * center, axis=-1, keepdims=True) + epsilon)
    normed = (center * spread * gain).astype(jnp.bfloat16)
    own = roll_forward(jnp.concatenate([normed, flat_cot], axis=1), shifts, levels, side)
    other = swap_cores(own)
    turned = jnp.concatenate([own.T, other.T], axis=1)

    onehot = (index_table[:, :, None] == jnp.arange(entries, dtype=jnp.int32)).astype(jnp.float32)
    own_table = lax.dynamic_slice_in_dim(bias_table, core * own_heads, own_heads, 2)
    bias = jnp.einsum("qkr,lrh->lhqk", onehot, own_table, precision=lax.Precision.HIGHEST)
    row_number = lax.axis_index("lat") * side + jnp.arange(side, dtype=jnp.int32)
    group = row_number[None, :] >= (side * lax.axis_size("lat") - shifts[:, 0])[:, None]
    group = jnp.repeat(group, side, axis=1)
    allowed = group[:, :, None] == group[:, None, :]
    bias = jnp.where(allowed[:, None], bias, -1e30).reshape(levels, own_heads // 2, 2 * area, area)

    grad_tile, mixed, grad_qkv = pl.pallas_call(
        functools.partial(middle_kernel, area, head),
        out_shape=(
            jax.ShapeDtypeStruct((width, 4 * part), jnp.bfloat16),
            jax.ShapeDtypeStruct((2 * tile, part), jnp.bfloat16),
            jax.ShapeDtypeStruct((2 * tile, 3 * part), jnp.bfloat16),
        ),
        scratch_shapes=[
            pltpu.VMEM((2 * tile, 3 * part), jnp.bfloat16),
            pltpu.VMEM((2 * tile, part), jnp.bfloat16),
        ],
        compiler_params=pltpu.CompilerParams(vmem_limit_bytes=40 * 1024 * 1024),
        cost_estimate=pl.CostEstimate(
            flops=2 * 2 * 2 * tile * width * 4 * part, bytes_accessed=12_000_000, transcendentals=0
        ),
        name="attention",
    )(own, other, turned, w_own, bias)

    summed = lax.psum_scatter(grad_tile, "chip", scatter_dimension=0, tiled=True)

    attended_own, attended_other = pl.pallas_call(
        outer_kernel,
        out_shape=(
            jax.ShapeDtypeStruct((tile, 2 * width), jnp.float32),
            jax.ShapeDtypeStruct((tile, 2 * width), jnp.bfloat16),
        ),
        compiler_params=pltpu.CompilerParams(vmem_limit_bytes=40 * 1024 * 1024),
        cost_estimate=pl.CostEstimate(
            flops=2 * 2 * tile * width * 4 * part, bytes_accessed=8_000_000, transcendentals=0
        ),
        name="projections",
    )(mixed, grad_qkv, w_own)
    back = (attended_own + swap_cores(attended_other).astype(jnp.float32)).astype(jnp.bfloat16)
    back = roll_back(back, shifts, levels, side)
    output = (values + back[:, :width].astype(jnp.float32)).astype(jnp.bfloat16)
    scaled = center * spread
    upstream = back[:, width:].astype(jnp.float32) * gain
    grad_stream = spread * (
        upstream
        - jnp.mean(upstream, axis=-1, keepdims=True)
        - scaled * jnp.mean(upstream * scaled, axis=-1, keepdims=True)
    )
    grad_tokens = (flat_cot.astype(jnp.float32) + grad_stream).astype(jnp.bfloat16)

    summed = lax.psum(summed, "lat") if lax.axis_size("lat") > 1 else summed
    top, bottom = summed[:own_rows], summed[own_rows:]
    mine = jnp.where(first_core, top, bottom)
    theirs = swap_cores(jnp.where(first_core, bottom, top))
    token_count = tile * lax.axis_size("lat") * lax.axis_size("chip") * cores
    both = jnp.stack(
        [
            jnp.where(first_core, mine, theirs).reshape(own_rows, 4, part),
            jnp.where(first_core, theirs, mine).reshape(own_rows, 4, part),
        ],
        axis=2,
    )
    grad_weights = both.reshape(own_rows, -1).astype(jnp.float32) * (1.0 / math.sqrt(token_count))
    return (output.reshape(tokens.shape), grad_tokens.reshape(tokens.shape), grad_weights)


def solution(mesh):
    sizes = dict(mesh.shape)
    devices = mesh.devices.reshape(sizes["grp"], sizes["lon"] // 2, 2, sizes["lat"])
    finer = Mesh(devices, ("grp", "chip", "core", "lat"))
    return jax.shard_map(
        on_device,
        mesh=finer,
        in_specs=(
            P("grp", "lat", LON, None),
            P(("grp", "lat"), LON),
            P(),
            P(),
            P(LON, None),
            P(),
            P(),
            P("lat", None, None),
            P("grp", "lat", LON, None),
        ),
        out_specs=(
            P("grp", "lat", LON, None),
            P("grp", "lat", LON, None),
            P(("grp",) + LON, None),
        ),
        check_vma=False,
    )
```

```python
import functools
import math

import jax
import jax.numpy as jnp
from jax import lax
from jax.experimental import pallas as pl
from jax.experimental.pallas import tpu as pltpu
from jax.sharding import Mesh
from jax.sharding import PartitionSpec as P

epsilon = 1e-05
LON = ("far", "near", "side", "core")


def along_lon(shard, by):
    count = math.prod(lax.axis_size(axis) for axis in LON)
    return lax.ppermute(shard, LON, [(i, (i + by) % count) for i in range(count)])


def along_lat(shard, by):
    count = lax.axis_size("lat")
    return lax.ppermute(shard, "lat", [(i, (i + by) % count) for i in range(count)])


def swap(shard, axis):
    return lax.ppermute(shard, axis, [(0, 1), (1, 0)])


def pick(rows, cols, levels, side, over_rows):
    tile = levels * side * side
    shape = (tile, 2 * tile)
    target = lax.broadcasted_iota(jnp.int32, shape, 0)
    source = lax.broadcasted_iota(jnp.int32, shape, 1)
    level = target // (side * side)
    row = target // side % side
    col = target % side
    from_row = jnp.full_like(row, rows[levels - 1])
    from_col = jnp.full_like(col, cols[levels - 1])
    for l in range(levels - 1):
        from_row = jnp.where(level == l, rows[l], from_row)
        from_col = jnp.where(level == l, cols[l], from_col)
    from_row = row + from_row
    from_col = col + from_col
    which = (from_row if over_rows else from_col) // side
    wanted = which * tile + level * side * side + from_row % side * side + from_col % side
    return (source == wanted).astype(jnp.bfloat16)


def picked(onehot, first, second):
    both = jnp.concatenate([first, second], axis=0)
    return jnp.dot(onehot, both, preferred_element_type=jnp.float32).astype(jnp.bfloat16)


def roll_forward(field, shifts, levels, side):
    zeros = jnp.zeros_like(shifts[:, 0])
    rows = shifts[:, 0]
    if lax.axis_size("lat") > 1:
        field = picked(pick(rows, zeros, levels, side, True), field, along_lat(field, -1))
        rows = zeros
    return picked(pick(rows, shifts[:, 1], levels, side, False), field, along_lon(field, -1))


def roll_back(field, shifts, levels, side):
    zeros = jnp.zeros_like(shifts[:, 0])
    rows = side - shifts[:, 0]
    more = lax.axis_size("lat") > 1
    field = picked(
        pick(zeros if more else rows, side - shifts[:, 1], levels, side, False),
        along_lon(field, 1),
        field,
    )
    if more:
        field = picked(pick(rows, zeros, levels, side, True), along_lat(field, 1), field)
    return field


def attention_kernel(area, head, pieces, *refs):
    place_ref, normed_refs, cot_refs, bias_ref = refs[0], refs[1:3], refs[3:5], refs[5]
    piece_refs = refs[6 : 6 + pieces]
    grad_ref, full_ref, w_ref, qkv_ref, gm_ref, sems, out_sem = refs[6 + pieces :]
    tile = normed_refs[0].shape[0]
    part = w_ref.shape[1] // 4
    levels, pairs = bias_ref.shape[:2]
    scale = 1.0 / math.sqrt(head)
    copies = []
    for i, piece in enumerate(piece_refs):
        rows = pl.ds(pl.multiple_of(place_ref[i] * piece.shape[0], 16), piece.shape[0])
        copies.append(pltpu.make_async_copy(piece, w_ref.at[rows, :], sems.at[i]))
        copies[-1].start()
    for copy in copies:
        copy.wait()
    out_copy = pltpu.make_async_copy(w_ref, full_ref, out_sem)
    out_copy.start()
    for t in range(2):
        rows = pl.ds(t * tile, tile)
        for n in range(3):
            cols = pl.ds(n * part, part)
            qkv_ref[rows, cols] = jnp.dot(
                normed_refs[t][...], w_ref[:, cols], preferred_element_type=jnp.float32
            ).astype(jnp.bfloat16)
        gm_ref[rows, :] = jnp.dot(
            cot_refs[t][...], w_ref[:, 3 * part :], preferred_element_type=jnp.float32
        ).astype(jnp.bfloat16)
    lane = lax.broadcasted_iota(jnp.int32, (area, 2 * head), 1)
    left = lane < head

    def stacked(pair):
        zero = jnp.zeros_like(pair)
        return jnp.concatenate([jnp.where(left, pair, zero), jnp.where(left, zero, pair)], axis=0)

    def unstacked(product):
        return jnp.where(left, product[:area], product[area:]).astype(jnp.bfloat16)

    def across(a, b):
        return lax.dot_general(a, b, (((1,), (1,)), ((), ())), preferred_element_type=jnp.float32)

    def down(a, b):
        return lax.dot_general(a, b, (((0,), (0,)), ((), ())), preferred_element_type=jnp.float32)

    for w in range(2 * tile // area):
        rows = pl.ds(w * area, area)
        for p in range(pairs):
            at = p * 2 * head
            q_cols, k_cols, v_cols, m_cols = (pl.ds(n * part + at, 2 * head) for n in range(4))
            query = stacked(qkv_ref[rows, q_cols])
            keys = qkv_ref[rows, k_cols]
            values = qkv_ref[rows, v_cols]
            upstream = stacked(gm_ref[rows, q_cols])
            scores = across(query, keys) * scale + bias_ref[w % levels, p]
            expo = jnp.exp(scores - jnp.max(scores, axis=-1, keepdims=True))
            probs = expo / jnp.sum(expo, axis=-1, keepdims=True)
            probs_b = probs.astype(jnp.bfloat16)
            grad_ref[rows, m_cols] = unstacked(
                jnp.dot(probs_b, values, preferred_element_type=jnp.float32)
            )
            grad_probs = across(upstream, values)
            grad_ref[rows, v_cols] = down(probs_b, upstream).astype(jnp.bfloat16)
            inner = jnp.sum(probs * grad_probs, axis=-1, keepdims=True)
            grad_scores = (probs * (grad_probs - inner) * scale).astype(jnp.bfloat16)
            grad_ref[rows, q_cols] = unstacked(
                jnp.dot(grad_scores, keys, preferred_element_type=jnp.float32)
            )
            grad_ref[rows, k_cols] = down(grad_scores, query).astype(jnp.bfloat16)
    out_copy.wait()


def weights_kernel(turned_ref, own_ref, other_ref, *out_refs):
    rows, columns = out_refs[0].shape
    tokens = own_ref.shape[0]
    part = columns // 2
    for i in range(len(out_refs) // 2):
        for n in range(4):
            cols = pl.ds(n * part, part)
            kind = 1 if n == 3 else 0
            at = pl.ds(i * rows, rows)
            out_refs[2 * i + n // 2][:, pl.ds(n % 2 * part, part)] = (
                jnp.dot(turned_ref[kind, at, :tokens], own_ref[:, cols], preferred_element_type=jnp.float32)
                + jnp.dot(turned_ref[kind, at, tokens:], other_ref[:, cols], preferred_element_type=jnp.float32)
            ).astype(jnp.bfloat16)


def outer_kernel(grad_ref, w_ref, own_ref, other_ref):
    tile = own_ref.shape[0]
    width = w_ref.shape[0]
    part = w_ref.shape[1] // 4
    step = width // 4
    for n in range(4):
        rows = pl.ds(n * step, step)
        for k, w_cols in enumerate((pl.ds(3 * part, part), pl.ds(0, 3 * part))):
            product = lax.dot_general(
                grad_ref[:, w_cols], w_ref[rows, w_cols], (((1,), (1,)), ((), ())), preferred_element_type=jnp.float32
            )
            cols = pl.ds(k * width + n * step, step)
            own_ref[:, cols] = product[:tile]
            other_ref[:, cols] = product[tile:].astype(jnp.bfloat16)


def on_device(tokens, land, surface, gain, weights, shifts, index_table, bias_table, cotangent):
    levels, side, _, width = tokens.shape
    area = side * side
    tile = levels * area
    heads = bias_table.shape[2]
    entries = bias_table.shape[1]
    own_rows = weights.shape[0]
    part = weights.shape[1] // 8
    head = weights.shape[1] // 4 // heads
    own_heads = heads // 2
    far, near, beside, core = (lax.axis_index(axis) for axis in LON)
    grp = lax.axis_index("grp")
    first = near == 0
    f32 = jnp.float32

    def place(f, n, s, c):
        return ((far ^ f) * 4 + (near ^ n) * 2 + (beside ^ s)) * 2 + (core ^ c)

    halves = weights.reshape(own_rows, 4, 2, part)
    low = halves[:, :, 0].reshape(own_rows, 4 * part)
    high = halves[:, :, 1].reshape(own_rows, 4 * part)
    mine = jnp.where(first, low, high)
    came = swap(jnp.where(first, high, low), "near")
    flat_cot = cotangent.reshape(tile, width)
    surface_term = jnp.where(land[None, :, :, None] == 1, surface[1], surface[0])
    stream = (tokens.astype(f32) + surface_term).astype(jnp.bfloat16).reshape(tile, width)
    values = stream.astype(f32)
    center = values - jnp.mean(values, axis=-1, keepdims=True)
    spread = lax.rsqrt(jnp.mean(center * center, axis=-1, keepdims=True) + epsilon)
    normed = (center * spread * gain).astype(jnp.bfloat16)

    first_grp = grp == 0
    across_far = swap(jnp.where(first_grp, mine, came), "far")
    other_half = jnp.where(first_grp, 1, 0)
    far_side = swap(across_far, "side")
    found = [
        (mine, 0, 0, 0),
        (came, 0, 1, 0),
        (swap(mine, "side"), 0, 0, 1),
        (swap(came, "side"), 0, 1, 1),
        (across_far, 1, 1 - other_half, 0),
        (swap(across_far, "grp"), 1, other_half, 0),
        (far_side, 1, 1 - other_half, 1),
        (swap(far_side, "grp"), 1, other_half, 1),
    ]
    pieces = [piece for piece, *_ in found] + [swap(piece, "core") for piece, *_ in found]
    places = jnp.stack([place(f, n, s, c) for c in (0, 1) for _, f, n, s in found]).astype(jnp.int32)

    own_cot = roll_forward(flat_cot, shifts, levels, side)
    other_cot = swap(own_cot, "near")
    own_normed = roll_forward(normed, shifts, levels, side)
    other_normed = swap(own_normed, "near")

    def turned(own, other):
        both = jnp.concatenate([own, other], axis=0)
        full = jnp.concatenate([both, swap(both, "core")], axis=0).T
        blocks = full.reshape(-1, own_rows, full.shape[1])
        return jnp.concatenate(
            [
                lax.dynamic_index_in_dim(blocks, place(f, n, s, 0), 0, keepdims=False)
                for f in (1, 0)
                for s in (1, 0)
                for n in (1, 0)
            ],
            axis=0,
        )

    turned_both = jnp.stack([turned(own_normed, other_normed), turned(own_cot, other_cot)])

    onehot = (index_table[:, :, None] == jnp.arange(entries, dtype=jnp.int32)).astype(f32)
    own_table = lax.dynamic_slice_in_dim(bias_table, near * own_heads, own_heads, 2)
    bias = jnp.einsum("qkr,lrh->lhqk", onehot, own_table, precision=lax.Precision.HIGHEST)
    row_number = lax.axis_index("lat") * side + jnp.arange(side, dtype=jnp.int32)
    group = row_number[None, :] >= (side * lax.axis_size("lat") - shifts[:, 0])[:, None]
    group = jnp.repeat(group, side, axis=1)
    allowed = group[:, :, None] == group[:, None, :]
    bias = jnp.where(allowed[:, None], bias, -1e30).reshape(levels, own_heads // 2, 2 * area, area)

    vmem = pl.BlockSpec(memory_space=pltpu.VMEM)
    anywhere = pl.BlockSpec(memory_space=pl.ANY)
    grad, w_full = pl.pallas_call(
        functools.partial(attention_kernel, area, head, len(pieces)),
        out_shape=(
            jax.ShapeDtypeStruct((2 * tile, 4 * part), jnp.bfloat16),
            jax.ShapeDtypeStruct((width, 4 * part), jnp.bfloat16),
        ),
        in_specs=[pl.BlockSpec(memory_space=pltpu.SMEM)] + [vmem] * 5 + [anywhere] * len(pieces),
        out_specs=(vmem, anywhere),
        scratch_shapes=[
            pltpu.VMEM((width, 4 * part), jnp.bfloat16),
            pltpu.VMEM((2 * tile, 3 * part), jnp.bfloat16),
            pltpu.VMEM((2 * tile, part), jnp.bfloat16),
            pltpu.SemaphoreType.DMA((len(pieces),)),
            pltpu.SemaphoreType.DMA,
        ],
        compiler_params=pltpu.CompilerParams(vmem_limit_bytes=32 * 1024 * 1024),
        cost_estimate=pl.CostEstimate(flops=2_400_000_000, bytes_accessed=12_000_000, transcendentals=0),
        name="attention",
    )(places, own_normed, other_normed, own_cot, other_cot, bias, *pieces)

    blocks = pl.pallas_call(
        weights_kernel,
        out_shape=[jax.ShapeDtypeStruct((own_rows, 2 * part), jnp.bfloat16)] * 16,
        compiler_params=pltpu.CompilerParams(vmem_limit_bytes=32 * 1024 * 1024),
        cost_estimate=pl.CostEstimate(flops=2_400_000_000, bytes_accessed=6_000_000, transcendentals=0),
        name="weight_gradient",
    )(turned_both, grad, swap(grad, "core"))

    def block(f, s, n, h):
        return blocks[(((1 - f) * 2 + 1 - s) * 2 + 1 - n) * 2 + h]

    order = [(1, 0), (1, 1), (0, 0), (0, 1)]
    arrived = {}
    for n, h in order:
        added = block(1, 0, n, h).astype(f32) + swap(block(1, 1, n, h), "side").astype(f32)
        arrived[n, h] = swap(added.astype(jnp.bfloat16), "far")
    total = {}
    for n, h in order:
        total[n, h] = (
            block(0, 0, n, h).astype(f32)
            + swap(block(0, 1, n, h), "side").astype(f32)
            + arrived[n, h].astype(f32)
        )

    attended_own, attended_other = pl.pallas_call(
        outer_kernel,
        out_shape=(
            jax.ShapeDtypeStruct((tile, 2 * width), f32),
            jax.ShapeDtypeStruct((tile, 2 * width), jnp.bfloat16),
        ),
        compiler_params=pltpu.CompilerParams(vmem_limit_bytes=32 * 1024 * 1024),
        cost_estimate=pl.CostEstimate(flops=1_200_000_000, bytes_accessed=8_000_000, transcendentals=0),
        name="projections",
    )(grad, w_full)
    back = (attended_own + swap(attended_other, "near").astype(f32)).astype(jnp.bfloat16)
    back = roll_back(back, shifts, levels, side)
    output = (values + back[:, :width].astype(f32)).astype(jnp.bfloat16)
    scaled = center * spread
    upstream = back[:, width:].astype(f32) * gain
    grad_stream = spread * (
        upstream
        - jnp.mean(upstream, axis=-1, keepdims=True)
        - scaled * jnp.mean(upstream * scaled, axis=-1, keepdims=True)
    )
    grad_tokens = (flat_cot.astype(f32) + grad_stream).astype(jnp.bfloat16)

    theirs = [swap(total[1, h].astype(jnp.bfloat16), "near").astype(f32) for h in (0, 1)]
    token_count = tile * lax.axis_size("lat") * math.prod(lax.axis_size(axis) for axis in LON)
    columns = []
    for h in (0, 1):
        for k in (0, 1):
            kept = total[0, h][:, k * part : (k + 1) * part]
            other = theirs[h][:, k * part : (k + 1) * part]
            columns += [jnp.where(first, kept, other), jnp.where(first, other, kept)]
    summed = jnp.concatenate(columns, axis=1)
    if lax.axis_size("lat") > 1:
        summed = lax.psum(summed.astype(jnp.bfloat16), "lat").astype(f32)
    grad_weights = summed * (1.0 / math.sqrt(token_count))
    return (output.reshape(tokens.shape), grad_tokens.reshape(tokens.shape), grad_weights)


def solution(mesh):
    sizes = dict(mesh.shape)
    devices = mesh.devices.reshape(sizes["grp"], sizes["lon"] // 8, 2, 2, 2, sizes["lat"])
    finer = Mesh(devices, ("grp",) + LON + ("lat",))
    return jax.shard_map(
        on_device,
        mesh=finer,
        in_specs=(
            P("grp", "lat", LON, None),
            P(("grp", "lat"), LON),
            P(),
            P(),
            P(LON, None),
            P(),
            P(),
            P("lat", None, None),
            P("grp", "lat", LON, None),
        ),
        out_specs=(
            P("grp", "lat", LON, None),
            P("grp", "lat", LON, None),
            P(("grp",) + LON, None),
        ),
        check_vma=False,
    )
```

```python
import functools
import math

import jax
import jax.numpy as jnp
from jax import lax
from jax.experimental import pallas as pl
from jax.experimental.pallas import tpu as pltpu
from jax.sharding import Mesh
from jax.sharding import PartitionSpec as P

epsilon = 1e-05
LON = ("far", "near", "side", "core")


def along_lon(shard, by):
    count = math.prod(lax.axis_size(axis) for axis in LON)
    return lax.ppermute(shard, LON, [(i, (i + by) % count) for i in range(count)])


def along_lat(shard, by):
    count = lax.axis_size("lat")
    return lax.ppermute(shard, "lat", [(i, (i + by) % count) for i in range(count)])


def swap(shard, axis):
    return lax.ppermute(shard, axis, [(0, 1), (1, 0)])


def pick(rows, cols, levels, side, over_rows):
    tile = levels * side * side
    shape = (tile, 2 * tile)
    target = lax.broadcasted_iota(jnp.int32, shape, 0)
    source = lax.broadcasted_iota(jnp.int32, shape, 1)
    level = target // (side * side)
    row = target // side % side
    col = target % side
    from_row = jnp.full_like(row, rows[levels - 1])
    from_col = jnp.full_like(col, cols[levels - 1])
    for l in range(levels - 1):
        from_row = jnp.where(level == l, rows[l], from_row)
        from_col = jnp.where(level == l, cols[l], from_col)
    from_row = row + from_row
    from_col = col + from_col
    which = (from_row if over_rows else from_col) // side
    wanted = which * tile + level * side * side + from_row % side * side + from_col % side
    return (source == wanted).astype(jnp.bfloat16)


def picked(onehot, first, second):
    both = jnp.concatenate([first, second], axis=0)
    return jnp.dot(onehot, both, preferred_element_type=jnp.float32).astype(jnp.bfloat16)


def roll_back(field, shifts, levels, side):
    zeros = jnp.zeros_like(shifts[:, 0])
    rows = side - shifts[:, 0]
    more = lax.axis_size("lat") > 1
    field = picked(
        pick(zeros if more else rows, side - shifts[:, 1], levels, side, False),
        along_lon(field, 1),
        field,
    )
    if more:
        field = picked(pick(rows, zeros, levels, side, True), along_lat(field, 1), field)
    return field


def turned_rolls(info_ref, *refs):
    fields, (kept_ref, sent_ref, both_ref, turned_ref, sems) = refs[:4], refs[4:]
    tile = fields[0].shape[0]
    rows = kept_ref.shape[1] // 8
    levels, side = 2, 8
    area = tile // levels
    copies = [
        pltpu.make_async_copy(field, both_ref.at[i // 2, pl.ds(i % 2 * tile, tile), :], sems.at[i])
        for i, field in enumerate(fields)
    ]
    for copy in copies:
        copy.start()
    target = lax.broadcasted_iota(jnp.int32, (tile, 2 * tile), 0)
    source = lax.broadcasted_iota(jnp.int32, (tile, 2 * tile), 1)
    upper = target < area
    row = ((target >> 3) & 7) + jnp.where(upper, info_ref[0], info_ref[2])
    col = (target & 7) + jnp.where(upper, info_ref[1], info_ref[3])
    wanted = jnp.where(col >= side, tile, 0) + jnp.where(upper, 0, area) + (row & 7) * side + (col & 7)
    onehot = jnp.where(source == wanted, 1.0, 0.0).astype(jnp.bfloat16)
    for k in (1, 0):
        copies[2 * k].wait()
        copies[2 * k + 1].wait()
        rolled = jnp.dot(onehot, both_ref[k], preferred_element_type=jnp.float32)
        turned_ref[...] = rolled.T.astype(jnp.bfloat16)
        for i in range(8):
            at = pl.ds(i * rows, rows)
            kept_ref[k, at, :] = turned_ref[pl.ds(pl.multiple_of(info_ref[4 + i] * rows, 16), rows), :]
            sent_ref[k, at, :] = turned_ref[pl.ds(pl.multiple_of(info_ref[12 + i] * rows, 16), rows), :]


def down(a, b):
    return lax.dot_general(a, b, (((0,), (0,)), ((), ())), preferred_element_type=jnp.float32)


def across(a, b):
    return lax.dot_general(a, b, (((1,), (1,)), ((), ())), preferred_element_type=jnp.float32)


def products_kernel(place_ref, *refs):
    tiles, pieces = refs[:4], refs[4:12]
    kept_ref, sent_ref, full_ref, tile_ref, w_ref, sems, out_sem = refs[12:]
    tile = tiles[0].shape[2]
    part = w_ref.shape[1] // 4
    copies = []
    for i, piece in enumerate(pieces):
        rows = pl.ds(pl.multiple_of(place_ref[i] * piece.shape[0], 16), piece.shape[0])
        copies.append(pltpu.make_async_copy(piece, w_ref.at[rows, :], sems.at[i]))
    for j, source in enumerate(tiles):
        copies.append(pltpu.make_async_copy(source, tile_ref.at[j], sems.at[8 + j]))
    for copy in copies:
        copy.start()
    for copy in copies:
        copy.wait()
    out_copy = pltpu.make_async_copy(w_ref, full_ref, out_sem)
    out_copy.start()
    for j in (1, 3, 0, 2):
        rows = pl.ds(j // 2 * tile, tile)
        for n in range(4):
            cols = pl.ds(n * part, part)
            product = down(tile_ref[j, n // 3], w_ref[:, cols])
            if j % 2:
                sent_ref[rows, cols] = product.astype(jnp.bfloat16)
            else:
                kept_ref[rows, cols] = product
    out_copy.wait()


def attention_kernel(area, head, kept_ref, came_ref, bias_ref, grad_ref, qkv_ref):
    part = grad_ref.shape[1] // 4
    levels, pairs = bias_ref.shape[:2]
    scale = 1.0 / math.sqrt(head)
    lane = lax.broadcasted_iota(jnp.int32, (area, 2 * head), 1)
    left = lane < head

    def stacked(pair):
        zero = jnp.zeros_like(pair)
        return jnp.concatenate([jnp.where(left, pair, zero), jnp.where(left, zero, pair)], axis=0)

    def unstacked(product):
        return jnp.where(left, product[:area], product[area:]).astype(jnp.bfloat16)

    qkv_ref[...] = (kept_ref[...] + came_ref[...].astype(jnp.float32)).astype(jnp.bfloat16)
    for w in range(grad_ref.shape[0] // area):
        rows = pl.ds(w * area, area)
        for p in range(pairs):
            q_cols, k_cols, v_cols, m_cols = (pl.ds(n * part + p * 2 * head, 2 * head) for n in range(4))
            query = stacked(qkv_ref[rows, q_cols])
            keys = qkv_ref[rows, k_cols]
            values = qkv_ref[rows, v_cols]
            upstream = stacked(qkv_ref[rows, m_cols])
            scores = across(query, keys) * scale + bias_ref[w % levels, p]
            expo = jnp.exp(scores - jnp.max(scores, axis=-1, keepdims=True))
            probs = expo / jnp.sum(expo, axis=-1, keepdims=True)
            probs_b = probs.astype(jnp.bfloat16)
            grad_ref[rows, m_cols] = unstacked(
                jnp.dot(probs_b, values, preferred_element_type=jnp.float32)
            )
            grad_probs = across(upstream, values)
            grad_ref[rows, v_cols] = down(probs_b, upstream).astype(jnp.bfloat16)
            inner = jnp.sum(probs * grad_probs, axis=-1, keepdims=True)
            grad_scores = (probs * (grad_probs - inner) * scale).astype(jnp.bfloat16)
            grad_ref[rows, q_cols] = unstacked(
                jnp.dot(grad_scores, keys, preferred_element_type=jnp.float32)
            )
            grad_ref[rows, k_cols] = down(grad_scores, query).astype(jnp.bfloat16)


def weights_kernel(near_ref, *refs):
    tiles, (own_ref, other_ref), out_refs = refs[:4], refs[4:6], refs[6:14]
    tile_ref, sum_ref, sems = refs[14:]
    tile = tiles[0].shape[2]
    part = own_ref.shape[1] // 4
    rows = out_refs[0].shape[0]
    copies = [pltpu.make_async_copy(source, tile_ref.at[j], sems.at[j]) for j, source in enumerate(tiles)]
    for copy in copies:
        copy.start()
    for copy in copies:
        copy.wait()
    for n in range(4):
        cols = pl.ds(n * part, part)
        total = None
        for t in range(2):
            tokens = pl.ds(t * tile, tile)
            left = jnp.concatenate([tile_ref[2 * t, n // 3], tile_ref[2 * t + 1, n // 3]], axis=1)
            right = jnp.concatenate([own_ref[tokens, cols], other_ref[tokens, cols]], axis=0)
            product = jnp.dot(left, right, preferred_element_type=jnp.float32)
            total = product if total is None else total + product
        sum_ref[:, cols] = total.astype(jnp.bfloat16)
    near = near_ref[0]
    for i, out_ref in enumerate(out_refs):
        wanted = 1 - near if i % 2 == 0 else near
        out_ref[...] = sum_ref[pl.ds(pl.multiple_of((i // 2 * 2 + wanted) * rows, 16), rows), :]


def outer_kernel(place_ref, grad_ref, mine_ref, theirs_ref, own_ref, other_ref, w_ref, sems):
    tile = own_ref.shape[0]
    width = w_ref.shape[0]
    rows = width // 16
    part = w_ref.shape[1] // 4
    step = width // 4
    copies = []
    for i in range(16):
        source = (mine_ref if i < 8 else theirs_ref).at[pl.ds(i % 8 * rows, rows), :]
        into = w_ref.at[pl.ds(pl.multiple_of(place_ref[i] * rows, 16), rows), :]
        copies.append(pltpu.make_async_copy(source, into, sems.at[i]))
    for copy in copies:
        copy.start()
    for copy in copies:
        copy.wait()
    for n in range(4):
        at = pl.ds(n * step, step)
        for k, w_cols in enumerate((pl.ds(3 * part, part), pl.ds(0, 3 * part))):
            product = across(grad_ref[:, w_cols], w_ref[at, w_cols])
            cols = pl.ds(k * width + n * step, step)
            own_ref[:, cols] = product[:tile]
            other_ref[:, cols] = product[tile:].astype(jnp.bfloat16)


def after(value, earlier):
    return lax.optimization_barrier((value, earlier))[0]


def kernel_call(body, outs, in_specs, out_specs, scratch, flops, moved, name):
    return pl.pallas_call(
        body,
        out_shape=outs,
        in_specs=in_specs,
        out_specs=out_specs,
        scratch_shapes=scratch,
        compiler_params=pltpu.CompilerParams(vmem_limit_bytes=32 * 1024 * 1024),
        cost_estimate=pl.CostEstimate(flops=flops, bytes_accessed=moved, transcendentals=0),
        name=name,
    )


def on_device(tokens, land, surface, gain, weights, shifts, index_table, bias_table, cotangent):
    levels, side, _, width = tokens.shape
    area = side * side
    tile = levels * area
    heads = bias_table.shape[2]
    entries = bias_table.shape[1]
    own_rows = weights.shape[0]
    part = weights.shape[1] // 8
    head = weights.shape[1] // 4 // heads
    own_heads = heads // 2
    far, near, beside, core = (lax.axis_index(axis) for axis in LON)
    grp = lax.axis_index("grp")
    first = near == 0
    f32 = jnp.float32

    def place(f, n, s, c):
        return ((far ^ f) * 4 + (near ^ n) * 2 + (beside ^ s)) * 2 + (core ^ c)

    low = jnp.concatenate([weights[:, 2 * k * part : (2 * k + 1) * part] for k in range(4)], axis=1)
    high = jnp.concatenate([weights[:, (2 * k + 1) * part : (2 * k + 2) * part] for k in range(4)], axis=1)
    mine = jnp.where(first, low, high)
    came = swap(jnp.where(first, high, low), "near")
    flat_cot = cotangent.reshape(tile, width)
    surface_term = jnp.where(land[None, :, :, None] == 1, surface[1], surface[0])
    stream = (tokens.astype(f32) + surface_term).astype(jnp.bfloat16).reshape(tile, width)
    values = stream.astype(f32)
    center = values - jnp.mean(values, axis=-1, keepdims=True)
    spread = lax.rsqrt(jnp.mean(center * center, axis=-1, keepdims=True) + epsilon)
    normed = (center * spread * gain).astype(jnp.bfloat16)

    first_grp = grp == 0
    across_far = swap(jnp.where(first_grp, mine, came), "far")
    far_side = swap(across_far, "side")
    held = near ^ grp
    pieces = [
        (mine, 0, 0, near),
        (came, 0, 0, 1 - near),
        (swap(after(mine, came), "side"), 0, 1, near),
        (swap(came, "side"), 0, 1, 1 - near),
        (across_far, 1, 0, held),
        (swap(across_far, "grp"), 1, 0, 1 - held),
        (far_side, 1, 1, held),
        (swap(far_side, "grp"), 1, 1, 1 - held),
    ]
    order = [(f, s, n) for f in (1, 0) for s in (1, 0) for n in (0, 1)]
    places = jnp.stack([(1 - f) * 4 + (1 - s) * 2 + n for _, f, s, n in pieces]).astype(jnp.int32)
    natural = [place(f, near ^ n, s, c) for c in (0, 1) for f, s, n in order]

    vmem = pl.BlockSpec(memory_space=pltpu.VMEM)
    smem = pl.BlockSpec(memory_space=pltpu.SMEM)
    anywhere = pl.BlockSpec(memory_space=pl.ANY)
    dma = pltpu.SemaphoreType.DMA

    rows, below_normed, below_cot = shifts[:, 0], normed, flat_cot
    if lax.axis_size("lat") > 1:
        zeros = jnp.zeros_like(rows)
        onehot_rows = pick(rows, zeros, levels, side, True)
        below_normed = picked(onehot_rows, normed, along_lat(normed, -1))
        below_cot = picked(onehot_rows, flat_cot, along_lat(flat_cot, -1))
        rows = zeros
    info = jnp.concatenate(
        [jnp.stack([rows, shifts[:, 1]], axis=1).reshape(-1), jnp.stack(natural)]
    ).astype(jnp.int32)
    half = width // 2
    turned = jax.ShapeDtypeStruct((2, half, tile), jnp.bfloat16)
    own_turned, sent_turned = kernel_call(
        turned_rolls,
        (turned, turned),
        [smem] + [anywhere] * 4,
        (vmem, vmem),
        [
            pltpu.VMEM((2, 2 * tile, width), jnp.bfloat16),
            pltpu.VMEM((width, tile), jnp.bfloat16),
            dma((4,)),
        ],
        2 * 2 * 2 * tile * tile * width,
        3_000_000,
        "turned_rolls",
    )(info, below_normed, along_lon(below_normed, -1), below_cot, along_lon(below_cot, -1))
    core_turned = swap(sent_turned, "core")
    tiles = [own_turned, core_turned, swap(own_turned, "near"), swap(core_turned, "near")]

    onehot = (index_table[:, :, None] == jnp.arange(entries, dtype=jnp.int32)).astype(f32)
    own_table = lax.dynamic_slice_in_dim(bias_table, near * own_heads, own_heads, 2)
    bias = jnp.einsum("qkr,lrh->lhqk", onehot, own_table, precision=lax.Precision.HIGHEST)
    row_number = lax.axis_index("lat") * side + jnp.arange(side, dtype=jnp.int32)
    group = row_number[None, :] >= (side * lax.axis_size("lat") - shifts[:, 0])[:, None]
    group = jnp.repeat(group, side, axis=1)
    allowed = group[:, :, None] == group[:, None, :]
    bias = jnp.where(allowed[:, None], bias, -1e30).reshape(levels, own_heads // 2, 2 * area, area)

    bf16 = jnp.bfloat16
    kept, sent, w_mine = kernel_call(
        products_kernel,
        (
            jax.ShapeDtypeStruct((2 * tile, 4 * part), f32),
            jax.ShapeDtypeStruct((2 * tile, 4 * part), bf16),
            jax.ShapeDtypeStruct((half, 4 * part), bf16),
        ),
        [smem] + [anywhere] * 12,
        (vmem, vmem, anywhere),
        [
            pltpu.VMEM((4, 2, half, tile), bf16),
            pltpu.VMEM((half, 4 * part), bf16),
            dma((12,)),
            dma,
        ],
        1_200_000_000,
        9_000_000,
        "products",
    )(places, *tiles, *[piece for piece, *_ in pieces])
    crossed = swap(sent, "core")
    grad = kernel_call(
        functools.partial(attention_kernel, area, head),
        jax.ShapeDtypeStruct((2 * tile, 4 * part), bf16),
        [vmem] * 3,
        vmem,
        [pltpu.VMEM((2 * tile, 4 * part), bf16)],
        1_000_000_000,
        4_000_000,
        "attention",
    )(kept, crossed, bias)
    w_theirs = swap(after(w_mine, crossed), "core")
    grad_theirs = swap(grad, "core")
    blocks = kernel_call(
        weights_kernel,
        [jax.ShapeDtypeStruct((own_rows, 4 * part), bf16)] * 8,
        [smem] + [anywhere] * 4 + [vmem] * 2,
        [vmem] * 8,
        [
            pltpu.VMEM((4, 2, half, tile), bf16),
            pltpu.VMEM((half, 4 * part), bf16),
            dma((4,)),
        ],
        1_200_000_000,
        6_000_000,
        "weight_gradient",
    )(near.astype(jnp.int32).reshape(1), *tiles, grad, grad_theirs)

    def block(f, s, n):
        return blocks[((1 - f) * 2 + 1 - s) * 2 + 1 - n]

    side_far_1 = swap(block(1, 1, 1), "side")
    side_far_0 = swap(after(block(1, 1, 0), side_far_1), "side")
    far_1 = swap((block(1, 0, 1).astype(f32) + side_far_1.astype(f32)).astype(bf16), "far")
    far_0 = swap((block(1, 0, 0).astype(f32) + side_far_0.astype(f32)).astype(bf16), "far")
    side_1 = swap(after(block(0, 1, 1), side_far_0), "side")
    side_0 = swap(after(block(0, 1, 0), side_1), "side")
    total_1 = (block(0, 0, 1).astype(f32) + side_1.astype(f32) + far_1.astype(f32)).astype(bf16)
    theirs = swap(total_1, "near").astype(f32)
    total_0 = block(0, 0, 0).astype(f32) + side_0.astype(f32) + far_0.astype(f32)

    attended_own, attended_other = kernel_call(
        outer_kernel,
        (
            jax.ShapeDtypeStruct((tile, 2 * width), f32),
            jax.ShapeDtypeStruct((tile, 2 * width), bf16),
        ),
        [smem, vmem, anywhere, anywhere],
        (vmem, vmem),
        [pltpu.VMEM((width, 4 * part), bf16), dma((16,))],
        1_200_000_000,
        8_000_000,
        "projections",
    )(jnp.stack(natural).astype(jnp.int32), grad, w_mine, w_theirs)
    back = (attended_own + swap(attended_other, "near").astype(f32)).astype(jnp.bfloat16)
    back = roll_back(back, shifts, levels, side)
    output = (values + back[:, :width].astype(f32)).astype(jnp.bfloat16)
    scaled = center * spread
    upstream = back[:, width:].astype(f32) * gain
    grad_stream = spread * (
        upstream
        - jnp.mean(upstream, axis=-1, keepdims=True)
        - scaled * jnp.mean(upstream * scaled, axis=-1, keepdims=True)
    )
    grad_tokens = (flat_cot.astype(f32) + grad_stream).astype(jnp.bfloat16)

    token_count = tile * lax.axis_size("lat") * math.prod(lax.axis_size(axis) for axis in LON)
    columns = []
    for k in range(4):
        cols = slice(k * part, (k + 1) * part)
        columns += [
            jnp.where(first, total_0[:, cols], theirs[:, cols]),
            jnp.where(first, theirs[:, cols], total_0[:, cols]),
        ]
    summed = jnp.concatenate(columns, axis=1)
    if lax.axis_size("lat") > 1:
        summed = lax.psum(summed.astype(jnp.bfloat16), "lat").astype(f32)
    grad_weights = summed * (1.0 / math.sqrt(token_count))
    return (output.reshape(tokens.shape), grad_tokens.reshape(tokens.shape), grad_weights)


def solution(mesh):
    sizes = dict(mesh.shape)
    devices = mesh.devices.reshape(sizes["grp"], sizes["lon"] // 8, 2, 2, 2, sizes["lat"])
    finer = Mesh(devices, ("grp",) + LON + ("lat",))
    return jax.shard_map(
        on_device,
        mesh=finer,
        in_specs=(
            P("grp", "lat", LON, None),
            P(("grp", "lat"), LON),
            P(),
            P(),
            P(LON, None),
            P(),
            P(),
            P("lat", None, None),
            P("grp", "lat", LON, None),
        ),
        out_specs=(
            P("grp", "lat", LON, None),
            P("grp", "lat", LON, None),
            P(("grp",) + LON, None),
        ),
        check_vma=False,
    )
```

```python
import functools
import math

import jax
import jax.numpy as jnp
from jax import lax
from jax.experimental import pallas as pl
from jax.experimental.pallas import tpu as pltpu
from jax.sharding import Mesh
from jax.sharding import PartitionSpec as P

epsilon = 1e-05
LON = ("far", "near", "side", "core")


def along_lon(shard, by):
    count = math.prod(lax.axis_size(axis) for axis in LON)
    return lax.ppermute(shard, LON, [(i, (i + by) % count) for i in range(count)])


def along_lat(shard, by):
    count = lax.axis_size("lat")
    return lax.ppermute(shard, "lat", [(i, (i + by) % count) for i in range(count)])


def swap(shard, axis):
    return lax.ppermute(shard, axis, [(0, 1), (1, 0)])


def pick(rows, cols, levels, side, over_rows):
    tile = levels * side * side
    shape = (tile, 2 * tile)
    target = lax.broadcasted_iota(jnp.int32, shape, 0)
    source = lax.broadcasted_iota(jnp.int32, shape, 1)
    level = target // (side * side)
    row = target // side % side
    col = target % side
    from_row = jnp.full_like(row, rows[levels - 1])
    from_col = jnp.full_like(col, cols[levels - 1])
    for l in range(levels - 1):
        from_row = jnp.where(level == l, rows[l], from_row)
        from_col = jnp.where(level == l, cols[l], from_col)
    from_row = row + from_row
    from_col = col + from_col
    which = (from_row if over_rows else from_col) // side
    wanted = which * tile + level * side * side + from_row % side * side + from_col % side
    return (source == wanted).astype(jnp.bfloat16)


def picked(onehot, first, second):
    both = jnp.concatenate([first, second], axis=0)
    return jnp.dot(onehot, both, preferred_element_type=jnp.float32).astype(jnp.bfloat16)


def roll_back(field, shifts, levels, side):
    zeros = jnp.zeros_like(shifts[:, 0])
    rows = side - shifts[:, 0]
    more = lax.axis_size("lat") > 1
    field = picked(
        pick(zeros if more else rows, side - shifts[:, 1], levels, side, False),
        along_lon(field, 1),
        field,
    )
    if more:
        field = picked(pick(rows, zeros, levels, side, True), along_lat(field, 1), field)
    return field


def turned_rolls(info_ref, *refs):
    fields, (kept_ref, sent_ref, both_ref, turned_ref, sems) = refs[:4], refs[4:]
    tile = fields[0].shape[0]
    rows = kept_ref.shape[1] // 8
    levels, side = 2, 8
    area = tile // levels
    copies = [
        pltpu.make_async_copy(field, both_ref.at[i // 2, pl.ds(i % 2 * tile, tile), :], sems.at[i])
        for i, field in enumerate(fields)
    ]
    for copy in copies:
        copy.start()
    target = lax.broadcasted_iota(jnp.int32, (tile, 2 * tile), 0)
    source = lax.broadcasted_iota(jnp.int32, (tile, 2 * tile), 1)
    upper = target < area
    row = ((target >> 3) & 7) + jnp.where(upper, info_ref[0], info_ref[2])
    col = (target & 7) + jnp.where(upper, info_ref[1], info_ref[3])
    wanted = jnp.where(col >= side, tile, 0) + jnp.where(upper, 0, area) + (row & 7) * side + (col & 7)
    onehot = jnp.where(source == wanted, 1.0, 0.0).astype(jnp.bfloat16)
    for k in (1, 0):
        copies[2 * k].wait()
        copies[2 * k + 1].wait()
        rolled = jnp.dot(onehot, both_ref[k], preferred_element_type=jnp.float32)
        turned_ref[...] = rolled.T.astype(jnp.bfloat16)
        for i in range(8):
            at = pl.ds(i * rows, rows)
            kept_ref[k, at, :] = turned_ref[pl.ds(pl.multiple_of(info_ref[4 + i] * rows, 16), rows), :]
            sent_ref[k, at, :] = turned_ref[pl.ds(pl.multiple_of(info_ref[12 + i] * rows, 16), rows), :]


def down(a, b):
    return lax.dot_general(a, b, (((0,), (0,)), ((), ())), preferred_element_type=jnp.float32)


def across(a, b):
    return lax.dot_general(a, b, (((1,), (1,)), ((), ())), preferred_element_type=jnp.float32)


def products_kernel(place_ref, *refs):
    tiles, pieces = refs[:4], refs[4:12]
    kept_ref, sent_ref, full_ref, tile_ref, w_ref, sems, out_sem = refs[12:]
    tile = tiles[0].shape[2]
    part = w_ref.shape[1] // 4
    copies = []
    for i, piece in enumerate(pieces):
        rows = pl.ds(pl.multiple_of(place_ref[i] * piece.shape[0], 16), piece.shape[0])
        copies.append(pltpu.make_async_copy(piece, w_ref.at[rows, :], sems.at[i]))
    for j, source in enumerate(tiles):
        copies.append(pltpu.make_async_copy(source, tile_ref.at[j], sems.at[8 + j]))
    for copy in copies:
        copy.start()
    for copy in copies:
        copy.wait()
    out_copy = pltpu.make_async_copy(w_ref, full_ref, out_sem)
    out_copy.start()
    for j in (1, 3, 0, 2):
        rows = pl.ds(j // 2 * tile, tile)
        for n in range(4):
            cols = pl.ds(n * part, part)
            product = down(tile_ref[j, n // 3], w_ref[:, cols])
            if j % 2:
                sent_ref[rows, cols] = product.astype(jnp.bfloat16)
            else:
                kept_ref[rows, cols] = product
    out_copy.wait()


def attention_kernel(area, head, kept_ref, came_ref, bias_ref, grad_ref, qkv_ref):
    part = grad_ref.shape[1] // 4
    levels, pairs = bias_ref.shape[:2]
    scale = 1.0 / math.sqrt(head)
    lane = lax.broadcasted_iota(jnp.int32, (area, 2 * head), 1)
    left = lane < head

    def stacked(pair):
        zero = jnp.zeros_like(pair)
        return jnp.concatenate([jnp.where(left, pair, zero), jnp.where(left, zero, pair)], axis=0)

    def unstacked(product):
        return jnp.where(left, product[:area], product[area:]).astype(jnp.bfloat16)

    qkv_ref[...] = (kept_ref[...] + came_ref[...].astype(jnp.float32)).astype(jnp.bfloat16)
    for w in range(grad_ref.shape[0] // area):
        rows = pl.ds(w * area, area)
        for p in range(pairs):
            q_cols, k_cols, v_cols, m_cols = (pl.ds(n * part + p * 2 * head, 2 * head) for n in range(4))
            query = stacked(qkv_ref[rows, q_cols])
            keys = qkv_ref[rows, k_cols]
            values = qkv_ref[rows, v_cols]
            upstream = stacked(qkv_ref[rows, m_cols])
            scores = across(query, keys) * scale + bias_ref[w % levels, p]
            expo = jnp.exp(scores - jnp.max(scores, axis=-1, keepdims=True))
            probs = expo / jnp.sum(expo, axis=-1, keepdims=True)
            probs_b = probs.astype(jnp.bfloat16)
            grad_ref[rows, m_cols] = unstacked(
                jnp.dot(probs_b, values, preferred_element_type=jnp.float32)
            )
            grad_probs = across(upstream, values)
            grad_ref[rows, v_cols] = down(probs_b, upstream).astype(jnp.bfloat16)
            inner = jnp.sum(probs * grad_probs, axis=-1, keepdims=True)
            grad_scores = (probs * (grad_probs - inner) * scale).astype(jnp.bfloat16)
            grad_ref[rows, q_cols] = unstacked(
                jnp.dot(grad_scores, keys, preferred_element_type=jnp.float32)
            )
            grad_ref[rows, k_cols] = down(grad_scores, query).astype(jnp.bfloat16)


def weights_kernel(near_ref, *refs):
    tiles, (own_ref, other_ref), out_refs = refs[:4], refs[4:6], refs[6:14]
    tile_ref, sum_ref, sems = refs[14:]
    tile = tiles[0].shape[2]
    part = own_ref.shape[1] // 4
    rows = out_refs[0].shape[0]
    copies = [pltpu.make_async_copy(source, tile_ref.at[j], sems.at[j]) for j, source in enumerate(tiles)]
    for copy in copies:
        copy.start()
    for copy in copies:
        copy.wait()
    for n in range(4):
        cols = pl.ds(n * part, part)
        total = None
        for t in range(2):
            tokens = pl.ds(t * tile, tile)
            left = jnp.concatenate([tile_ref[2 * t, n // 3], tile_ref[2 * t + 1, n // 3]], axis=1)
            right = jnp.concatenate([own_ref[tokens, cols], other_ref[tokens, cols]], axis=0)
            product = jnp.dot(left, right, preferred_element_type=jnp.float32)
            total = product if total is None else total + product
        sum_ref[:, cols] = total.astype(jnp.bfloat16)
    near = near_ref[0]
    for i, out_ref in enumerate(out_refs):
        wanted = 1 - near if i % 2 == 0 else near
        out_ref[...] = sum_ref[pl.ds(pl.multiple_of((i // 2 * 2 + wanted) * rows, 16), rows), :]


def outer_kernel(place_ref, grad_ref, mine_ref, theirs_ref, own_ref, other_ref, w_ref, sems):
    tile = own_ref.shape[0]
    width = w_ref.shape[0]
    rows = width // 16
    part = w_ref.shape[1] // 4
    step = width // 4
    copies = []
    for i in range(16):
        source = (mine_ref if i < 8 else theirs_ref).at[pl.ds(i % 8 * rows, rows), :]
        into = w_ref.at[pl.ds(pl.multiple_of(place_ref[i] * rows, 16), rows), :]
        copies.append(pltpu.make_async_copy(source, into, sems.at[i]))
    for copy in copies:
        copy.start()
    for copy in copies:
        copy.wait()
    for n in range(4):
        at = pl.ds(n * step, step)
        for k, w_cols in enumerate((pl.ds(3 * part, part), pl.ds(0, 3 * part))):
            product = across(grad_ref[:, w_cols], w_ref[at, w_cols])
            cols = pl.ds(k * width + n * step, step)
            own_ref[:, cols] = product[:tile]
            other_ref[:, cols] = product[tile:].astype(jnp.bfloat16)


def after(value, earlier):
    return lax.optimization_barrier((value, earlier))[0]


def kernel_call(body, outs, in_specs, out_specs, scratch, flops, moved, name):
    return pl.pallas_call(
        body,
        out_shape=outs,
        in_specs=in_specs,
        out_specs=out_specs,
        scratch_shapes=scratch,
        compiler_params=pltpu.CompilerParams(vmem_limit_bytes=58 * 1024 * 1024),
        cost_estimate=pl.CostEstimate(flops=flops, bytes_accessed=moved, transcendentals=0),
        name=name,
    )


def on_device(tokens, land, surface, gain, weights, shifts, index_table, bias_table, cotangent):
    levels, side, _, width = tokens.shape
    area = side * side
    tile = levels * area
    heads = bias_table.shape[2]
    entries = bias_table.shape[1]
    own_rows = weights.shape[0]
    part = weights.shape[1] // 8
    head = weights.shape[1] // 4 // heads
    own_heads = heads // 2
    far, near, beside, core = (lax.axis_index(axis) for axis in LON)
    first = near == 0
    f32 = jnp.float32

    def place(f, n, s, c):
        return ((far ^ f) * 4 + (near ^ n) * 2 + (beside ^ s)) * 2 + (core ^ c)

    low = jnp.concatenate([weights[:, 2 * k * part : (2 * k + 1) * part] for k in range(4)], axis=1)
    high = jnp.concatenate([weights[:, (2 * k + 1) * part : (2 * k + 2) * part] for k in range(4)], axis=1)
    mine = jnp.where(first, low, high)
    came = swap(jnp.where(first, high, low), "near")
    flat_cot = cotangent.reshape(tile, width)
    surface_term = jnp.where(land[None, :, :, None] == 1, surface[1], surface[0])
    stream = (tokens.astype(f32) + surface_term).astype(jnp.bfloat16).reshape(tile, width)
    values = stream.astype(f32)
    center = values - jnp.mean(values, axis=-1, keepdims=True)
    spread = lax.rsqrt(jnp.mean(center * center, axis=-1, keepdims=True) + epsilon)
    normed = (center * spread * gain).astype(jnp.bfloat16)

    mine_far = swap(mine, "far")
    came_far = swap(after(came, mine_far), "far")
    pieces = [
        (mine, 0, 0, near),
        (came, 0, 0, 1 - near),
        (swap(mine, "side"), 0, 1, near),
        (swap(came, "side"), 0, 1, 1 - near),
        (mine_far, 1, 0, near),
        (came_far, 1, 0, 1 - near),
        (swap(mine_far, "side"), 1, 1, near),
        (swap(came_far, "side"), 1, 1, 1 - near),
    ]
    order = [(f, s, n) for f in (1, 0) for s in (1, 0) for n in (0, 1)]
    places = jnp.stack([(1 - f) * 4 + (1 - s) * 2 + n for _, f, s, n in pieces]).astype(jnp.int32)
    natural = [place(f, near ^ n, s, c) for c in (0, 1) for f, s, n in order]

    vmem = pl.BlockSpec(memory_space=pltpu.VMEM)
    smem = pl.BlockSpec(memory_space=pltpu.SMEM)
    anywhere = pl.BlockSpec(memory_space=pl.ANY)
    dma = pltpu.SemaphoreType.DMA

    rows, below_normed, below_cot = shifts[:, 0], normed, flat_cot
    if lax.axis_size("lat") > 1:
        zeros = jnp.zeros_like(rows)
        onehot_rows = pick(rows, zeros, levels, side, True)
        below_normed = picked(onehot_rows, normed, along_lat(normed, -1))
        below_cot = picked(onehot_rows, flat_cot, along_lat(flat_cot, -1))
        rows = zeros
    info = jnp.concatenate(
        [jnp.stack([rows, shifts[:, 1]], axis=1).reshape(-1), jnp.stack(natural)]
    ).astype(jnp.int32)
    half = width // 2
    turned = jax.ShapeDtypeStruct((2, half, tile), jnp.bfloat16)
    own_turned, sent_turned = kernel_call(
        turned_rolls,
        (turned, turned),
        [smem] + [anywhere] * 4,
        (vmem, vmem),
        [
            pltpu.VMEM((2, 2 * tile, width), jnp.bfloat16),
            pltpu.VMEM((width, tile), jnp.bfloat16),
            dma((4,)),
        ],
        2 * 2 * 2 * tile * tile * width,
        3_000_000,
        "turned_rolls",
    )(info, below_normed, along_lon(below_normed, -1), below_cot, along_lon(below_cot, -1))
    core_turned = swap(sent_turned, "core")
    tiles = [own_turned, core_turned, swap(own_turned, "near"), swap(core_turned, "near")]

    onehot = (index_table[:, :, None] == jnp.arange(entries, dtype=jnp.int32)).astype(f32)
    own_table = lax.dynamic_slice_in_dim(bias_table, near * own_heads, own_heads, 2)
    bias = jnp.einsum("qkr,lrh->lhqk", onehot, own_table, precision=lax.Precision.HIGHEST)
    row_number = lax.axis_index("lat") * side + jnp.arange(side, dtype=jnp.int32)
    group = row_number[None, :] >= (side * lax.axis_size("lat") - shifts[:, 0])[:, None]
    group = jnp.repeat(group, side, axis=1)
    allowed = group[:, :, None] == group[:, None, :]
    bias = jnp.where(allowed[:, None], bias, -1e30).reshape(levels, own_heads // 2, 2 * area, area)

    bf16 = jnp.bfloat16
    kept, sent, w_mine = kernel_call(
        products_kernel,
        (
            jax.ShapeDtypeStruct((2 * tile, 4 * part), f32),
            jax.ShapeDtypeStruct((2 * tile, 4 * part), bf16),
            jax.ShapeDtypeStruct((half, 4 * part), bf16),
        ),
        [smem] + [anywhere] * 12,
        (vmem, vmem, anywhere),
        [
            pltpu.VMEM((4, 2, half, tile), bf16),
            pltpu.VMEM((half, 4 * part), bf16),
            dma((12,)),
            dma,
        ],
        1_200_000_000,
        9_000_000,
        "products",
    )(places, *tiles, *[piece for piece, *_ in pieces])
    crossed = swap(sent, "core")
    grad = kernel_call(
        functools.partial(attention_kernel, area, head),
        jax.ShapeDtypeStruct((2 * tile, 4 * part), bf16),
        [vmem] * 3,
        vmem,
        [pltpu.VMEM((2 * tile, 4 * part), bf16)],
        1_000_000_000,
        4_000_000,
        "attention",
    )(kept, crossed, bias)
    w_theirs = swap(after(w_mine, crossed), "core")
    grad_theirs = swap(grad, "core")
    attended_own, attended_other = kernel_call(
        outer_kernel,
        (
            jax.ShapeDtypeStruct((tile, 2 * width), f32),
            jax.ShapeDtypeStruct((tile, 2 * width), bf16),
        ),
        [smem, vmem, anywhere, anywhere],
        (vmem, vmem),
        [pltpu.VMEM((width, 4 * part), bf16), dma((16,))],
        1_200_000_000,
        8_000_000,
        "projections",
    )(jnp.stack(natural).astype(jnp.int32), grad, w_mine, w_theirs)
    blocks = kernel_call(
        weights_kernel,
        [jax.ShapeDtypeStruct((own_rows, 4 * part), bf16)] * 8,
        [smem] + [anywhere] * 4 + [vmem] * 2,
        [vmem] * 8,
        [
            pltpu.VMEM((4, 2, half, tile), bf16),
            pltpu.VMEM((half, 4 * part), bf16),
            dma((4,)),
        ],
        1_200_000_000,
        6_000_000,
        "weight_gradient",
    )(after(near.astype(jnp.int32).reshape(1), attended_other), *tiles, grad, grad_theirs)

    def block(f, s, n):
        return blocks[((1 - f) * 2 + 1 - s) * 2 + 1 - n]

    side_far_1 = swap(block(1, 1, 1), "side")
    side_far_0 = swap(after(block(1, 1, 0), side_far_1), "side")
    far_1 = swap((block(1, 0, 1).astype(f32) + side_far_1.astype(f32)).astype(bf16), "far")
    far_0 = swap(after((block(1, 0, 0).astype(f32) + side_far_0.astype(f32)).astype(bf16), far_1), "far")
    side_1 = swap(after(block(0, 1, 1), side_far_0), "side")
    side_0 = swap(after(block(0, 1, 0), side_1), "side")
    total_1 = (block(0, 0, 1).astype(f32) + side_1.astype(f32) + far_1.astype(f32)).astype(bf16)
    theirs = swap(total_1, "near").astype(f32)
    total_0 = block(0, 0, 0).astype(f32) + side_0.astype(f32) + far_0.astype(f32)

    back = (attended_own + swap(attended_other, "near").astype(f32)).astype(jnp.bfloat16)
    back = roll_back(back, shifts, levels, side)
    output = (values + back[:, :width].astype(f32)).astype(jnp.bfloat16)
    scaled = center * spread
    upstream = back[:, width:].astype(f32) * gain
    grad_stream = spread * (
        upstream
        - jnp.mean(upstream, axis=-1, keepdims=True)
        - scaled * jnp.mean(upstream * scaled, axis=-1, keepdims=True)
    )
    grad_tokens = (flat_cot.astype(f32) + grad_stream).astype(jnp.bfloat16)

    token_count = tile * lax.axis_size("lat") * math.prod(lax.axis_size(axis) for axis in LON)
    columns = []
    for k in range(4):
        cols = slice(k * part, (k + 1) * part)
        columns += [
            jnp.where(first, total_0[:, cols], theirs[:, cols]),
            jnp.where(first, theirs[:, cols], total_0[:, cols]),
        ]
    summed = jnp.concatenate(columns, axis=1)
    if lax.axis_size("lat") > 1:
        summed = lax.psum(summed.astype(jnp.bfloat16), "lat").astype(f32)
    grad_weights = summed * (1.0 / math.sqrt(token_count))
    return (output.reshape(tokens.shape), grad_tokens.reshape(tokens.shape), grad_weights)


def solution(mesh):
    sizes = dict(mesh.shape)
    devices = mesh.devices.reshape(sizes["grp"], sizes["lon"] // 8, 2, 2, 2, sizes["lat"])
    finer = Mesh(devices, ("grp",) + LON + ("lat",))
    return jax.shard_map(
        on_device,
        mesh=finer,
        in_specs=(
            P("grp", "lat", LON, None),
            P(("grp", "lat"), LON),
            P(),
            P(),
            P(LON, None),
            P(),
            P(),
            P("lat", None, None),
            P("grp", "lat", LON, None),
        ),
        out_specs=(
            P("grp", "lat", LON, None),
            P("grp", "lat", LON, None),
            P(("grp",) + LON, None),
        ),
        check_vma=False,
    )
```

```python
import functools
import math

import jax
import jax.numpy as jnp
from jax import lax
from jax.experimental import pallas as pl
from jax.experimental.pallas import tpu as pltpu
from jax.sharding import Mesh
from jax.sharding import PartitionSpec as P

epsilon = 1e-05
LON = ("far", "near", "side", "core")


def along_lon(shard, by):
    count = math.prod(lax.axis_size(axis) for axis in LON)
    return lax.ppermute(shard, LON, [(i, (i + by) % count) for i in range(count)])


def along_lat(shard, by):
    count = lax.axis_size("lat")
    return lax.ppermute(shard, "lat", [(i, (i + by) % count) for i in range(count)])


def swap(shard, axis):
    return lax.ppermute(shard, axis, [(0, 1), (1, 0)])


def pick(rows, cols, levels, side, over_rows):
    tile = levels * side * side
    shape = (tile, 2 * tile)
    target = lax.broadcasted_iota(jnp.int32, shape, 0)
    source = lax.broadcasted_iota(jnp.int32, shape, 1)
    level = target // (side * side)
    row = target // side % side
    col = target % side
    from_row = jnp.full_like(row, rows[levels - 1])
    from_col = jnp.full_like(col, cols[levels - 1])
    for l in range(levels - 1):
        from_row = jnp.where(level == l, rows[l], from_row)
        from_col = jnp.where(level == l, cols[l], from_col)
    from_row = row + from_row
    from_col = col + from_col
    which = (from_row if over_rows else from_col) // side
    wanted = which * tile + level * side * side + from_row % side * side + from_col % side
    return (source == wanted).astype(jnp.bfloat16)


def picked(onehot, first, second):
    both = jnp.concatenate([first, second], axis=0)
    return jnp.dot(onehot, both, preferred_element_type=jnp.float32).astype(jnp.bfloat16)


def roll_back(field, shifts, levels, side):
    zeros = jnp.zeros_like(shifts[:, 0])
    rows = side - shifts[:, 0]
    more = lax.axis_size("lat") > 1
    field = picked(
        pick(zeros if more else rows, side - shifts[:, 1], levels, side, False),
        along_lon(field, 1),
        field,
    )
    if more:
        field = picked(pick(rows, zeros, levels, side, True), along_lat(field, 1), field)
    return field


def turned_rolls(info_ref, gain_ref, *refs):
    fields, (kept_ref, sent_ref, both_ref, turned_ref, sems) = refs[:4], refs[4:]
    tile = fields[0].shape[0]
    rows = kept_ref.shape[1] // 8
    levels, side = 2, 8
    area = tile // levels
    copies = [
        pltpu.make_async_copy(field, both_ref.at[i // 2, pl.ds(i % 2 * tile, tile), :], sems.at[i])
        for i, field in enumerate(fields)
    ]
    for copy in copies:
        copy.start()
    target = lax.broadcasted_iota(jnp.int32, (tile, 2 * tile), 0)
    source = lax.broadcasted_iota(jnp.int32, (tile, 2 * tile), 1)
    upper = target < area
    row = ((target >> 3) & 7) + jnp.where(upper, info_ref[0], info_ref[2])
    col = (target & 7) + jnp.where(upper, info_ref[1], info_ref[3])
    wanted = jnp.where(col >= side, tile, 0) + jnp.where(upper, 0, area) + (row & 7) * side + (col & 7)
    onehot = jnp.where(source == wanted, 1.0, 0.0).astype(jnp.bfloat16)
    for k in (1, 0):
        copies[2 * k].wait()
        copies[2 * k + 1].wait()
        rolled = jnp.dot(onehot, both_ref[k], preferred_element_type=jnp.float32)
        if k == 0:
            center = rolled - jnp.mean(rolled, axis=-1, keepdims=True)
            spread = lax.rsqrt(jnp.mean(center * center, axis=-1, keepdims=True) + epsilon)
            rolled = center * spread * gain_ref[...]
        turned_ref[...] = rolled.T.astype(jnp.bfloat16)
        for i in range(8):
            at = pl.ds(i * rows, rows)
            kept_ref[k, at, :] = turned_ref[pl.ds(pl.multiple_of(info_ref[4 + i] * rows, 16), rows), :]
            sent_ref[k, at, :] = turned_ref[pl.ds(pl.multiple_of(info_ref[12 + i] * rows, 16), rows), :]


def down(a, b):
    return lax.dot_general(a, b, (((0,), (0,)), ((), ())), preferred_element_type=jnp.float32)


def across(a, b):
    return lax.dot_general(a, b, (((1,), (1,)), ((), ())), preferred_element_type=jnp.float32)


def products_kernel(place_ref, *refs):
    tiles, pieces = refs[:4], refs[4:12]
    kept_ref, sent_ref, full_ref, tile_ref, w_ref, sems, out_sem = refs[12:]
    tile = tiles[0].shape[2]
    part = w_ref.shape[1] // 4
    copies = []
    for i, piece in enumerate(pieces):
        rows = pl.ds(pl.multiple_of(place_ref[i] * piece.shape[0], 16), piece.shape[0])
        copies.append(pltpu.make_async_copy(piece, w_ref.at[rows, :], sems.at[i]))
    for j, source in enumerate(tiles):
        copies.append(pltpu.make_async_copy(source, tile_ref.at[j], sems.at[8 + j]))
    for copy in copies:
        copy.start()
    for copy in copies:
        copy.wait()
    out_copy = pltpu.make_async_copy(w_ref, full_ref, out_sem)
    out_copy.start()
    for j in (1, 3, 0, 2):
        rows = pl.ds(j // 2 * tile, tile)
        for n in range(4):
            cols = pl.ds(n * part, part)
            product = down(tile_ref[j, n // 3], w_ref[:, cols])
            if j % 2:
                sent_ref[rows, cols] = product.astype(jnp.bfloat16)
            else:
                kept_ref[rows, cols] = product
    out_copy.wait()


def attention_kernel(area, head, kept_ref, came_ref, bias_ref, grad_ref, qkv_ref, scores_ref, toward_ref, probs_ref, back_ref):
    part = grad_ref.shape[1] // 4
    levels, pairs = bias_ref.shape[:2]
    scale = 1.0 / math.sqrt(head)
    lane = lax.broadcasted_iota(jnp.int32, (area, 2 * head), 1)
    left = lane < head

    def stacked(pair):
        zero = jnp.zeros_like(pair)
        return jnp.concatenate([jnp.where(left, pair, zero), jnp.where(left, zero, pair)], axis=0)

    def unstacked(product):
        return jnp.where(left, product[:area], product[area:]).astype(jnp.bfloat16)

    windows = grad_ref.shape[0] // area
    groups = [(w * pairs + p, w, p) for w in range(windows) for p in range(pairs)]

    def view(w, p, n):
        return pl.ds(w * area, area), pl.ds(n * part + p * 2 * head, 2 * head)

    qkv_ref[...] = (kept_ref[...] + came_ref[...].astype(jnp.float32)).astype(jnp.bfloat16)
    for g, w, p in groups:
        scores_ref[g] = across(stacked(qkv_ref[view(w, p, 0)]), qkv_ref[view(w, p, 1)])
        toward_ref[g] = across(stacked(qkv_ref[view(w, p, 3)]), qkv_ref[view(w, p, 2)])
    for g, w, p in groups:
        scores = scores_ref[g] * scale + bias_ref[w % levels, p]
        expo = jnp.exp(scores - jnp.max(scores, axis=-1, keepdims=True))
        probs = expo / jnp.sum(expo, axis=-1, keepdims=True)
        grad_probs = toward_ref[g]
        inner = jnp.sum(probs * grad_probs, axis=-1, keepdims=True)
        probs_ref[g] = probs.astype(jnp.bfloat16)
        back_ref[g] = (probs * (grad_probs - inner) * scale).astype(jnp.bfloat16)
    for g, w, p in groups:
        probs_b, grad_scores = probs_ref[g], back_ref[g]
        grad_ref[view(w, p, 3)] = unstacked(
            jnp.dot(probs_b, qkv_ref[view(w, p, 2)], preferred_element_type=jnp.float32)
        )
        grad_ref[view(w, p, 0)] = unstacked(
            jnp.dot(grad_scores, qkv_ref[view(w, p, 1)], preferred_element_type=jnp.float32)
        )
        grad_ref[view(w, p, 2)] = down(probs_b, stacked(qkv_ref[view(w, p, 3)])).astype(jnp.bfloat16)
        grad_ref[view(w, p, 1)] = down(grad_scores, stacked(qkv_ref[view(w, p, 0)])).astype(jnp.bfloat16)


def weights_kernel(near_ref, *refs):
    tiles, (own_ref, other_ref), out_refs = refs[:4], refs[4:6], refs[6:14]
    tile_ref, sum_ref, sems = refs[14:]
    tile = tiles[0].shape[2]
    part = own_ref.shape[1] // 4
    rows = out_refs[0].shape[0]
    copies = [pltpu.make_async_copy(source, tile_ref.at[j], sems.at[j]) for j, source in enumerate(tiles)]
    for copy in copies:
        copy.start()
    for copy in copies:
        copy.wait()
    for n in range(4):
        cols = pl.ds(n * part, part)
        total = None
        for t in range(2):
            tokens = pl.ds(t * tile, tile)
            left = jnp.concatenate([tile_ref[2 * t, n // 3], tile_ref[2 * t + 1, n // 3]], axis=1)
            right = jnp.concatenate([own_ref[tokens, cols], other_ref[tokens, cols]], axis=0)
            product = jnp.dot(left, right, preferred_element_type=jnp.float32)
            total = product if total is None else total + product
        sum_ref[:, cols] = total.astype(jnp.bfloat16)
    near = near_ref[0]
    for i, out_ref in enumerate(out_refs):
        wanted = 1 - near if i % 2 == 0 else near
        out_ref[...] = sum_ref[pl.ds(pl.multiple_of((i // 2 * 2 + wanted) * rows, 16), rows), :]


def outer_kernel(place_ref, grad_ref, mine_ref, theirs_ref, own_ref, other_ref, w_ref, sems):
    tile = own_ref.shape[0]
    width = w_ref.shape[0]
    rows = width // 16
    part = w_ref.shape[1] // 4
    step = width // 4
    copies = []
    for i in range(16):
        source = (mine_ref if i < 8 else theirs_ref).at[pl.ds(i % 8 * rows, rows), :]
        into = w_ref.at[pl.ds(pl.multiple_of(place_ref[i] * rows, 16), rows), :]
        copies.append(pltpu.make_async_copy(source, into, sems.at[i]))
    for copy in copies:
        copy.start()
    for copy in copies:
        copy.wait()
    for n in range(4):
        at = pl.ds(n * step, step)
        for k, w_cols in enumerate((pl.ds(3 * part, part), pl.ds(0, 3 * part))):
            product = across(grad_ref[:, w_cols], w_ref[at, w_cols])
            cols = pl.ds(k * width + n * step, step)
            own_ref[:, cols] = product[:tile]
            other_ref[:, cols] = product[tile:].astype(jnp.bfloat16)


def after(value, earlier):
    return lax.optimization_barrier((value, earlier))[0]


def kernel_call(body, outs, in_specs, out_specs, scratch, flops, moved, name):
    return pl.pallas_call(
        body,
        out_shape=outs,
        in_specs=in_specs,
        out_specs=out_specs,
        scratch_shapes=scratch,
        compiler_params=pltpu.CompilerParams(vmem_limit_bytes=58 * 1024 * 1024),
        cost_estimate=pl.CostEstimate(flops=flops, bytes_accessed=moved, transcendentals=0),
        name=name,
    )


def on_device(tokens, land, surface, gain, weights, shifts, index_table, bias_table, cotangent):
    levels, side, _, width = tokens.shape
    area = side * side
    tile = levels * area
    heads = bias_table.shape[2]
    entries = bias_table.shape[1]
    own_rows = weights.shape[0]
    part = weights.shape[1] // 8
    head = weights.shape[1] // 4 // heads
    own_heads = heads // 2
    far, near, beside, core = (lax.axis_index(axis) for axis in LON)
    grp = lax.axis_index("grp")
    first = near == 0
    f32 = jnp.float32

    def place(f, n, s, c):
        return ((far ^ f) * 4 + (near ^ n) * 2 + (beside ^ s)) * 2 + (core ^ c)

    low = jnp.concatenate([weights[:, 2 * k * part : (2 * k + 1) * part] for k in range(4)], axis=1)
    high = jnp.concatenate([weights[:, (2 * k + 1) * part : (2 * k + 2) * part] for k in range(4)], axis=1)
    mine = jnp.where(first, low, high)
    came = swap(jnp.where(first, high, low), "near")
    flat_cot = cotangent.reshape(tile, width)
    surface_term = jnp.where(land[None, :, :, None] == 1, surface[1], surface[0])
    stream = (tokens.astype(f32) + surface_term).astype(jnp.bfloat16).reshape(tile, width)
    values = stream.astype(f32)
    center = values - jnp.mean(values, axis=-1, keepdims=True)
    spread = lax.rsqrt(jnp.mean(center * center, axis=-1, keepdims=True) + epsilon)

    held = near ^ grp
    mine_side = swap(mine, "side")
    came_side = swap(came, "side")
    across_far = swap(jnp.where(grp == 0, mine, came), "far")
    order = [(f, s, n) for f in (1, 0) for s in (1, 0) for n in (0, 1)]
    natural = [place(f, near ^ n, s, c) for c in (0, 1) for f, s, n in order]

    vmem = pl.BlockSpec(memory_space=pltpu.VMEM)
    smem = pl.BlockSpec(memory_space=pltpu.SMEM)
    anywhere = pl.BlockSpec(memory_space=pl.ANY)
    dma = pltpu.SemaphoreType.DMA

    rows, below, below_cot = shifts[:, 0], stream, flat_cot
    if lax.axis_size("lat") > 1:
        zeros = jnp.zeros_like(rows)
        onehot_rows = pick(rows, zeros, levels, side, True)
        below = picked(onehot_rows, stream, along_lat(stream, -1))
        below_cot = picked(onehot_rows, flat_cot, along_lat(flat_cot, -1))
        rows = zeros
    info = jnp.concatenate(
        [jnp.stack([rows, shifts[:, 1]], axis=1).reshape(-1), jnp.stack(natural)]
    ).astype(jnp.int32)
    half = width // 2
    turned = jax.ShapeDtypeStruct((2, half, tile), jnp.bfloat16)
    own_turned, sent_turned = kernel_call(
        turned_rolls,
        (turned, turned),
        [smem, vmem] + [anywhere] * 4,
        (vmem, vmem),
        [
            pltpu.VMEM((2, 2 * tile, width), jnp.bfloat16),
            pltpu.VMEM((width, tile), jnp.bfloat16),
            dma((4,)),
        ],
        2 * 2 * 2 * tile * tile * width,
        3_000_000,
        "turned_rolls",
    )(after(info, (mine_side, came_side)), gain.reshape(1, -1), below, along_lon(below, -1), below_cot, along_lon(below_cot, -1))
    far_side = swap(across_far, "side")
    pieces = [
        (mine, 0, 0, near),
        (came, 0, 0, 1 - near),
        (mine_side, 0, 1, near),
        (came_side, 0, 1, 1 - near),
        (across_far, 1, 0, held),
        (swap(across_far, "grp"), 1, 0, 1 - held),
        (far_side, 1, 1, held),
        (swap(far_side, "grp"), 1, 1, 1 - held),
    ]
    places = jnp.stack([(1 - f) * 4 + (1 - s) * 2 + n for _, f, s, n in pieces]).astype(jnp.int32)
    own_near, sent_near = swap(own_turned, "near"), swap(sent_turned, "near")
    tiles = [own_turned, swap(sent_turned, "core"), own_near, swap(sent_near, "core")]

    onehot = (index_table[:, :, None] == jnp.arange(entries, dtype=jnp.int32)).astype(f32)
    own_table = lax.dynamic_slice_in_dim(bias_table, near * own_heads, own_heads, 2)
    bias = jnp.einsum("qkr,lrh->lhqk", onehot, own_table, precision=lax.Precision.HIGHEST)
    row_number = lax.axis_index("lat") * side + jnp.arange(side, dtype=jnp.int32)
    group = row_number[None, :] >= (side * lax.axis_size("lat") - shifts[:, 0])[:, None]
    group = jnp.repeat(group, side, axis=1)
    allowed = group[:, :, None] == group[:, None, :]
    bias = jnp.where(allowed[:, None], bias, -1e30).reshape(levels, own_heads // 2, 2 * area, area)

    bf16 = jnp.bfloat16
    kept, sent, w_mine = kernel_call(
        products_kernel,
        (
            jax.ShapeDtypeStruct((2 * tile, 4 * part), f32),
            jax.ShapeDtypeStruct((2 * tile, 4 * part), bf16),
            jax.ShapeDtypeStruct((half, 4 * part), bf16),
        ),
        [smem] + [anywhere] * 12,
        (vmem, vmem, anywhere),
        [
            pltpu.VMEM((4, 2, half, tile), bf16),
            pltpu.VMEM((half, 4 * part), bf16),
            dma((12,)),
            dma,
        ],
        1_200_000_000,
        9_000_000,
        "products",
    )(after(places, bias), *tiles, *[piece for piece, *_ in pieces])
    crossed = swap(sent, "core")
    grad = kernel_call(
        functools.partial(attention_kernel, area, head),
        jax.ShapeDtypeStruct((2 * tile, 4 * part), bf16),
        [vmem] * 3,
        vmem,
        [pltpu.VMEM((2 * tile, 4 * part), bf16)]
        + [pltpu.VMEM((2 * tile // area * own_heads // 2, 2 * area, area), kind) for kind in (f32, f32, bf16, bf16)],
        1_000_000_000,
        4_000_000,
        "attention",
    )(kept, crossed, bias)
    w_theirs = swap(after(w_mine, crossed), "core")
    grad_theirs = swap(grad, "core")
    blocks = kernel_call(
        weights_kernel,
        [jax.ShapeDtypeStruct((own_rows, 4 * part), bf16)] * 8,
        [smem] + [anywhere] * 4 + [vmem] * 2,
        [vmem] * 8,
        [
            pltpu.VMEM((4, 2, half, tile), bf16),
            pltpu.VMEM((half, 4 * part), bf16),
            dma((4,)),
        ],
        1_200_000_000,
        6_000_000,
        "weight_gradient",
    )(near.astype(jnp.int32).reshape(1), *tiles, grad, grad_theirs)

    def block(f, s, n):
        return blocks[((1 - f) * 2 + 1 - s) * 2 + 1 - n]

    attended_own, attended_other = kernel_call(
        outer_kernel,
        (
            jax.ShapeDtypeStruct((tile, 2 * width), f32),
            jax.ShapeDtypeStruct((tile, 2 * width), bf16),
        ),
        [smem, vmem, anywhere, anywhere],
        (vmem, vmem),
        [pltpu.VMEM((width, 4 * part), bf16), dma((16,))],
        1_200_000_000,
        8_000_000,
        "projections",
    )(after(jnp.stack(natural).astype(jnp.int32), blocks[0]), grad, w_mine, w_theirs)
    side_far_1 = after(swap(block(1, 1, 1), "side"), attended_other)
    arrived_back = swap(attended_other, "near")
    side_far_0 = swap(after(block(1, 1, 0), side_far_1), "side")
    far_1 = swap((block(1, 0, 1).astype(f32) + side_far_1.astype(f32)).astype(bf16), "far")
    far_0 = swap(after((block(1, 0, 0).astype(f32) + side_far_0.astype(f32)).astype(bf16), (far_1, arrived_back)), "far")
    side_1 = swap(after(block(0, 1, 1), side_far_0), "side")
    side_0 = swap(after(block(0, 1, 0), side_1), "side")
    total_1 = (block(0, 0, 1).astype(f32) + side_1.astype(f32) + far_1.astype(f32)).astype(bf16)
    theirs = swap(total_1, "near").astype(f32)

    back = (attended_own + arrived_back.astype(f32)).astype(jnp.bfloat16)
    back = roll_back(back, shifts, levels, side)
    output = (values + back[:, :width].astype(f32)).astype(jnp.bfloat16)
    scaled = center * spread
    upstream = back[:, width:].astype(f32) * gain
    grad_stream = spread * (
        upstream
        - jnp.mean(upstream, axis=-1, keepdims=True)
        - scaled * jnp.mean(upstream * scaled, axis=-1, keepdims=True)
    )
    grad_tokens = (flat_cot.astype(f32) + grad_stream).astype(jnp.bfloat16)

    far_0 = after(far_0, (output, grad_tokens))
    total_0 = block(0, 0, 0).astype(f32) + side_0.astype(f32) + far_0.astype(f32)
    token_count = tile * lax.axis_size("lat") * math.prod(lax.axis_size(axis) for axis in LON)
    columns = []
    for k in range(4):
        cols = slice(k * part, (k + 1) * part)
        columns += [
            jnp.where(first, total_0[:, cols], theirs[:, cols]),
            jnp.where(first, theirs[:, cols], total_0[:, cols]),
        ]
    summed = jnp.concatenate(columns, axis=1)
    if lax.axis_size("lat") > 1:
        summed = lax.psum(summed.astype(jnp.bfloat16), "lat").astype(f32)
    grad_weights = summed * (1.0 / math.sqrt(token_count))
    return (output.reshape(tokens.shape), grad_tokens.reshape(tokens.shape), grad_weights)


def solution(mesh):
    sizes = dict(mesh.shape)
    devices = mesh.devices.reshape(sizes["grp"], sizes["lon"] // 8, 2, 2, 2, sizes["lat"])
    finer = Mesh(devices, ("grp",) + LON + ("lat",))
    return jax.shard_map(
        on_device,
        mesh=finer,
        in_specs=(
            P("grp", "lat", LON, None),
            P(("grp", "lat"), LON),
            P(),
            P(),
            P(LON, None),
            P(),
            P(),
            P("lat", None, None),
            P("grp", "lat", LON, None),
        ),
        out_specs=(
            P("grp", "lat", LON, None),
            P("grp", "lat", LON, None),
            P(("grp",) + LON, None),
        ),
        check_vma=False,
    )
```

```python
import functools
import math

import jax
import jax.numpy as jnp
from jax import lax
from jax.experimental import pallas as pl
from jax.experimental.pallas import tpu as pltpu
from jax.sharding import Mesh
from jax.sharding import PartitionSpec as P

epsilon = 1e-05
LON = ("far", "near", "side", "core")


def along_lon(shard, by):
    count = math.prod(lax.axis_size(axis) for axis in LON)
    return lax.ppermute(shard, LON, [(i, (i + by) % count) for i in range(count)])


def along_lat(shard, by):
    count = lax.axis_size("lat")
    return lax.ppermute(shard, "lat", [(i, (i + by) % count) for i in range(count)])


def swap(shard, axis):
    return lax.ppermute(shard, axis, [(0, 1), (1, 0)])


def pick(rows, cols, levels, side, over_rows):
    tile = levels * side * side
    shape = (tile, 2 * tile)
    target = lax.broadcasted_iota(jnp.int32, shape, 0)
    source = lax.broadcasted_iota(jnp.int32, shape, 1)
    level = target // (side * side)
    row = target // side % side
    col = target % side
    from_row = jnp.full_like(row, rows[levels - 1])
    from_col = jnp.full_like(col, cols[levels - 1])
    for l in range(levels - 1):
        from_row = jnp.where(level == l, rows[l], from_row)
        from_col = jnp.where(level == l, cols[l], from_col)
    from_row = row + from_row
    from_col = col + from_col
    which = (from_row if over_rows else from_col) // side
    wanted = which * tile + level * side * side + from_row % side * side + from_col % side
    return (source == wanted).astype(jnp.bfloat16)


def picked(onehot, first, second):
    both = jnp.concatenate([first, second], axis=0)
    return jnp.dot(onehot, both, preferred_element_type=jnp.float32).astype(jnp.bfloat16)


def roll_back(field, shifts, levels, side):
    zeros = jnp.zeros_like(shifts[:, 0])
    rows = side - shifts[:, 0]
    more = lax.axis_size("lat") > 1
    field = picked(
        pick(zeros if more else rows, side - shifts[:, 1], levels, side, False),
        along_lon(field, 1),
        field,
    )
    if more:
        field = picked(pick(rows, zeros, levels, side, True), along_lat(field, 1), field)
    return field


def turned_rolls(info_ref, gain_ref, *refs):
    fields, (kept_ref, sent_ref, both_ref, turned_ref, sems) = refs[:4], refs[4:]
    tile = fields[0].shape[0]
    rows = kept_ref.shape[1] // 8
    levels, side = 2, 8
    area = tile // levels
    copies = [
        pltpu.make_async_copy(field, both_ref.at[i // 2, pl.ds(i % 2 * tile, tile), :], sems.at[i])
        for i, field in enumerate(fields)
    ]
    for copy in copies:
        copy.start()
    target = lax.broadcasted_iota(jnp.int32, (tile, 2 * tile), 0)
    source = lax.broadcasted_iota(jnp.int32, (tile, 2 * tile), 1)
    upper = target < area
    row = ((target >> 3) & 7) + jnp.where(upper, info_ref[0], info_ref[2])
    col = (target & 7) + jnp.where(upper, info_ref[1], info_ref[3])
    wanted = jnp.where(col >= side, tile, 0) + jnp.where(upper, 0, area) + (row & 7) * side + (col & 7)
    onehot = jnp.where(source == wanted, 1.0, 0.0).astype(jnp.bfloat16)
    for k in (1, 0):
        copies[2 * k].wait()
        copies[2 * k + 1].wait()
        rolled = jnp.dot(onehot, both_ref[k], preferred_element_type=jnp.float32)
        if k == 0:
            center = rolled - jnp.mean(rolled, axis=-1, keepdims=True)
            spread = lax.rsqrt(jnp.mean(center * center, axis=-1, keepdims=True) + epsilon)
            rolled = center * spread * gain_ref[...]
        turned_ref[...] = rolled.T.astype(jnp.bfloat16)
        for i in range(8):
            at = pl.ds(i * rows, rows)
            kept_ref[k, at, :] = turned_ref[pl.ds(pl.multiple_of(info_ref[4 + i] * rows, 16), rows), :]
            sent_ref[k, at, :] = turned_ref[pl.ds(pl.multiple_of(info_ref[12 + i] * rows, 16), rows), :]


def down(a, b):
    return lax.dot_general(a, b, (((0,), (0,)), ((), ())), preferred_element_type=jnp.float32)


def across(a, b):
    return lax.dot_general(a, b, (((1,), (1,)), ((), ())), preferred_element_type=jnp.float32)


def products_kernel(place_ref, *refs):
    tiles, pieces = refs[:4], refs[4:12]
    kept_ref, sent_ref, full_ref, tile_ref, w_ref, sems, out_sem = refs[12:]
    tile = tiles[0].shape[2]
    part = w_ref.shape[1] // 4
    copies = []
    for i, piece in enumerate(pieces):
        rows = pl.ds(pl.multiple_of(place_ref[i] * piece.shape[0], 16), piece.shape[0])
        copies.append(pltpu.make_async_copy(piece, w_ref.at[rows, :], sems.at[i]))
    for j, source in enumerate(tiles):
        copies.append(pltpu.make_async_copy(source, tile_ref.at[j], sems.at[8 + j]))
    for copy in copies:
        copy.start()
    for copy in copies:
        copy.wait()
    out_copy = pltpu.make_async_copy(w_ref, full_ref, out_sem)
    out_copy.start()
    for j in (1, 3, 0, 2):
        rows = pl.ds(j // 2 * tile, tile)
        for n in range(4):
            cols = pl.ds(n * part, part)
            product = down(tile_ref[j, n // 3], w_ref[:, cols])
            if j % 2:
                sent_ref[rows, cols] = product.astype(jnp.bfloat16)
            else:
                kept_ref[rows, cols] = product
    out_copy.wait()


def attention_kernel(area, head, kept_ref, came_ref, bias_ref, grad_ref, qkv_ref, scores_ref, toward_ref, probs_ref, back_ref):
    part = grad_ref.shape[1] // 4
    levels, pairs = bias_ref.shape[:2]
    scale = 1.0 / math.sqrt(head)
    lane = lax.broadcasted_iota(jnp.int32, (area, 2 * head), 1)
    left = lane < head

    def stacked(pair):
        zero = jnp.zeros_like(pair)
        return jnp.concatenate([jnp.where(left, pair, zero), jnp.where(left, zero, pair)], axis=0)

    def unstacked(product):
        return jnp.where(left, product[:area], product[area:]).astype(jnp.bfloat16)

    windows = grad_ref.shape[0] // area
    groups = [(w * pairs + p, w, p) for w in range(windows) for p in range(pairs)]

    def view(w, p, n):
        return pl.ds(w * area, area), pl.ds(n * part + p * 2 * head, 2 * head)

    qkv_ref[...] = (kept_ref[...] + came_ref[...].astype(jnp.float32)).astype(jnp.bfloat16)
    for g, w, p in groups:
        scores_ref[g] = across(stacked(qkv_ref[view(w, p, 0)]), qkv_ref[view(w, p, 1)])
        toward_ref[g] = across(stacked(qkv_ref[view(w, p, 3)]), qkv_ref[view(w, p, 2)])
    for g, w, p in groups:
        scores = scores_ref[g] * scale + bias_ref[w % levels, p]
        expo = jnp.exp(scores - jnp.max(scores, axis=-1, keepdims=True))
        probs = expo / jnp.sum(expo, axis=-1, keepdims=True)
        grad_probs = toward_ref[g]
        inner = jnp.sum(probs * grad_probs, axis=-1, keepdims=True)
        probs_ref[g] = probs.astype(jnp.bfloat16)
        back_ref[g] = (probs * (grad_probs - inner) * scale).astype(jnp.bfloat16)
    for g, w, p in groups:
        probs_b, grad_scores = probs_ref[g], back_ref[g]
        grad_ref[view(w, p, 3)] = unstacked(
            jnp.dot(probs_b, qkv_ref[view(w, p, 2)], preferred_element_type=jnp.float32)
        )
        grad_ref[view(w, p, 0)] = unstacked(
            jnp.dot(grad_scores, qkv_ref[view(w, p, 1)], preferred_element_type=jnp.float32)
        )
        grad_ref[view(w, p, 2)] = down(probs_b, stacked(qkv_ref[view(w, p, 3)])).astype(jnp.bfloat16)
        grad_ref[view(w, p, 1)] = down(grad_scores, stacked(qkv_ref[view(w, p, 0)])).astype(jnp.bfloat16)


def weights_kernel(near_ref, *refs):
    tiles, (own_ref, other_ref), out_refs = refs[:4], refs[4:6], refs[6:14]
    tile_ref, sum_ref, sems = refs[14:]
    tile = tiles[0].shape[2]
    part = own_ref.shape[1] // 4
    rows = out_refs[0].shape[0]
    copies = [pltpu.make_async_copy(source, tile_ref.at[j], sems.at[j]) for j, source in enumerate(tiles)]
    for copy in copies:
        copy.start()
    for copy in copies:
        copy.wait()
    for n in range(4):
        cols = pl.ds(n * part, part)
        total = None
        for t in range(2):
            tokens = pl.ds(t * tile, tile)
            left = jnp.concatenate([tile_ref[2 * t, n // 3], tile_ref[2 * t + 1, n // 3]], axis=1)
            right = jnp.concatenate([own_ref[tokens, cols], other_ref[tokens, cols]], axis=0)
            product = jnp.dot(left, right, preferred_element_type=jnp.float32)
            total = product if total is None else total + product
        sum_ref[:, cols] = total.astype(jnp.bfloat16)
    near = near_ref[0]
    for i, out_ref in enumerate(out_refs):
        wanted = 1 - near if i % 2 == 0 else near
        out_ref[...] = sum_ref[pl.ds(pl.multiple_of((i // 2 * 2 + wanted) * rows, 16), rows), :]


def outer_kernel(place_ref, grad_ref, mine_ref, theirs_ref, own_ref, other_ref, w_ref, sems):
    tile = own_ref.shape[0]
    width = w_ref.shape[0]
    rows = width // 16
    part = w_ref.shape[1] // 4
    step = width // 4
    copies = []
    for i in range(16):
        source = (mine_ref if i < 8 else theirs_ref).at[pl.ds(i % 8 * rows, rows), :]
        into = w_ref.at[pl.ds(pl.multiple_of(place_ref[i] * rows, 16), rows), :]
        copies.append(pltpu.make_async_copy(source, into, sems.at[i]))
    for copy in copies:
        copy.start()
    for copy in copies:
        copy.wait()
    for n in range(4):
        at = pl.ds(n * step, step)
        for k, w_cols in enumerate((pl.ds(3 * part, part), pl.ds(0, 3 * part))):
            product = across(grad_ref[:, w_cols], w_ref[at, w_cols])
            cols = pl.ds(k * width + n * step, step)
            own_ref[:, cols] = product[:tile]
            other_ref[:, cols] = product[tile:].astype(jnp.bfloat16)


def after(value, earlier):
    return lax.optimization_barrier((value, earlier))[0]


def kernel_call(body, outs, in_specs, out_specs, scratch, flops, moved, name, room=58):
    return pl.pallas_call(
        body,
        out_shape=outs,
        in_specs=in_specs,
        out_specs=out_specs,
        scratch_shapes=scratch,
        compiler_params=pltpu.CompilerParams(vmem_limit_bytes=room * 1024 * 1024),
        cost_estimate=pl.CostEstimate(flops=flops, bytes_accessed=moved, transcendentals=0),
        name=name,
    )


def on_device(tokens, land, surface, gain, weights, shifts, index_table, bias_table, cotangent):
    levels, side, _, width = tokens.shape
    area = side * side
    tile = levels * area
    heads = bias_table.shape[2]
    entries = bias_table.shape[1]
    own_rows = weights.shape[0]
    part = weights.shape[1] // 8
    head = weights.shape[1] // 4 // heads
    own_heads = heads // 2
    far, near, beside, core = (lax.axis_index(axis) for axis in LON)
    grp = lax.axis_index("grp")
    first = near == 0
    f32 = jnp.float32

    def place(f, n, s, c):
        return ((far ^ f) * 4 + (near ^ n) * 2 + (beside ^ s)) * 2 + (core ^ c)

    low = jnp.concatenate([weights[:, 2 * k * part : (2 * k + 1) * part] for k in range(4)], axis=1)
    high = jnp.concatenate([weights[:, (2 * k + 1) * part : (2 * k + 2) * part] for k in range(4)], axis=1)
    mine = jnp.where(first, low, high)
    came = swap(jnp.where(first, high, low), "near")
    flat_cot = cotangent.reshape(tile, width)
    surface_term = jnp.where(land[None, :, :, None] == 1, surface[1], surface[0])
    stream = (tokens.astype(f32) + surface_term).astype(jnp.bfloat16).reshape(tile, width)
    values = stream.astype(f32)
    center = values - jnp.mean(values, axis=-1, keepdims=True)
    spread = lax.rsqrt(jnp.mean(center * center, axis=-1, keepdims=True) + epsilon)

    held = near ^ grp
    across_far = swap(jnp.where(grp == 0, mine, came), "far")
    order = [(f, s, n) for f in (1, 0) for s in (1, 0) for n in (0, 1)]
    natural = [place(f, near ^ n, s, c) for c in (0, 1) for f, s, n in order]

    vmem = pl.BlockSpec(memory_space=pltpu.VMEM)
    smem = pl.BlockSpec(memory_space=pltpu.SMEM)
    anywhere = pl.BlockSpec(memory_space=pl.ANY)
    dma = pltpu.SemaphoreType.DMA

    rows, below, below_cot = shifts[:, 0], stream, flat_cot
    if lax.axis_size("lat") > 1:
        zeros = jnp.zeros_like(rows)
        onehot_rows = pick(rows, zeros, levels, side, True)
        below = picked(onehot_rows, stream, along_lat(stream, -1))
        below_cot = picked(onehot_rows, flat_cot, along_lat(flat_cot, -1))
        rows = zeros
    info = jnp.concatenate(
        [jnp.stack([rows, shifts[:, 1]], axis=1).reshape(-1), jnp.stack(natural)]
    ).astype(jnp.int32)
    half = width // 2
    turned = jax.ShapeDtypeStruct((2, half, tile), jnp.bfloat16)
    own_turned, sent_turned = kernel_call(
        turned_rolls,
        (turned, turned),
        [smem, vmem] + [anywhere] * 4,
        (vmem, vmem),
        [
            pltpu.VMEM((2, 2 * tile, width), jnp.bfloat16),
            pltpu.VMEM((width, tile), jnp.bfloat16),
            dma((4,)),
        ],
        2 * 2 * 2 * tile * tile * width,
        3_000_000,
        "turned_rolls",
    )(info, gain.reshape(1, -1), below, along_lon(below, -1), below_cot, along_lon(below_cot, -1))
    mine_side = swap(after(mine, own_turned), "side")
    far_side = swap(across_far, "side")
    came_side = swap(after(came, far_side), "side")
    pieces = [
        (mine, 0, 0, near),
        (came, 0, 0, 1 - near),
        (mine_side, 0, 1, near),
        (came_side, 0, 1, 1 - near),
        (across_far, 1, 0, held),
        (swap(across_far, "grp"), 1, 0, 1 - held),
        (far_side, 1, 1, held),
        (swap(far_side, "grp"), 1, 1, 1 - held),
    ]
    places = jnp.stack([(1 - f) * 4 + (1 - s) * 2 + n for _, f, s, n in pieces]).astype(jnp.int32)
    own_near, sent_near = swap(own_turned, "near"), swap(sent_turned, "near")
    tiles = [own_turned, swap(sent_turned, "core"), own_near, swap(sent_near, "core")]

    onehot = (index_table[:, :, None] == jnp.arange(entries, dtype=jnp.int32)).astype(f32)
    own_table = lax.dynamic_slice_in_dim(bias_table, near * own_heads, own_heads, 2)
    bias = jnp.einsum("qkr,lrh->lhqk", onehot, own_table, precision=lax.Precision.HIGHEST)
    row_number = lax.axis_index("lat") * side + jnp.arange(side, dtype=jnp.int32)
    group = row_number[None, :] >= (side * lax.axis_size("lat") - shifts[:, 0])[:, None]
    group = jnp.repeat(group, side, axis=1)
    allowed = group[:, :, None] == group[:, None, :]
    bias = jnp.where(allowed[:, None], bias, -1e30).reshape(levels, own_heads // 2, 2 * area, area)

    bf16 = jnp.bfloat16
    kept, sent, w_mine = kernel_call(
        products_kernel,
        (
            jax.ShapeDtypeStruct((2 * tile, 4 * part), f32),
            jax.ShapeDtypeStruct((2 * tile, 4 * part), bf16),
            jax.ShapeDtypeStruct((half, 4 * part), bf16),
        ),
        [smem] + [anywhere] * 12,
        (vmem, vmem, anywhere),
        [
            pltpu.VMEM((4, 2, half, tile), bf16),
            pltpu.VMEM((half, 4 * part), bf16),
            dma((12,)),
            dma,
        ],
        1_200_000_000,
        9_000_000,
        "products",
    )(after(places, bias), *tiles, *[piece for piece, *_ in pieces])
    crossed = swap(sent, "core")
    grad = kernel_call(
        functools.partial(attention_kernel, area, head),
        jax.ShapeDtypeStruct((2 * tile, 4 * part), bf16),
        [vmem] * 3,
        vmem,
        [pltpu.VMEM((2 * tile, 4 * part), bf16)]
        + [pltpu.VMEM((2 * tile // area * own_heads // 2, 2 * area, area), kind) for kind in (f32, f32, bf16, bf16)],
        1_000_000_000,
        4_000_000,
        "attention",
        24,
    )(kept, crossed, bias)
    w_theirs = swap(after(w_mine, crossed), "core")
    grad_theirs = swap(grad, "core")
    attended_own, attended_other = kernel_call(
        outer_kernel,
        (
            jax.ShapeDtypeStruct((tile, 2 * width), f32),
            jax.ShapeDtypeStruct((tile, 2 * width), bf16),
        ),
        [smem, vmem, anywhere, anywhere],
        (vmem, vmem),
        [pltpu.VMEM((width, 4 * part), bf16), dma((16,))],
        1_200_000_000,
        8_000_000,
        "projections",
        24,
    )(jnp.stack(natural).astype(jnp.int32), grad, w_mine, w_theirs)
    blocks = kernel_call(
        weights_kernel,
        [jax.ShapeDtypeStruct((own_rows, 4 * part), bf16)] * 8,
        [smem] + [anywhere] * 4 + [vmem] * 2,
        [vmem] * 8,
        [
            pltpu.VMEM((4, 2, half, tile), bf16),
            pltpu.VMEM((half, 4 * part), bf16),
            dma((4,)),
        ],
        1_200_000_000,
        6_000_000,
        "weight_gradient",
        24,
    )(after(near.astype(jnp.int32).reshape(1), attended_other), *tiles, grad, grad_theirs)

    def block(f, s, n):
        return blocks[((1 - f) * 2 + 1 - s) * 2 + 1 - n]

    side_far_1 = swap(block(1, 1, 1), "side")
    arrived_back = swap(attended_other, "near")
    side_far_0 = swap(after(block(1, 1, 0), side_far_1), "side")
    far_1 = swap(after((block(1, 0, 1).astype(f32) + side_far_1.astype(f32)).astype(bf16), arrived_back), "far")
    far_0 = swap(after((block(1, 0, 0).astype(f32) + side_far_0.astype(f32)).astype(bf16), far_1), "far")
    side_1 = swap(after(block(0, 1, 1), side_far_0), "side")
    side_0 = swap(after(block(0, 1, 0), side_1), "side")
    total_1 = (block(0, 0, 1).astype(f32) + side_1.astype(f32) + far_1.astype(f32)).astype(bf16)
    theirs = swap(total_1, "near").astype(f32)

    back = (attended_own + arrived_back.astype(f32)).astype(jnp.bfloat16)
    back = roll_back(back, shifts, levels, side)
    output = (values + back[:, :width].astype(f32)).astype(jnp.bfloat16)
    scaled = center * spread
    upstream = back[:, width:].astype(f32) * gain
    grad_stream = spread * (
        upstream
        - jnp.mean(upstream, axis=-1, keepdims=True)
        - scaled * jnp.mean(upstream * scaled, axis=-1, keepdims=True)
    )
    grad_tokens = (flat_cot.astype(f32) + grad_stream).astype(jnp.bfloat16)

    far_0 = after(far_0, (output, grad_tokens))
    total_0 = block(0, 0, 0).astype(f32) + side_0.astype(f32) + far_0.astype(f32)
    token_count = tile * lax.axis_size("lat") * math.prod(lax.axis_size(axis) for axis in LON)
    columns = []
    for k in range(4):
        cols = slice(k * part, (k + 1) * part)
        columns += [
            jnp.where(first, total_0[:, cols], theirs[:, cols]),
            jnp.where(first, theirs[:, cols], total_0[:, cols]),
        ]
    summed = jnp.concatenate(columns, axis=1)
    if lax.axis_size("lat") > 1:
        summed = lax.psum(summed.astype(jnp.bfloat16), "lat").astype(f32)
    grad_weights = summed * (1.0 / math.sqrt(token_count))
    return (output.reshape(tokens.shape), grad_tokens.reshape(tokens.shape), grad_weights)


def solution(mesh):
    sizes = dict(mesh.shape)
    devices = mesh.devices.reshape(sizes["grp"], sizes["lon"] // 8, 2, 2, 2, sizes["lat"])
    finer = Mesh(devices, ("grp",) + LON + ("lat",))
    return jax.shard_map(
        on_device,
        mesh=finer,
        in_specs=(
            P("grp", "lat", LON, None),
            P(("grp", "lat"), LON),
            P(),
            P(),
            P(LON, None),
            P(),
            P(),
            P("lat", None, None),
            P("grp", "lat", LON, None),
        ),
        out_specs=(
            P("grp", "lat", LON, None),
            P("grp", "lat", LON, None),
            P(("grp",) + LON, None),
        ),
        check_vma=False,
    )
```

```python
import functools
import math

import jax
import jax.numpy as jnp
from jax import lax
from jax.experimental import pallas as pl
from jax.experimental.pallas import tpu as pltpu
from jax.sharding import Mesh
from jax.sharding import PartitionSpec as P

epsilon = 1e-05
LON = ("far", "near", "side", "core")


def along_lon(shard, by):
    count = math.prod(lax.axis_size(axis) for axis in LON)
    return lax.ppermute(shard, LON, [(i, (i + by) % count) for i in range(count)])


def along_lat(shard, by):
    count = lax.axis_size("lat")
    return lax.ppermute(shard, "lat", [(i, (i + by) % count) for i in range(count)])


def swap(shard, axis):
    return lax.ppermute(shard, axis, [(0, 1), (1, 0)])


def pick(rows, cols, levels, side, over_rows):
    tile = levels * side * side
    shape = (tile, 2 * tile)
    target = lax.broadcasted_iota(jnp.int32, shape, 0)
    source = lax.broadcasted_iota(jnp.int32, shape, 1)
    level = target // (side * side)
    row = target // side % side
    col = target % side
    from_row = jnp.full_like(row, rows[levels - 1])
    from_col = jnp.full_like(col, cols[levels - 1])
    for l in range(levels - 1):
        from_row = jnp.where(level == l, rows[l], from_row)
        from_col = jnp.where(level == l, cols[l], from_col)
    from_row = row + from_row
    from_col = col + from_col
    which = (from_row if over_rows else from_col) // side
    wanted = which * tile + level * side * side + from_row % side * side + from_col % side
    return (source == wanted).astype(jnp.bfloat16)


def picked(onehot, first, second):
    both = jnp.concatenate([first, second], axis=0)
    return jnp.dot(onehot, both, preferred_element_type=jnp.float32).astype(jnp.bfloat16)


def roll_back(field, shifts, levels, side, wait):
    zeros = jnp.zeros_like(shifts[:, 0])
    rows = side - shifts[:, 0]
    more = lax.axis_size("lat") > 1
    field = picked(
        pick(zeros if more else rows, side - shifts[:, 1], levels, side, False),
        after(along_lon(field, 1), wait),
        field,
    )
    if more:
        field = picked(pick(rows, zeros, levels, side, True), along_lat(field, 1), field)
    return field


def turned_rolls(info_ref, gain_ref, *refs):
    fields, (kept_ref, sent_ref, both_ref, turned_ref, sems) = refs[:4], refs[4:]
    tile = fields[0].shape[0]
    rows = kept_ref.shape[1] // 8
    levels, side = 2, 8
    area = tile // levels
    copies = [
        pltpu.make_async_copy(field, both_ref.at[i // 2, pl.ds(i % 2 * tile, tile), :], sems.at[i])
        for i, field in enumerate(fields)
    ]
    for copy in copies:
        copy.start()
    target = lax.broadcasted_iota(jnp.int32, (tile, 2 * tile), 0)
    source = lax.broadcasted_iota(jnp.int32, (tile, 2 * tile), 1)
    upper = target < area
    row = ((target >> 3) & 7) + jnp.where(upper, info_ref[0], info_ref[2])
    col = (target & 7) + jnp.where(upper, info_ref[1], info_ref[3])
    wanted = jnp.where(col >= side, tile, 0) + jnp.where(upper, 0, area) + (row & 7) * side + (col & 7)
    onehot = jnp.where(source == wanted, 1.0, 0.0).astype(jnp.bfloat16)
    for k in (1, 0):
        copies[2 * k].wait()
        copies[2 * k + 1].wait()
        rolled = jnp.dot(onehot, both_ref[k], preferred_element_type=jnp.float32)
        if k == 0:
            center = rolled - jnp.mean(rolled, axis=-1, keepdims=True)
            spread = lax.rsqrt(jnp.mean(center * center, axis=-1, keepdims=True) + epsilon)
            rolled = center * spread * gain_ref[...]
        turned_ref[...] = rolled.T.astype(jnp.bfloat16)
        for i in range(8):
            at = pl.ds(i * rows, rows)
            kept_ref[k, at, :] = turned_ref[pl.ds(pl.multiple_of(info_ref[4 + i] * rows, 16), rows), :]
            sent_ref[k, at, :] = turned_ref[pl.ds(pl.multiple_of(info_ref[12 + i] * rows, 16), rows), :]


def down(a, b):
    return lax.dot_general(a, b, (((0,), (0,)), ((), ())), preferred_element_type=jnp.float32)


def across(a, b):
    return lax.dot_general(a, b, (((1,), (1,)), ((), ())), preferred_element_type=jnp.float32)


def products_kernel(place_ref, *refs):
    tiles, pieces = refs[:4], refs[4:12]
    kept_ref, sent_ref, full_ref, tile_ref, w_ref, sems, out_sem = refs[12:]
    tile = tiles[0].shape[2]
    part = w_ref.shape[1] // 4
    copies = []
    for i, piece in enumerate(pieces):
        rows = pl.ds(pl.multiple_of(place_ref[i] * piece.shape[0], 16), piece.shape[0])
        copies.append(pltpu.make_async_copy(piece, w_ref.at[rows, :], sems.at[i]))
    for j, source in enumerate(tiles):
        copies.append(pltpu.make_async_copy(source, tile_ref.at[j], sems.at[8 + j]))
    for copy in copies:
        copy.start()
    for copy in copies:
        copy.wait()
    out_copy = pltpu.make_async_copy(w_ref, full_ref, out_sem)
    out_copy.start()
    for j in (1, 3, 0, 2):
        rows = pl.ds(j // 2 * tile, tile)
        for n in range(4):
            cols = pl.ds(n * part, part)
            product = down(tile_ref[j, n // 3], w_ref[:, cols])
            if j % 2:
                sent_ref[rows, cols] = product.astype(jnp.bfloat16)
            else:
                kept_ref[rows, cols] = product
    out_copy.wait()


def attention_kernel(area, head, kept_ref, came_ref, bias_ref, grad_ref, qkv_ref, scores_ref, toward_ref, probs_ref, back_ref):
    part = grad_ref.shape[1] // 4
    levels, pairs = bias_ref.shape[:2]
    scale = 1.0 / math.sqrt(head)
    lane = lax.broadcasted_iota(jnp.int32, (area, 2 * head), 1)
    left = lane < head

    def stacked(pair):
        zero = jnp.zeros_like(pair)
        return jnp.concatenate([jnp.where(left, pair, zero), jnp.where(left, zero, pair)], axis=0)

    def unstacked(product):
        return jnp.where(left, product[:area], product[area:]).astype(jnp.bfloat16)

    windows = grad_ref.shape[0] // area
    groups = [(w * pairs + p, w, p) for w in range(windows) for p in range(pairs)]

    def view(w, p, n):
        return pl.ds(w * area, area), pl.ds(n * part + p * 2 * head, 2 * head)

    qkv_ref[...] = (kept_ref[...] + came_ref[...].astype(jnp.float32)).astype(jnp.bfloat16)
    for g, w, p in groups:
        scores_ref[g] = across(stacked(qkv_ref[view(w, p, 0)]), qkv_ref[view(w, p, 1)])
        toward_ref[g] = across(stacked(qkv_ref[view(w, p, 3)]), qkv_ref[view(w, p, 2)])
    for g, w, p in groups:
        scores = scores_ref[g] * scale + bias_ref[w % levels, p]
        expo = jnp.exp(scores - jnp.max(scores, axis=-1, keepdims=True))
        probs = expo / jnp.sum(expo, axis=-1, keepdims=True)
        grad_probs = toward_ref[g]
        inner = jnp.sum(probs * grad_probs, axis=-1, keepdims=True)
        probs_ref[g] = probs.astype(jnp.bfloat16)
        back_ref[g] = (probs * (grad_probs - inner) * scale).astype(jnp.bfloat16)
    for g, w, p in groups:
        probs_b, grad_scores = probs_ref[g], back_ref[g]
        grad_ref[view(w, p, 3)] = unstacked(
            jnp.dot(probs_b, qkv_ref[view(w, p, 2)], preferred_element_type=jnp.float32)
        )
        grad_ref[view(w, p, 0)] = unstacked(
            jnp.dot(grad_scores, qkv_ref[view(w, p, 1)], preferred_element_type=jnp.float32)
        )
        grad_ref[view(w, p, 2)] = down(probs_b, stacked(qkv_ref[view(w, p, 3)])).astype(jnp.bfloat16)
        grad_ref[view(w, p, 1)] = down(grad_scores, stacked(qkv_ref[view(w, p, 0)])).astype(jnp.bfloat16)


def weights_kernel(near_ref, *refs):
    tiles, (own_ref, other_ref), out_refs = refs[:4], refs[4:6], refs[6:14]
    tile_ref, sum_ref, sems = refs[14:]
    tile = tiles[0].shape[2]
    part = own_ref.shape[1] // 4
    rows = out_refs[0].shape[0]
    copies = [pltpu.make_async_copy(source, tile_ref.at[j], sems.at[j]) for j, source in enumerate(tiles)]
    for copy in copies:
        copy.start()
    for copy in copies:
        copy.wait()
    for n in range(4):
        cols = pl.ds(n * part, part)
        total = None
        for t in range(2):
            tokens = pl.ds(t * tile, tile)
            left = jnp.concatenate([tile_ref[2 * t, n // 3], tile_ref[2 * t + 1, n // 3]], axis=1)
            right = jnp.concatenate([own_ref[tokens, cols], other_ref[tokens, cols]], axis=0)
            product = jnp.dot(left, right, preferred_element_type=jnp.float32)
            total = product if total is None else total + product
        sum_ref[:, cols] = total.astype(jnp.bfloat16)
    near = near_ref[0]
    for i, out_ref in enumerate(out_refs):
        wanted = 1 - near if i % 2 == 0 else near
        out_ref[...] = sum_ref[pl.ds(pl.multiple_of((i // 2 * 2 + wanted) * rows, 16), rows), :]


def outer_kernel(place_ref, grad_ref, mine_ref, theirs_ref, own_ref, other_ref, w_ref, sems):
    tile = own_ref.shape[0]
    width = w_ref.shape[0]
    rows = width // 16
    part = w_ref.shape[1] // 4
    step = width // 4
    copies = []
    for i in range(16):
        source = (mine_ref if i < 8 else theirs_ref).at[pl.ds(i % 8 * rows, rows), :]
        into = w_ref.at[pl.ds(pl.multiple_of(place_ref[i] * rows, 16), rows), :]
        copies.append(pltpu.make_async_copy(source, into, sems.at[i]))
    for copy in copies:
        copy.start()
    for copy in copies:
        copy.wait()
    for n in range(4):
        at = pl.ds(n * step, step)
        for k, w_cols in enumerate((pl.ds(3 * part, part), pl.ds(0, 3 * part))):
            product = across(grad_ref[:, w_cols], w_ref[at, w_cols])
            cols = pl.ds(k * width + n * step, step)
            own_ref[:, cols] = product[:tile]
            other_ref[:, cols] = product[tile:].astype(jnp.bfloat16)


def after(value, earlier):
    return lax.optimization_barrier((value, earlier))[0]


def kernel_call(body, outs, in_specs, out_specs, scratch, flops, moved, name, room=58):
    return pl.pallas_call(
        body,
        out_shape=outs,
        in_specs=in_specs,
        out_specs=out_specs,
        scratch_shapes=scratch,
        compiler_params=pltpu.CompilerParams(vmem_limit_bytes=room * 1024 * 1024),
        cost_estimate=pl.CostEstimate(flops=flops, bytes_accessed=moved, transcendentals=0),
        name=name,
    )


def on_device(tokens, land, surface, gain, weights, shifts, index_table, bias_table, cotangent):
    levels, side, _, width = tokens.shape
    area = side * side
    tile = levels * area
    heads = bias_table.shape[2]
    entries = bias_table.shape[1]
    own_rows = weights.shape[0]
    part = weights.shape[1] // 8
    head = weights.shape[1] // 4 // heads
    own_heads = heads // 2
    far, near, beside, core = (lax.axis_index(axis) for axis in LON)
    grp = lax.axis_index("grp")
    first = near == 0
    f32 = jnp.float32

    def place(f, n, s, c):
        return ((far ^ f) * 4 + (near ^ n) * 2 + (beside ^ s)) * 2 + (core ^ c)

    low = jnp.concatenate([weights[:, 2 * k * part : (2 * k + 1) * part] for k in range(4)], axis=1)
    high = jnp.concatenate([weights[:, (2 * k + 1) * part : (2 * k + 2) * part] for k in range(4)], axis=1)
    mine = jnp.where(first, low, high)
    came = swap(jnp.where(first, high, low), "near")
    flat_cot = cotangent.reshape(tile, width)
    surface_term = jnp.where(land[None, :, :, None] == 1, surface[1], surface[0])
    stream = (tokens.astype(f32) + surface_term).astype(jnp.bfloat16).reshape(tile, width)
    values = stream.astype(f32)
    center = values - jnp.mean(values, axis=-1, keepdims=True)
    spread = lax.rsqrt(jnp.mean(center * center, axis=-1, keepdims=True) + epsilon)

    held = near ^ grp
    half_piece = jnp.where(grp == 0, mine, came)
    across_far = swap(half_piece, "far")
    order = [(f, s, n) for f in (1, 0) for s in (1, 0) for n in (0, 1)]
    natural = [place(f, near ^ n, s, c) for c in (0, 1) for f, s, n in order]

    vmem = pl.BlockSpec(memory_space=pltpu.VMEM)
    smem = pl.BlockSpec(memory_space=pltpu.SMEM)
    anywhere = pl.BlockSpec(memory_space=pl.ANY)
    dma = pltpu.SemaphoreType.DMA

    rows, below, below_cot = shifts[:, 0], stream, flat_cot
    if lax.axis_size("lat") > 1:
        zeros = jnp.zeros_like(rows)
        onehot_rows = pick(rows, zeros, levels, side, True)
        below = picked(onehot_rows, stream, along_lat(stream, -1))
        below_cot = picked(onehot_rows, flat_cot, along_lat(flat_cot, -1))
        rows = zeros
    info = jnp.concatenate(
        [jnp.stack([rows, shifts[:, 1]], axis=1).reshape(-1), jnp.stack(natural)]
    ).astype(jnp.int32)
    half = width // 2
    turned = jax.ShapeDtypeStruct((2, half, tile), jnp.bfloat16)
    own_turned, sent_turned = kernel_call(
        turned_rolls,
        (turned, turned),
        [smem, vmem] + [anywhere] * 4,
        (vmem, vmem),
        [
            pltpu.VMEM((2, 2 * tile, width), jnp.bfloat16),
            pltpu.VMEM((width, tile), jnp.bfloat16),
            dma((4,)),
        ],
        2 * 2 * 2 * tile * tile * width,
        3_000_000,
        "turned_rolls",
    )(info, gain.reshape(1, -1), below, along_lon(below, -1), below_cot, along_lon(below_cot, -1))
    half_side = swap(after(half_piece, own_turned), "side")
    far_side = swap(across_far, "side")
    side_grp, far_grp = swap(half_side, "grp"), swap(across_far, "grp")
    pieces = [
        (mine, 0, 0, near),
        (came, 0, 0, 1 - near),
        (half_side, 0, 1, held),
        (side_grp, 0, 1, 1 - held),
        (across_far, 1, 0, held),
        (far_grp, 1, 0, 1 - held),
        (far_side, 1, 1, held),
        (swap(far_side, "grp"), 1, 1, 1 - held),
    ]
    places = jnp.stack([(1 - f) * 4 + (1 - s) * 2 + n for _, f, s, n in pieces]).astype(jnp.int32)
    own_near, sent_near = swap(own_turned, "near"), swap(sent_turned, "near")
    tiles = [own_turned, swap(after(sent_turned, (sent_near, side_grp)), "core"), own_near, swap(after(sent_near, (far_grp, side_grp)), "core")]

    onehot = (index_table[:, :, None] == jnp.arange(entries, dtype=jnp.int32)).astype(f32)
    own_table = lax.dynamic_slice_in_dim(bias_table, near * own_heads, own_heads, 2)
    bias = jnp.einsum("qkr,lrh->lhqk", onehot, own_table, precision=lax.Precision.HIGHEST)
    row_number = lax.axis_index("lat") * side + jnp.arange(side, dtype=jnp.int32)
    group = row_number[None, :] >= (side * lax.axis_size("lat") - shifts[:, 0])[:, None]
    group = jnp.repeat(group, side, axis=1)
    allowed = group[:, :, None] == group[:, None, :]
    bias = jnp.where(allowed[:, None], bias, -1e30).reshape(levels, own_heads // 2, 2 * area, area)

    bf16 = jnp.bfloat16
    kept, sent, w_mine = kernel_call(
        products_kernel,
        (
            jax.ShapeDtypeStruct((2 * tile, 4 * part), f32),
            jax.ShapeDtypeStruct((2 * tile, 4 * part), bf16),
            jax.ShapeDtypeStruct((half, 4 * part), bf16),
        ),
        [smem] + [anywhere] * 12,
        (vmem, vmem, anywhere),
        [
            pltpu.VMEM((4, 2, half, tile), bf16),
            pltpu.VMEM((half, 4 * part), bf16),
            dma((12,)),
            dma,
        ],
        1_200_000_000,
        9_000_000,
        "products",
    )(after(places, bias), *tiles, *[piece for piece, *_ in pieces])
    crossed = swap(sent, "core")
    grad = kernel_call(
        functools.partial(attention_kernel, area, head),
        jax.ShapeDtypeStruct((2 * tile, 4 * part), bf16),
        [vmem] * 3,
        vmem,
        [pltpu.VMEM((2 * tile, 4 * part), bf16)]
        + [pltpu.VMEM((2 * tile // area * own_heads // 2, 2 * area, area), kind) for kind in (f32, f32, bf16, bf16)],
        1_000_000_000,
        4_000_000,
        "attention",
    )(kept, crossed, bias)
    w_theirs = swap(after(w_mine, crossed), "core")
    grad_theirs = swap(grad, "core")
    attended_own, attended_other = kernel_call(
        outer_kernel,
        (
            jax.ShapeDtypeStruct((tile, 2 * width), f32),
            jax.ShapeDtypeStruct((tile, 2 * width), bf16),
        ),
        [smem, vmem, anywhere, anywhere],
        (vmem, vmem),
        [pltpu.VMEM((width, 4 * part), bf16), dma((16,))],
        1_200_000_000,
        8_000_000,
        "projections",
        24,
    )(jnp.stack(natural).astype(jnp.int32), grad, w_mine, w_theirs)
    blocks = kernel_call(
        weights_kernel,
        [jax.ShapeDtypeStruct((own_rows, 4 * part), bf16)] * 8,
        [smem] + [anywhere] * 4 + [vmem] * 2,
        [vmem] * 8,
        [
            pltpu.VMEM((4, 2, half, tile), bf16),
            pltpu.VMEM((half, 4 * part), bf16),
            dma((4,)),
        ],
        1_200_000_000,
        6_000_000,
        "weight_gradient",
        24,
    )(after(near.astype(jnp.int32).reshape(1), attended_other), *tiles, grad, grad_theirs)

    def block(f, s, n):
        return blocks[((1 - f) * 2 + 1 - s) * 2 + 1 - n]

    side_far_1 = swap(block(1, 1, 1), "side")
    arrived_back = swap(attended_other, "near")
    side_far_0 = swap(after(block(1, 1, 0), (side_far_1, arrived_back)), "side")
    far_1 = swap((block(1, 0, 1).astype(f32) + side_far_1.astype(f32)).astype(bf16), "far")
    far_0 = swap(after((block(1, 0, 0).astype(f32) + side_far_0.astype(f32)).astype(bf16), side_far_1), "far")
    side_1 = swap(after(block(0, 1, 1), side_far_0), "side")
    side_0 = swap(after(block(0, 1, 0), side_1), "side")
    total_1 = (block(0, 0, 1).astype(f32) + side_1.astype(f32) + far_1.astype(f32)).astype(bf16)
    theirs = swap(total_1, "near").astype(f32)

    back = (attended_own + arrived_back.astype(f32)).astype(jnp.bfloat16)
    back = roll_back(back, shifts, levels, side, far_0)
    output = (values + back[:, :width].astype(f32)).astype(jnp.bfloat16)
    scaled = center * spread
    upstream = back[:, width:].astype(f32) * gain
    grad_stream = spread * (
        upstream
        - jnp.mean(upstream, axis=-1, keepdims=True)
        - scaled * jnp.mean(upstream * scaled, axis=-1, keepdims=True)
    )
    grad_tokens = (flat_cot.astype(f32) + grad_stream).astype(jnp.bfloat16)

    far_0 = after(far_0, (output, grad_tokens))
    total_0 = block(0, 0, 0).astype(f32) + side_0.astype(f32) + far_0.astype(f32)
    token_count = tile * lax.axis_size("lat") * math.prod(lax.axis_size(axis) for axis in LON)
    columns = []
    for k in range(4):
        cols = slice(k * part, (k + 1) * part)
        columns += [
            jnp.where(first, total_0[:, cols], theirs[:, cols]),
            jnp.where(first, theirs[:, cols], total_0[:, cols]),
        ]
    summed = jnp.concatenate(columns, axis=1)
    if lax.axis_size("lat") > 1:
        summed = lax.psum(summed.astype(jnp.bfloat16), "lat").astype(f32)
    grad_weights = summed * (1.0 / math.sqrt(token_count))
    return (output.reshape(tokens.shape), grad_tokens.reshape(tokens.shape), grad_weights)


def solution(mesh):
    sizes = dict(mesh.shape)
    devices = mesh.devices.reshape(sizes["grp"], sizes["lon"] // 8, 2, 2, 2, sizes["lat"])
    finer = Mesh(devices, ("grp",) + LON + ("lat",))
    return jax.shard_map(
        on_device,
        mesh=finer,
        in_specs=(
            P("grp", "lat", LON, None),
            P(("grp", "lat"), LON),
            P(),
            P(),
            P(LON, None),
            P(),
            P(),
            P("lat", None, None),
            P("grp", "lat", LON, None),
        ),
        out_specs=(
            P("grp", "lat", LON, None),
            P("grp", "lat", LON, None),
            P(("grp",) + LON, None),
        ),
        check_vma=False,
    )
```

```python
import functools
import math

import jax
import jax.numpy as jnp
from jax import lax
from jax.experimental import pallas as pl
from jax.experimental.pallas import tpu as pltpu
from jax.sharding import Mesh
from jax.sharding import PartitionSpec as P

epsilon = 1e-05
LON = ("far", "near", "side", "core")


def along_lon(shard, by):
    count = math.prod(lax.axis_size(axis) for axis in LON)
    return lax.ppermute(shard, LON, [(i, (i + by) % count) for i in range(count)])


def along_lat(shard, by):
    count = lax.axis_size("lat")
    return lax.ppermute(shard, "lat", [(i, (i + by) % count) for i in range(count)])


def swap(shard, axis):
    return lax.ppermute(shard, axis, [(0, 1), (1, 0)])


def pick(rows, cols, levels, side, over_rows):
    tile = levels * side * side
    shape = (tile, 2 * tile)
    target = lax.broadcasted_iota(jnp.int32, shape, 0)
    source = lax.broadcasted_iota(jnp.int32, shape, 1)
    level = target // (side * side)
    row = target // side % side
    col = target % side
    from_row = jnp.full_like(row, rows[levels - 1])
    from_col = jnp.full_like(col, cols[levels - 1])
    for l in range(levels - 1):
        from_row = jnp.where(level == l, rows[l], from_row)
        from_col = jnp.where(level == l, cols[l], from_col)
    from_row = row + from_row
    from_col = col + from_col
    which = (from_row if over_rows else from_col) // side
    wanted = which * tile + level * side * side + from_row % side * side + from_col % side
    return (source == wanted).astype(jnp.bfloat16)


def picked(onehot, first, second):
    both = jnp.concatenate([first, second], axis=0)
    return jnp.dot(onehot, both, preferred_element_type=jnp.float32).astype(jnp.bfloat16)


def roll_back(field, shifts, levels, side, wait):
    zeros = jnp.zeros_like(shifts[:, 0])
    rows = side - shifts[:, 0]
    more = lax.axis_size("lat") > 1
    field = picked(
        pick(zeros if more else rows, side - shifts[:, 1], levels, side, False),
        after(along_lon(field, 1), wait),
        field,
    )
    if more:
        field = picked(pick(rows, zeros, levels, side, True), along_lat(field, 1), field)
    return field


def turned_rolls(info_ref, gain_ref, *refs):
    fields, (kept_ref, sent_ref, both_ref, turned_ref, sems) = refs[:4], refs[4:]
    tile = fields[0].shape[0]
    rows = kept_ref.shape[1] // 8
    levels, side = 2, 8
    area = tile // levels
    copies = [
        pltpu.make_async_copy(field, both_ref.at[i // 2, pl.ds(i % 2 * tile, tile), :], sems.at[i])
        for i, field in enumerate(fields)
    ]
    for copy in copies:
        copy.start()
    target = lax.broadcasted_iota(jnp.int32, (tile, 2 * tile), 0)
    source = lax.broadcasted_iota(jnp.int32, (tile, 2 * tile), 1)
    upper = target < area
    row = ((target >> 3) & 7) + jnp.where(upper, info_ref[0], info_ref[2])
    col = (target & 7) + jnp.where(upper, info_ref[1], info_ref[3])
    wanted = jnp.where(col >= side, tile, 0) + jnp.where(upper, 0, area) + (row & 7) * side + (col & 7)
    onehot = jnp.where(source == wanted, 1.0, 0.0).astype(jnp.bfloat16)
    for k in (1, 0):
        copies[2 * k].wait()
        copies[2 * k + 1].wait()
        rolled = jnp.dot(onehot, both_ref[k], preferred_element_type=jnp.float32)
        if k == 0:
            center = rolled - jnp.mean(rolled, axis=-1, keepdims=True)
            spread = lax.rsqrt(jnp.mean(center * center, axis=-1, keepdims=True) + epsilon)
            rolled = center * spread * gain_ref[...]
        turned_ref[...] = rolled.T.astype(jnp.bfloat16)
        for i in range(8):
            at = pl.ds(i * rows, rows)
            kept_ref[k, at, :] = turned_ref[pl.ds(pl.multiple_of(info_ref[4 + i] * rows, 16), rows), :]
            sent_ref[k, at, :] = turned_ref[pl.ds(pl.multiple_of(info_ref[12 + i] * rows, 16), rows), :]


def down(a, b):
    return lax.dot_general(a, b, (((0,), (0,)), ((), ())), preferred_element_type=jnp.float32)


def across(a, b):
    return lax.dot_general(a, b, (((1,), (1,)), ((), ())), preferred_element_type=jnp.float32)


def products_kernel(place_ref, *refs):
    tiles, pieces = refs[:4], refs[4:12]
    kept_ref, sent_ref, full_ref, tile_ref, w_ref, sems, out_sem = refs[12:]
    tile = tiles[0].shape[2]
    part = w_ref.shape[1] // 4
    copies = []
    for i, piece in enumerate(pieces):
        rows = pl.ds(pl.multiple_of(place_ref[i] * piece.shape[0], 16), piece.shape[0])
        copies.append(pltpu.make_async_copy(piece, w_ref.at[rows, :], sems.at[i]))
    for j, source in enumerate(tiles):
        copies.append(pltpu.make_async_copy(source, tile_ref.at[j], sems.at[8 + j]))
    for copy in copies:
        copy.start()
    for copy in copies:
        copy.wait()
    out_copy = pltpu.make_async_copy(w_ref, full_ref, out_sem)
    out_copy.start()
    for j in (1, 3, 0, 2):
        rows = pl.ds(j // 2 * tile, tile)
        for n in range(4):
            cols = pl.ds(n * part, part)
            product = down(tile_ref[j, n // 3], w_ref[:, cols])
            if j % 2:
                sent_ref[rows, cols] = product.astype(jnp.bfloat16)
            else:
                kept_ref[rows, cols] = product
    out_copy.wait()


def attention_kernel(area, head, kept_ref, came_ref, bias_ref, grad_ref, qkv_ref, scores_ref, toward_ref, probs_ref, back_ref):
    part = grad_ref.shape[1] // 4
    levels, pairs = bias_ref.shape[:2]
    scale = 1.0 / math.sqrt(head)
    lane = lax.broadcasted_iota(jnp.int32, (area, 2 * head), 1)
    left = lane < head

    def stacked(pair):
        zero = jnp.zeros_like(pair)
        return jnp.concatenate([jnp.where(left, pair, zero), jnp.where(left, zero, pair)], axis=0)

    def unstacked(product):
        return jnp.where(left, product[:area], product[area:]).astype(jnp.bfloat16)

    windows = grad_ref.shape[0] // area
    groups = [(w * pairs + p, w, p) for w in range(windows) for p in range(pairs)]

    def view(w, p, n):
        return pl.ds(w * area, area), pl.ds(n * part + p * 2 * head, 2 * head)

    qkv_ref[...] = (kept_ref[...] + came_ref[...].astype(jnp.float32)).astype(jnp.bfloat16)
    for g, w, p in groups:
        scores_ref[g] = across(stacked(qkv_ref[view(w, p, 0)]), qkv_ref[view(w, p, 1)])
        toward_ref[g] = across(stacked(qkv_ref[view(w, p, 3)]), qkv_ref[view(w, p, 2)])
    for g, w, p in groups:
        scores = scores_ref[g] * scale + bias_ref[w % levels, p]
        expo = jnp.exp(scores - jnp.max(scores, axis=-1, keepdims=True))
        probs = expo / jnp.sum(expo, axis=-1, keepdims=True)
        grad_probs = toward_ref[g]
        inner = jnp.sum(probs * grad_probs, axis=-1, keepdims=True)
        probs_ref[g] = probs.astype(jnp.bfloat16)
        back_ref[g] = (probs * (grad_probs - inner) * scale).astype(jnp.bfloat16)
    for g, w, p in groups:
        probs_b, grad_scores = probs_ref[g], back_ref[g]
        grad_ref[view(w, p, 3)] = unstacked(
            jnp.dot(probs_b, qkv_ref[view(w, p, 2)], preferred_element_type=jnp.float32)
        )
        grad_ref[view(w, p, 0)] = unstacked(
            jnp.dot(grad_scores, qkv_ref[view(w, p, 1)], preferred_element_type=jnp.float32)
        )
        grad_ref[view(w, p, 2)] = down(probs_b, stacked(qkv_ref[view(w, p, 3)])).astype(jnp.bfloat16)
        grad_ref[view(w, p, 1)] = down(grad_scores, stacked(qkv_ref[view(w, p, 0)])).astype(jnp.bfloat16)


def weights_kernel(near_ref, *refs):
    tiles, (own_ref, other_ref), out_refs = refs[:4], refs[4:6], refs[6:14]
    tile_ref, sum_ref, sems = refs[14:]
    tile = tiles[0].shape[2]
    part = own_ref.shape[1] // 4
    rows = out_refs[0].shape[0]
    copies = [pltpu.make_async_copy(source, tile_ref.at[j], sems.at[j]) for j, source in enumerate(tiles)]
    for copy in copies:
        copy.start()
    for copy in copies:
        copy.wait()
    for n in range(4):
        cols = pl.ds(n * part, part)
        total = None
        for t in range(2):
            tokens = pl.ds(t * tile, tile)
            left = jnp.concatenate([tile_ref[2 * t, n // 3], tile_ref[2 * t + 1, n // 3]], axis=1)
            right = jnp.concatenate([own_ref[tokens, cols], other_ref[tokens, cols]], axis=0)
            product = jnp.dot(left, right, preferred_element_type=jnp.float32)
            total = product if total is None else total + product
        sum_ref[:, cols] = total.astype(jnp.bfloat16)
    near = near_ref[0]
    for i, out_ref in enumerate(out_refs):
        wanted = 1 - near if i % 2 == 0 else near
        out_ref[...] = sum_ref[pl.ds(pl.multiple_of((i // 2 * 2 + wanted) * rows, 16), rows), :]


def outer_kernel(place_ref, grad_ref, mine_ref, theirs_ref, own_ref, other_ref, w_ref, sems):
    tile = own_ref.shape[0]
    width = w_ref.shape[0]
    rows = width // 16
    part = w_ref.shape[1] // 4
    step = width // 4
    copies = []
    for i in range(16):
        source = (mine_ref if i < 8 else theirs_ref).at[pl.ds(i % 8 * rows, rows), :]
        into = w_ref.at[pl.ds(pl.multiple_of(place_ref[i] * rows, 16), rows), :]
        copies.append(pltpu.make_async_copy(source, into, sems.at[i]))
    for copy in copies:
        copy.start()
    for copy in copies:
        copy.wait()
    for n in range(4):
        at = pl.ds(n * step, step)
        for k, w_cols in enumerate((pl.ds(3 * part, part), pl.ds(0, 3 * part))):
            product = across(grad_ref[:, w_cols], w_ref[at, w_cols])
            cols = pl.ds(k * width + n * step, step)
            own_ref[:, cols] = product[:tile]
            other_ref[:, cols] = product[tile:].astype(jnp.bfloat16)


def after(value, earlier):
    return lax.optimization_barrier((value, earlier))[0]


def kernel_call(body, outs, in_specs, out_specs, scratch, flops, moved, name, room=58):
    return pl.pallas_call(
        body,
        out_shape=outs,
        in_specs=in_specs,
        out_specs=out_specs,
        scratch_shapes=scratch,
        compiler_params=pltpu.CompilerParams(vmem_limit_bytes=room * 1024 * 1024),
        cost_estimate=pl.CostEstimate(flops=flops, bytes_accessed=moved, transcendentals=0),
        name=name,
    )


def on_device(tokens, land, surface, gain, weights, shifts, index_table, bias_table, cotangent):
    levels, side, _, width = tokens.shape
    area = side * side
    tile = levels * area
    heads = bias_table.shape[2]
    entries = bias_table.shape[1]
    own_rows = weights.shape[0]
    part = weights.shape[1] // 8
    head = weights.shape[1] // 4 // heads
    own_heads = heads // 2
    far, near, beside, core = (lax.axis_index(axis) for axis in LON)
    grp = lax.axis_index("grp")
    first = near == 0
    f32 = jnp.float32

    def place(f, n, s, c):
        return ((far ^ f) * 4 + (near ^ n) * 2 + (beside ^ s)) * 2 + (core ^ c)

    low = jnp.concatenate([weights[:, 2 * k * part : (2 * k + 1) * part] for k in range(4)], axis=1)
    high = jnp.concatenate([weights[:, (2 * k + 1) * part : (2 * k + 2) * part] for k in range(4)], axis=1)
    mine = jnp.where(first, low, high)
    came = swap(jnp.where(first, high, low), "near")
    flat_cot = cotangent.reshape(tile, width)
    surface_term = jnp.where(land[None, :, :, None] == 1, surface[1], surface[0])
    stream = (tokens.astype(f32) + surface_term).astype(jnp.bfloat16).reshape(tile, width)
    values = stream.astype(f32)
    center = values - jnp.mean(values, axis=-1, keepdims=True)
    spread = lax.rsqrt(jnp.mean(center * center, axis=-1, keepdims=True) + epsilon)

    held = near ^ grp
    half_piece = jnp.where(grp == 0, mine, came)
    across_far = swap(half_piece, "far")
    order = [(f, s, n) for f in (1, 0) for s in (1, 0) for n in (0, 1)]
    natural = [place(f, near ^ n, s, c) for c in (0, 1) for f, s, n in order]

    vmem = pl.BlockSpec(memory_space=pltpu.VMEM)
    smem = pl.BlockSpec(memory_space=pltpu.SMEM)
    anywhere = pl.BlockSpec(memory_space=pl.ANY)
    dma = pltpu.SemaphoreType.DMA

    rows, below, below_cot = shifts[:, 0], stream, flat_cot
    if lax.axis_size("lat") > 1:
        zeros = jnp.zeros_like(rows)
        onehot_rows = pick(rows, zeros, levels, side, True)
        below = picked(onehot_rows, stream, along_lat(stream, -1))
        below_cot = picked(onehot_rows, flat_cot, along_lat(flat_cot, -1))
        rows = zeros
    info = jnp.concatenate(
        [jnp.stack([rows, shifts[:, 1]], axis=1).reshape(-1), jnp.stack(natural)]
    ).astype(jnp.int32)
    half = width // 2
    turned = jax.ShapeDtypeStruct((2, half, tile), jnp.bfloat16)
    own_turned, sent_turned = kernel_call(
        turned_rolls,
        (turned, turned),
        [smem, vmem] + [anywhere] * 4,
        (vmem, vmem),
        [
            pltpu.VMEM((2, 2 * tile, width), jnp.bfloat16),
            pltpu.VMEM((width, tile), jnp.bfloat16),
            dma((4,)),
        ],
        2 * 2 * 2 * tile * tile * width,
        3_000_000,
        "turned_rolls",
    )(info, gain.reshape(1, -1), below, along_lon(below, -1), below_cot, along_lon(below_cot, -1))
    half_side = swap(after(half_piece, own_turned), "side")
    far_side = swap(across_far, "side")
    side_grp, far_grp = swap(half_side, "grp"), swap(across_far, "grp")
    pieces = [
        (mine, 0, 0, near),
        (came, 0, 0, 1 - near),
        (half_side, 0, 1, held),
        (side_grp, 0, 1, 1 - held),
        (across_far, 1, 0, held),
        (far_grp, 1, 0, 1 - held),
        (far_side, 1, 1, held),
        (swap(far_side, "grp"), 1, 1, 1 - held),
    ]
    places = jnp.stack([(1 - f) * 4 + (1 - s) * 2 + n for _, f, s, n in pieces]).astype(jnp.int32)
    own_near, sent_near = swap(own_turned, "near"), swap(sent_turned, "near")
    tiles = [own_turned, swap(after(sent_turned, (sent_near, side_grp)), "core"), own_near, swap(after(sent_near, (far_grp, side_grp)), "core")]

    onehot = (index_table[:, :, None] == jnp.arange(entries, dtype=jnp.int32)).astype(f32)
    own_table = lax.dynamic_slice_in_dim(bias_table, near * own_heads, own_heads, 2)
    bias = jnp.einsum("qkr,lrh->lhqk", onehot, own_table, precision=lax.Precision.HIGHEST)
    row_number = lax.axis_index("lat") * side + jnp.arange(side, dtype=jnp.int32)
    group = row_number[None, :] >= (side * lax.axis_size("lat") - shifts[:, 0])[:, None]
    group = jnp.repeat(group, side, axis=1)
    allowed = group[:, :, None] == group[:, None, :]
    bias = jnp.where(allowed[:, None], bias, -1e30).reshape(levels, own_heads // 2, 2 * area, area)

    bf16 = jnp.bfloat16
    kept, sent, w_mine = kernel_call(
        products_kernel,
        (
            jax.ShapeDtypeStruct((2 * tile, 4 * part), f32),
            jax.ShapeDtypeStruct((2 * tile, 4 * part), bf16),
            jax.ShapeDtypeStruct((half, 4 * part), bf16),
        ),
        [smem] + [anywhere] * 12,
        (vmem, vmem, anywhere),
        [
            pltpu.VMEM((4, 2, half, tile), bf16),
            pltpu.VMEM((half, 4 * part), bf16),
            dma((12,)),
            dma,
        ],
        1_200_000_000,
        9_000_000,
        "products",
    )(after(places, bias), *tiles, *[piece for piece, *_ in pieces])
    crossed = swap(sent, "core")
    grad = kernel_call(
        functools.partial(attention_kernel, area, head),
        jax.ShapeDtypeStruct((2 * tile, 4 * part), bf16),
        [vmem] * 3,
        vmem,
        [pltpu.VMEM((2 * tile, 4 * part), bf16)]
        + [pltpu.VMEM((2 * tile // area * own_heads // 2, 2 * area, area), kind) for kind in (f32, f32, bf16, bf16)],
        1_000_000_000,
        4_000_000,
        "attention",
    )(kept, crossed, bias)
    w_theirs = swap(after(w_mine, crossed), "core")
    grad_theirs = swap(grad, "core")
    attended_own, attended_other = kernel_call(
        outer_kernel,
        (
            jax.ShapeDtypeStruct((tile, 2 * width), f32),
            jax.ShapeDtypeStruct((tile, 2 * width), bf16),
        ),
        [smem, vmem, anywhere, anywhere],
        (vmem, vmem),
        [pltpu.VMEM((width, 4 * part), bf16), dma((16,))],
        1_200_000_000,
        8_000_000,
        "projections",
        24,
    )(jnp.stack(natural).astype(jnp.int32), grad, w_mine, w_theirs)
    blocks = kernel_call(
        weights_kernel,
        [jax.ShapeDtypeStruct((own_rows, 4 * part), bf16)] * 8,
        [smem] + [anywhere] * 4 + [vmem] * 2,
        [vmem] * 8,
        [
            pltpu.VMEM((4, 2, half, tile), bf16),
            pltpu.VMEM((half, 4 * part), bf16),
            dma((4,)),
        ],
        1_200_000_000,
        6_000_000,
        "weight_gradient",
        24,
    )(after(near.astype(jnp.int32).reshape(1), attended_other), *tiles, grad, grad_theirs)

    def block(f, s, n):
        return blocks[((1 - f) * 2 + 1 - s) * 2 + 1 - n]

    side_far_1 = swap(block(1, 1, 1), "side")
    arrived_back = swap(attended_other, "near")
    side_far_0 = swap(after(block(1, 1, 0), side_far_1), "side")
    side_far_0 = after(side_far_0, arrived_back)
    far_1 = swap((block(1, 0, 1).astype(f32) + side_far_1.astype(f32)).astype(bf16), "far")
    far_0 = swap(after((block(1, 0, 0).astype(f32) + side_far_0.astype(f32)).astype(bf16), side_far_1), "far")
    side_1 = swap(after(block(0, 1, 1), (side_far_0, arrived_back)), "side")
    side_0 = swap(after(block(0, 1, 0), side_1), "side")
    total_1 = (block(0, 0, 1).astype(f32) + side_1.astype(f32) + far_1.astype(f32)).astype(bf16)
    theirs = swap(total_1, "near").astype(f32)

    back = (attended_own + arrived_back.astype(f32)).astype(jnp.bfloat16)
    back = roll_back(back, shifts, levels, side, far_0)
    output = (values + back[:, :width].astype(f32)).astype(jnp.bfloat16)
    scaled = center * spread
    upstream = back[:, width:].astype(f32) * gain
    grad_stream = spread * (
        upstream
        - jnp.mean(upstream, axis=-1, keepdims=True)
        - scaled * jnp.mean(upstream * scaled, axis=-1, keepdims=True)
    )
    grad_tokens = (flat_cot.astype(f32) + grad_stream).astype(jnp.bfloat16)

    far_0 = after(far_0, (output, grad_tokens))
    total_0 = block(0, 0, 0).astype(f32) + side_0.astype(f32) + far_0.astype(f32)
    token_count = tile * lax.axis_size("lat") * math.prod(lax.axis_size(axis) for axis in LON)
    columns = []
    for k in range(4):
        cols = slice(k * part, (k + 1) * part)
        columns += [
            jnp.where(first, total_0[:, cols], theirs[:, cols]),
            jnp.where(first, theirs[:, cols], total_0[:, cols]),
        ]
    summed = jnp.concatenate(columns, axis=1)
    if lax.axis_size("lat") > 1:
        summed = lax.psum(summed.astype(jnp.bfloat16), "lat").astype(f32)
    grad_weights = summed * (1.0 / math.sqrt(token_count))
    return (output.reshape(tokens.shape), grad_tokens.reshape(tokens.shape), grad_weights)


def solution(mesh):
    sizes = dict(mesh.shape)
    devices = mesh.devices.reshape(sizes["grp"], sizes["lon"] // 8, 2, 2, 2, sizes["lat"])
    finer = Mesh(devices, ("grp",) + LON + ("lat",))
    return jax.shard_map(
        on_device,
        mesh=finer,
        in_specs=(
            P("grp", "lat", LON, None),
            P(("grp", "lat"), LON),
            P(),
            P(),
            P(LON, None),
            P(),
            P(),
            P("lat", None, None),
            P("grp", "lat", LON, None),
        ),
        out_specs=(
            P("grp", "lat", LON, None),
            P("grp", "lat", LON, None),
            P(("grp",) + LON, None),
        ),
        check_vma=False,
    )
```

```python
import functools
import math

import jax
import jax.numpy as jnp
from jax import lax
from jax.experimental import pallas as pl
from jax.experimental.pallas import tpu as pltpu
from jax.sharding import Mesh
from jax.sharding import PartitionSpec as P

epsilon = 1e-05
LON = ("far", "near", "side", "core")


def along_lon(shard, by):
    count = math.prod(lax.axis_size(axis) for axis in LON)
    return lax.ppermute(shard, LON, [(i, (i + by) % count) for i in range(count)])


def along_lat(shard, by):
    count = lax.axis_size("lat")
    return lax.ppermute(shard, "lat", [(i, (i + by) % count) for i in range(count)])


def swap(shard, axis):
    return lax.ppermute(shard, axis, [(0, 1), (1, 0)])


def pick(rows, cols, levels, side, over_rows):
    tile = levels * side * side
    shape = (tile, 2 * tile)
    target = lax.broadcasted_iota(jnp.int32, shape, 0)
    source = lax.broadcasted_iota(jnp.int32, shape, 1)
    level = target // (side * side)
    row = target // side % side
    col = target % side
    from_row = jnp.full_like(row, rows[levels - 1])
    from_col = jnp.full_like(col, cols[levels - 1])
    for l in range(levels - 1):
        from_row = jnp.where(level == l, rows[l], from_row)
        from_col = jnp.where(level == l, cols[l], from_col)
    from_row = row + from_row
    from_col = col + from_col
    which = (from_row if over_rows else from_col) // side
    wanted = which * tile + level * side * side + from_row % side * side + from_col % side
    return (source == wanted).astype(jnp.bfloat16)


def picked(onehot, first, second):
    both = jnp.concatenate([first, second], axis=0)
    return jnp.dot(onehot, both, preferred_element_type=jnp.float32).astype(jnp.bfloat16)


def roll_back(field, shifts, levels, side, wait):
    zeros = jnp.zeros_like(shifts[:, 0])
    rows = side - shifts[:, 0]
    more = lax.axis_size("lat") > 1
    field = picked(
        pick(zeros if more else rows, side - shifts[:, 1], levels, side, False),
        after(along_lon(field, 1), wait),
        field,
    )
    if more:
        field = picked(pick(rows, zeros, levels, side, True), along_lat(field, 1), field)
    return field


def turned_rolls(info_ref, gain_ref, *refs):
    fields, (kept_ref, sent_ref, both_ref, turned_ref, sems) = refs[:4], refs[4:]
    tile = fields[0].shape[0]
    rows = kept_ref.shape[1] // 8
    levels, side = 2, 8
    area = tile // levels
    copies = [
        pltpu.make_async_copy(field, both_ref.at[i // 2, pl.ds(i % 2 * tile, tile), :], sems.at[i])
        for i, field in enumerate(fields)
    ]
    for copy in copies:
        copy.start()
    target = lax.broadcasted_iota(jnp.int32, (tile, 2 * tile), 0)
    source = lax.broadcasted_iota(jnp.int32, (tile, 2 * tile), 1)
    upper = target < area
    row = ((target >> 3) & 7) + jnp.where(upper, info_ref[0], info_ref[2])
    col = (target & 7) + jnp.where(upper, info_ref[1], info_ref[3])
    wanted = jnp.where(col >= side, tile, 0) + jnp.where(upper, 0, area) + (row & 7) * side + (col & 7)
    onehot = jnp.where(source == wanted, 1.0, 0.0).astype(jnp.bfloat16)
    for k in (1, 0):
        copies[2 * k].wait()
        copies[2 * k + 1].wait()
        rolled = jnp.dot(onehot, both_ref[k], preferred_element_type=jnp.float32)
        if k == 0:
            center = rolled - jnp.mean(rolled, axis=-1, keepdims=True)
            spread = lax.rsqrt(jnp.mean(center * center, axis=-1, keepdims=True) + epsilon)
            rolled = center * spread * gain_ref[...]
        turned_ref[...] = rolled.astype(jnp.bfloat16).T
        for i in range(8):
            at = pl.ds(i * rows, rows)
            kept_ref[k, at, :] = turned_ref[pl.ds(pl.multiple_of(info_ref[4 + i] * rows, 16), rows), :]
            sent_ref[k, at, :] = turned_ref[pl.ds(pl.multiple_of(info_ref[12 + i] * rows, 16), rows), :]


def down(a, b):
    return lax.dot_general(a, b, (((0,), (0,)), ((), ())), preferred_element_type=jnp.float32)


def across(a, b):
    return lax.dot_general(a, b, (((1,), (1,)), ((), ())), preferred_element_type=jnp.float32)


def products_kernel(place_ref, *refs):
    tiles, pieces = refs[:4], refs[4:12]
    kept_ref, sent_ref, full_ref, tile_ref, x_ref, w_ref, sems, out_sem = refs[12:]
    tile = tiles[0].shape[2]
    part = w_ref.shape[1] // 4
    copies = []
    for i, piece in enumerate(pieces):
        rows = pl.ds(pl.multiple_of(place_ref[i] * piece.shape[0], 16), piece.shape[0])
        copies.append(pltpu.make_async_copy(piece, w_ref.at[rows, :], sems.at[i]))
    for j, source in enumerate(tiles):
        copies.append(pltpu.make_async_copy(source, tile_ref.at[j], sems.at[8 + j]))
    for copy in copies:
        copy.start()
    for j, at in enumerate((0, 2, 1, 3)):
        copies[8 + j].wait()
        for kind in range(2):
            x_ref[kind, pl.ds(at * tile, tile), :] = tile_ref[j, kind].T
    for copy in copies[:8]:
        copy.wait()
    out_copy = pltpu.make_async_copy(w_ref, full_ref, out_sem)
    out_copy.start()
    for n in range(4):
        cols = pl.ds(n * part, part)
        product = jnp.dot(x_ref[n // 3], w_ref[:, cols], preferred_element_type=jnp.float32)
        kept_ref[:, cols] = product[: 2 * tile]
        sent_ref[:, cols] = product[2 * tile :].astype(jnp.bfloat16)
    out_copy.wait()


def attention_kernel(area, head, kept_ref, came_ref, bias_ref, grad_ref, qkv_ref, scores_ref, toward_ref, probs_ref, back_ref):
    part = grad_ref.shape[1] // 4
    levels, pairs = bias_ref.shape[:2]
    scale = 1.0 / math.sqrt(head)
    lane = lax.broadcasted_iota(jnp.int32, (area, 2 * head), 1)
    left = lane < head

    def stacked(pair):
        zero = jnp.zeros_like(pair)
        return jnp.concatenate([jnp.where(left, pair, zero), jnp.where(left, zero, pair)], axis=0)

    def unstacked(product):
        return jnp.where(left, product[:area], product[area:]).astype(jnp.bfloat16)

    windows = grad_ref.shape[0] // area
    groups = [(w * pairs + p, w, p) for w in range(windows) for p in range(pairs)]

    def view(w, p, n):
        return pl.ds(w * area, area), pl.ds(n * part + p * 2 * head, 2 * head)

    qkv_ref[...] = (kept_ref[...] + came_ref[...].astype(jnp.float32)).astype(jnp.bfloat16)
    for g, w, p in groups:
        scores_ref[g] = across(stacked(qkv_ref[view(w, p, 0)]), qkv_ref[view(w, p, 1)])
        toward_ref[g] = across(stacked(qkv_ref[view(w, p, 3)]), qkv_ref[view(w, p, 2)])
    for g, w, p in groups:
        scores = scores_ref[g] * scale + bias_ref[w % levels, p]
        expo = jnp.exp(scores - jnp.max(scores, axis=-1, keepdims=True))
        probs = expo / jnp.sum(expo, axis=-1, keepdims=True)
        grad_probs = toward_ref[g]
        inner = jnp.sum(probs * grad_probs, axis=-1, keepdims=True)
        probs_ref[g] = probs.astype(jnp.bfloat16)
        back_ref[g] = (probs * (grad_probs - inner) * scale).astype(jnp.bfloat16)
    for g, w, p in groups:
        probs_b, grad_scores = probs_ref[g], back_ref[g]
        grad_ref[view(w, p, 3)] = unstacked(
            jnp.dot(probs_b, qkv_ref[view(w, p, 2)], preferred_element_type=jnp.float32)
        )
        grad_ref[view(w, p, 0)] = unstacked(
            jnp.dot(grad_scores, qkv_ref[view(w, p, 1)], preferred_element_type=jnp.float32)
        )
        grad_ref[view(w, p, 2)] = down(probs_b, stacked(qkv_ref[view(w, p, 3)])).astype(jnp.bfloat16)
        grad_ref[view(w, p, 1)] = down(grad_scores, stacked(qkv_ref[view(w, p, 0)])).astype(jnp.bfloat16)


def weights_kernel(near_ref, *refs):
    tiles, (own_ref, other_ref), out_refs = refs[:4], refs[4:6], refs[6:14]
    tile_ref, sum_ref, sems = refs[14:]
    tile = tiles[0].shape[2]
    part = own_ref.shape[1] // 4
    rows = out_refs[0].shape[0]
    copies = [pltpu.make_async_copy(source, tile_ref.at[j], sems.at[j]) for j, source in enumerate(tiles)]
    for copy in copies:
        copy.start()
    for copy in copies:
        copy.wait()
    for n in range(4):
        cols = pl.ds(n * part, part)
        total = None
        for t in range(2):
            tokens = pl.ds(t * tile, tile)
            left = jnp.concatenate([tile_ref[2 * t, n // 3], tile_ref[2 * t + 1, n // 3]], axis=1)
            right = jnp.concatenate([own_ref[tokens, cols], other_ref[tokens, cols]], axis=0)
            product = jnp.dot(left, right, preferred_element_type=jnp.float32)
            total = product if total is None else total + product
        sum_ref[:, cols] = total.astype(jnp.bfloat16)
    near = near_ref[0]
    for i, out_ref in enumerate(out_refs):
        wanted = 1 - near if i % 2 == 0 else near
        out_ref[...] = sum_ref[pl.ds(pl.multiple_of((i // 2 * 2 + wanted) * rows, 16), rows), :]


def outer_kernel(place_ref, grad_ref, mine_ref, theirs_ref, own_ref, other_ref, w_ref, sems):
    tile = own_ref.shape[0]
    width = w_ref.shape[0]
    rows = width // 16
    part = w_ref.shape[1] // 4
    step = width // 4
    copies = []
    for i in range(16):
        source = (mine_ref if i < 8 else theirs_ref).at[pl.ds(i % 8 * rows, rows), :]
        into = w_ref.at[pl.ds(pl.multiple_of(place_ref[i] * rows, 16), rows), :]
        copies.append(pltpu.make_async_copy(source, into, sems.at[i]))
    for copy in copies:
        copy.start()
    for copy in copies:
        copy.wait()
    for n in range(4):
        at = pl.ds(n * step, step)
        for k, w_cols in enumerate((pl.ds(3 * part, part), pl.ds(0, 3 * part))):
            product = across(grad_ref[:, w_cols], w_ref[at, w_cols])
            cols = pl.ds(k * width + n * step, step)
            own_ref[:, cols] = product[:tile]
            other_ref[:, cols] = product[tile:].astype(jnp.bfloat16)


def after(value, earlier):
    return lax.optimization_barrier((value, earlier))[0]


def kernel_call(body, outs, in_specs, out_specs, scratch, flops, moved, name, room=58):
    return pl.pallas_call(
        body,
        out_shape=outs,
        in_specs=in_specs,
        out_specs=out_specs,
        scratch_shapes=scratch,
        compiler_params=pltpu.CompilerParams(vmem_limit_bytes=room * 1024 * 1024),
        cost_estimate=pl.CostEstimate(flops=flops, bytes_accessed=moved, transcendentals=0),
        name=name,
    )


def on_device(tokens, land, surface, gain, weights, shifts, index_table, bias_table, cotangent):
    levels, side, _, width = tokens.shape
    area = side * side
    tile = levels * area
    heads = bias_table.shape[2]
    entries = bias_table.shape[1]
    own_rows = weights.shape[0]
    part = weights.shape[1] // 8
    head = weights.shape[1] // 4 // heads
    own_heads = heads // 2
    far, near, beside, core = (lax.axis_index(axis) for axis in LON)
    grp = lax.axis_index("grp")
    first = near == 0
    f32 = jnp.float32

    def place(f, n, s, c):
        return ((far ^ f) * 4 + (near ^ n) * 2 + (beside ^ s)) * 2 + (core ^ c)

    low = jnp.concatenate([weights[:, 2 * k * part : (2 * k + 1) * part] for k in range(4)], axis=1)
    high = jnp.concatenate([weights[:, (2 * k + 1) * part : (2 * k + 2) * part] for k in range(4)], axis=1)
    mine = jnp.where(first, low, high)
    came = swap(jnp.where(first, high, low), "near")
    flat_cot = cotangent.reshape(tile, width)
    surface_term = jnp.where(land[None, :, :, None] == 1, surface[1], surface[0])
    stream = (tokens.astype(f32) + surface_term).astype(jnp.bfloat16).reshape(tile, width)
    values = stream.astype(f32)
    center = values - jnp.mean(values, axis=-1, keepdims=True)
    spread = lax.rsqrt(jnp.mean(center * center, axis=-1, keepdims=True) + epsilon)

    held = near ^ grp
    half_piece = jnp.where(grp == 0, mine, came)
    across_far = swap(half_piece, "far")
    order = [(f, s, n) for f in (1, 0) for s in (1, 0) for n in (0, 1)]
    natural = [place(f, near ^ n, s, c) for c in (0, 1) for f, s, n in order]

    vmem = pl.BlockSpec(memory_space=pltpu.VMEM)
    smem = pl.BlockSpec(memory_space=pltpu.SMEM)
    anywhere = pl.BlockSpec(memory_space=pl.ANY)
    dma = pltpu.SemaphoreType.DMA

    rows, below, below_cot = shifts[:, 0], stream, flat_cot
    if lax.axis_size("lat") > 1:
        zeros = jnp.zeros_like(rows)
        onehot_rows = pick(rows, zeros, levels, side, True)
        below = picked(onehot_rows, stream, along_lat(stream, -1))
        below_cot = picked(onehot_rows, flat_cot, along_lat(flat_cot, -1))
        rows = zeros
    moved, moved_cot = along_lon(below, -1), along_lon(below_cot, -1)
    info = jnp.concatenate(
        [jnp.stack([rows, shifts[:, 1]], axis=1).reshape(-1), jnp.stack(natural)]
    ).astype(jnp.int32)
    half = width // 2
    turned = jax.ShapeDtypeStruct((2, half, tile), jnp.bfloat16)
    own_turned, sent_turned = kernel_call(
        turned_rolls,
        (turned, turned),
        [smem, vmem] + [anywhere] * 4,
        (vmem, vmem),
        [
            pltpu.VMEM((2, 2 * tile, width), jnp.bfloat16),
            pltpu.VMEM((width, tile), jnp.bfloat16),
            dma((4,)),
        ],
        2 * 2 * 2 * tile * tile * width,
        3_000_000,
        "turned_rolls",
        24,
    )(info, gain.reshape(1, -1), below, moved, below_cot, moved_cot)
    mine_side = swap(after(mine, (moved, moved_cot)), "side")
    across_far = after(across_far, mine_side)
    far_side, far_grp = swap(across_far, "side"), swap(across_far, "grp")
    came_side = swap(after(came, far_side), "side")
    pieces = [
        (mine, 0, 0, near),
        (came, 0, 0, 1 - near),
        (mine_side, 0, 1, near),
        (came_side, 0, 1, 1 - near),
        (across_far, 1, 0, held),
        (far_grp, 1, 0, 1 - held),
        (far_side, 1, 1, held),
        (swap(far_side, "grp"), 1, 1, 1 - held),
    ]
    places = jnp.stack([(1 - f) * 4 + (1 - s) * 2 + n for _, f, s, n in pieces]).astype(jnp.int32)
    own_near, sent_near = swap(own_turned, "near"), swap(sent_turned, "near")
    tiles = [own_turned, swap(after(sent_turned, (sent_near, far_grp)), "core"), own_near, swap(after(sent_near, far_grp), "core")]

    onehot = (index_table[:, :, None] == jnp.arange(entries, dtype=jnp.int32)).astype(f32)
    own_table = lax.dynamic_slice_in_dim(bias_table, near * own_heads, own_heads, 2)
    bias = jnp.einsum("qkr,lrh->lhqk", onehot, own_table, precision=lax.Precision.HIGHEST)
    row_number = lax.axis_index("lat") * side + jnp.arange(side, dtype=jnp.int32)
    group = row_number[None, :] >= (side * lax.axis_size("lat") - shifts[:, 0])[:, None]
    group = jnp.repeat(group, side, axis=1)
    allowed = group[:, :, None] == group[:, None, :]
    bias = jnp.where(allowed[:, None], bias, -1e30).reshape(levels, own_heads // 2, 2 * area, area)

    bf16 = jnp.bfloat16
    kept, sent, w_mine = kernel_call(
        products_kernel,
        (
            jax.ShapeDtypeStruct((2 * tile, 4 * part), f32),
            jax.ShapeDtypeStruct((2 * tile, 4 * part), bf16),
            jax.ShapeDtypeStruct((half, 4 * part), bf16),
        ),
        [smem] + [anywhere] * 12,
        (vmem, vmem, anywhere),
        [
            pltpu.VMEM((4, 2, half, tile), bf16),
            pltpu.VMEM((2, 4 * tile, half), bf16),
            pltpu.VMEM((half, 4 * part), bf16),
            dma((12,)),
            dma,
        ],
        1_200_000_000,
        9_000_000,
        "products",
    )(after(places, bias), *tiles, *[piece for piece, *_ in pieces])
    crossed = swap(sent, "core")
    grad = kernel_call(
        functools.partial(attention_kernel, area, head),
        jax.ShapeDtypeStruct((2 * tile, 4 * part), bf16),
        [vmem] * 3,
        vmem,
        [pltpu.VMEM((2 * tile, 4 * part), bf16)]
        + [pltpu.VMEM((2 * tile // area * own_heads // 2, 2 * area, area), kind) for kind in (f32, f32, bf16, bf16)],
        1_000_000_000,
        4_000_000,
        "attention",
    )(kept, crossed, bias)
    w_theirs = swap(after(w_mine, crossed), "core")
    grad_theirs = swap(grad, "core")
    attended_own, attended_other = kernel_call(
        outer_kernel,
        (
            jax.ShapeDtypeStruct((tile, 2 * width), f32),
            jax.ShapeDtypeStruct((tile, 2 * width), bf16),
        ),
        [smem, vmem, anywhere, anywhere],
        (vmem, vmem),
        [pltpu.VMEM((width, 4 * part), bf16), dma((16,))],
        1_200_000_000,
        8_000_000,
        "projections",
        24,
    )(jnp.stack(natural).astype(jnp.int32), grad, w_mine, w_theirs)
    blocks = kernel_call(
        weights_kernel,
        [jax.ShapeDtypeStruct((own_rows, 4 * part), bf16)] * 8,
        [smem] + [anywhere] * 4 + [vmem] * 2,
        [vmem] * 8,
        [
            pltpu.VMEM((4, 2, half, tile), bf16),
            pltpu.VMEM((half, 4 * part), bf16),
            dma((4,)),
        ],
        1_200_000_000,
        6_000_000,
        "weight_gradient",
        24,
    )(after(near.astype(jnp.int32).reshape(1), attended_other), *tiles, grad, grad_theirs)

    def block(f, s, n):
        return blocks[((1 - f) * 2 + 1 - s) * 2 + 1 - n]

    side_far_1 = swap(block(1, 1, 1), "side")
    arrived_back = swap(attended_other, "near")
    side_far_0 = swap(after(block(1, 1, 0), side_far_1), "side")
    side_far_0 = after(side_far_0, arrived_back)
    far_1 = swap((block(1, 0, 1).astype(f32) + side_far_1.astype(f32)).astype(bf16), "far")
    far_0 = swap(after((block(1, 0, 0).astype(f32) + side_far_0.astype(f32)).astype(bf16), side_far_1), "far")
    side_1 = swap(after(block(0, 1, 1), (side_far_0, arrived_back)), "side")
    side_0 = swap(after(block(0, 1, 0), side_1), "side")
    total_1 = (block(0, 0, 1).astype(f32) + side_1.astype(f32) + far_1.astype(f32)).astype(bf16)
    theirs = swap(total_1, "near").astype(f32)

    back = (attended_own + arrived_back.astype(f32)).astype(jnp.bfloat16)
    back = roll_back(back, shifts, levels, side, far_0)
    output = (values + back[:, :width].astype(f32)).astype(jnp.bfloat16)
    scaled = center * spread
    upstream = back[:, width:].astype(f32) * gain
    grad_stream = spread * (
        upstream
        - jnp.mean(upstream, axis=-1, keepdims=True)
        - scaled * jnp.mean(upstream * scaled, axis=-1, keepdims=True)
    )
    grad_tokens = (flat_cot.astype(f32) + grad_stream).astype(jnp.bfloat16)

    far_0 = after(far_0, (output, grad_tokens))
    total_0 = block(0, 0, 0).astype(f32) + side_0.astype(f32) + far_0.astype(f32)
    token_count = tile * lax.axis_size("lat") * math.prod(lax.axis_size(axis) for axis in LON)
    columns = []
    for k in range(4):
        cols = slice(k * part, (k + 1) * part)
        columns += [
            jnp.where(first, total_0[:, cols], theirs[:, cols]),
            jnp.where(first, theirs[:, cols], total_0[:, cols]),
        ]
    summed = jnp.concatenate(columns, axis=1)
    if lax.axis_size("lat") > 1:
        summed = lax.psum(summed.astype(jnp.bfloat16), "lat").astype(f32)
    grad_weights = summed * (1.0 / math.sqrt(token_count))
    return (output.reshape(tokens.shape), grad_tokens.reshape(tokens.shape), grad_weights)


def solution(mesh):
    sizes = dict(mesh.shape)
    devices = mesh.devices.reshape(sizes["grp"], sizes["lon"] // 8, 2, 2, 2, sizes["lat"])
    finer = Mesh(devices, ("grp",) + LON + ("lat",))
    return jax.shard_map(
        on_device,
        mesh=finer,
        in_specs=(
            P("grp", "lat", LON, None),
            P(("grp", "lat"), LON),
            P(),
            P(),
            P(LON, None),
            P(),
            P(),
            P("lat", None, None),
            P("grp", "lat", LON, None),
        ),
        out_specs=(
            P("grp", "lat", LON, None),
            P("grp", "lat", LON, None),
            P(("grp",) + LON, None),
        ),
        check_vma=False,
    )
```

```python
import functools
import math

import jax
import jax.numpy as jnp
from jax import lax
from jax.experimental import pallas as pl
from jax.experimental.pallas import tpu as pltpu
from jax.sharding import Mesh
from jax.sharding import PartitionSpec as P

epsilon = 1e-05
LON = ("far", "near", "side", "core")


def along_lon(shard, by):
    count = math.prod(lax.axis_size(axis) for axis in LON)
    return lax.ppermute(shard, LON, [(i, (i + by) % count) for i in range(count)])


def along_lat(shard, by):
    count = lax.axis_size("lat")
    return lax.ppermute(shard, "lat", [(i, (i + by) % count) for i in range(count)])


def swap(shard, axis):
    return lax.ppermute(shard, axis, [(0, 1), (1, 0)])


def pick(rows, cols, levels, side, over_rows):
    tile = levels * side * side
    shape = (tile, 2 * tile)
    target = lax.broadcasted_iota(jnp.int32, shape, 0)
    source = lax.broadcasted_iota(jnp.int32, shape, 1)
    level = target // (side * side)
    row = target // side % side
    col = target % side
    from_row = jnp.full_like(row, rows[levels - 1])
    from_col = jnp.full_like(col, cols[levels - 1])
    for l in range(levels - 1):
        from_row = jnp.where(level == l, rows[l], from_row)
        from_col = jnp.where(level == l, cols[l], from_col)
    from_row = row + from_row
    from_col = col + from_col
    which = (from_row if over_rows else from_col) // side
    wanted = which * tile + level * side * side + from_row % side * side + from_col % side
    return (source == wanted).astype(jnp.bfloat16)


def picked(onehot, first, second):
    both = jnp.concatenate([first, second], axis=0)
    return jnp.dot(onehot, both, preferred_element_type=jnp.float32).astype(jnp.bfloat16)


def roll_back(field, shifts, levels, side, wait):
    zeros = jnp.zeros_like(shifts[:, 0])
    rows = side - shifts[:, 0]
    more = lax.axis_size("lat") > 1
    field = picked(
        pick(zeros if more else rows, side - shifts[:, 1], levels, side, False),
        after(along_lon(field, 1), wait),
        field,
    )
    if more:
        field = picked(pick(rows, zeros, levels, side, True), along_lat(field, 1), field)
    return field


def turned_rolls(info_ref, gain_ref, *refs):
    fields, (kept_ref, sent_ref, both_ref, turned_ref, sems) = refs[:4], refs[4:]
    tile = fields[0].shape[0]
    rows = kept_ref.shape[1] // 8
    levels, side = 2, 8
    area = tile // levels
    copies = [
        pltpu.make_async_copy(field, both_ref.at[i // 2, pl.ds(i % 2 * tile, tile), :], sems.at[i])
        for i, field in enumerate(fields)
    ]
    for copy in copies:
        copy.start()
    target = lax.broadcasted_iota(jnp.int32, (tile, 2 * tile), 0)
    source = lax.broadcasted_iota(jnp.int32, (tile, 2 * tile), 1)
    upper = target < area
    row = ((target >> 3) & 7) + jnp.where(upper, info_ref[0], info_ref[2])
    col = (target & 7) + jnp.where(upper, info_ref[1], info_ref[3])
    wanted = jnp.where(col >= side, tile, 0) + jnp.where(upper, 0, area) + (row & 7) * side + (col & 7)
    onehot = jnp.where(source == wanted, 1.0, 0.0).astype(jnp.bfloat16)
    for k in (1, 0):
        copies[2 * k].wait()
        copies[2 * k + 1].wait()
        rolled = jnp.dot(onehot, both_ref[k], preferred_element_type=jnp.float32)
        if k == 0:
            center = rolled - jnp.mean(rolled, axis=-1, keepdims=True)
            spread = lax.rsqrt(jnp.mean(center * center, axis=-1, keepdims=True) + epsilon)
            rolled = center * spread * gain_ref[...]
        turned_ref[...] = rolled.astype(jnp.bfloat16).T
        for i in range(8):
            at = pl.ds(i * rows, rows)
            kept_ref[k, at, :] = turned_ref[pl.ds(pl.multiple_of(info_ref[4 + i] * rows, 16), rows), :]
            sent_ref[k, at, :] = turned_ref[pl.ds(pl.multiple_of(info_ref[12 + i] * rows, 16), rows), :]


def down(a, b):
    return lax.dot_general(a, b, (((0,), (0,)), ((), ())), preferred_element_type=jnp.float32)


def across(a, b):
    return lax.dot_general(a, b, (((1,), (1,)), ((), ())), preferred_element_type=jnp.float32)


def products_kernel(place_ref, *refs):
    tiles, pieces = refs[:4], refs[4:12]
    kept_ref, sent_ref, full_ref, tile_ref, x_ref, w_ref, sems, out_sem = refs[12:]
    tile = tiles[0].shape[2]
    part = w_ref.shape[1] // 4
    copies = []
    for i, piece in enumerate(pieces):
        rows = pl.ds(pl.multiple_of(place_ref[i] * piece.shape[0], 16), piece.shape[0])
        copies.append(pltpu.make_async_copy(piece, w_ref.at[rows, :], sems.at[i]))
    for j, source in enumerate(tiles):
        copies.append(pltpu.make_async_copy(source, tile_ref.at[j], sems.at[8 + j]))
    for copy in copies:
        copy.start()
    for j, at in enumerate((0, 2, 1, 3)):
        copies[8 + j].wait()
        for kind in range(2):
            x_ref[kind, pl.ds(at * tile, tile), :] = tile_ref[j, kind].T
    for copy in copies[:8]:
        copy.wait()
    out_copy = pltpu.make_async_copy(w_ref, full_ref, out_sem)
    out_copy.start()
    for n in range(4):
        cols = pl.ds(n * part, part)
        product = jnp.dot(x_ref[n // 3], w_ref[:, cols], preferred_element_type=jnp.float32)
        kept_ref[:, cols] = product[: 2 * tile]
        sent_ref[:, cols] = product[2 * tile :].astype(jnp.bfloat16)
    out_copy.wait()


def attention_kernel(area, head, kept_ref, came_ref, bias_ref, grad_ref, qkv_ref, scores_ref, toward_ref, probs_ref, back_ref):
    part = grad_ref.shape[1] // 4
    levels, pairs = bias_ref.shape[:2]
    scale = 1.0 / math.sqrt(head)
    lane = lax.broadcasted_iota(jnp.int32, (area, 2 * head), 1)
    left = lane < head

    def stacked(pair):
        zero = jnp.zeros_like(pair)
        return jnp.concatenate([jnp.where(left, pair, zero), jnp.where(left, zero, pair)], axis=0)

    def unstacked(product):
        return jnp.where(left, product[:area], product[area:]).astype(jnp.bfloat16)

    windows = grad_ref.shape[0] // area
    groups = [(w * pairs + p, w, p) for w in range(windows) for p in range(pairs)]

    def view(w, p, n):
        return pl.ds(w * area, area), pl.ds(n * part + p * 2 * head, 2 * head)

    qkv_ref[...] = (kept_ref[...] + came_ref[...].astype(jnp.float32)).astype(jnp.bfloat16)
    for g, w, p in groups:
        scores_ref[g] = across(stacked(qkv_ref[view(w, p, 0)]), qkv_ref[view(w, p, 1)])
        toward_ref[g] = across(stacked(qkv_ref[view(w, p, 3)]), qkv_ref[view(w, p, 2)])
    for g, w, p in groups:
        scores = scores_ref[g] * scale + bias_ref[w % levels, p]
        expo = jnp.exp(scores - jnp.max(scores, axis=-1, keepdims=True))
        probs = expo / jnp.sum(expo, axis=-1, keepdims=True)
        grad_probs = toward_ref[g]
        inner = jnp.sum(probs * grad_probs, axis=-1, keepdims=True)
        probs_ref[g] = probs.astype(jnp.bfloat16)
        back_ref[g] = (probs * (grad_probs - inner) * scale).astype(jnp.bfloat16)
    for g, w, p in groups:
        probs_b, grad_scores = probs_ref[g], back_ref[g]
        grad_ref[view(w, p, 3)] = unstacked(
            jnp.dot(probs_b, qkv_ref[view(w, p, 2)], preferred_element_type=jnp.float32)
        )
        grad_ref[view(w, p, 0)] = unstacked(
            jnp.dot(grad_scores, qkv_ref[view(w, p, 1)], preferred_element_type=jnp.float32)
        )
        grad_ref[view(w, p, 2)] = down(probs_b, stacked(qkv_ref[view(w, p, 3)])).astype(jnp.bfloat16)
        grad_ref[view(w, p, 1)] = down(grad_scores, stacked(qkv_ref[view(w, p, 0)])).astype(jnp.bfloat16)


def weights_kernel(near_ref, *refs):
    tiles, (own_ref, other_ref), out_refs = refs[:4], refs[4:6], refs[6:14]
    tile_ref, sum_ref, sems = refs[14:]
    tile = tiles[0].shape[2]
    part = own_ref.shape[1] // 4
    rows = out_refs[0].shape[0]
    copies = [pltpu.make_async_copy(source, tile_ref.at[j], sems.at[j]) for j, source in enumerate(tiles)]
    for copy in copies:
        copy.start()
    for copy in copies:
        copy.wait()
    for n in range(4):
        cols = pl.ds(n * part, part)
        total = None
        for t in range(2):
            tokens = pl.ds(t * tile, tile)
            left = jnp.concatenate([tile_ref[2 * t, n // 3], tile_ref[2 * t + 1, n // 3]], axis=1)
            right = jnp.concatenate([own_ref[tokens, cols], other_ref[tokens, cols]], axis=0)
            product = jnp.dot(left, right, preferred_element_type=jnp.float32)
            total = product if total is None else total + product
        sum_ref[:, cols] = total.astype(jnp.bfloat16)
    near = near_ref[0]
    for i, out_ref in enumerate(out_refs):
        wanted = 1 - near if i % 2 == 0 else near
        out_ref[...] = sum_ref[pl.ds(pl.multiple_of((i // 2 * 2 + wanted) * rows, 16), rows), :]


def outer_kernel(place_ref, grad_ref, mine_ref, theirs_ref, own_ref, other_ref, w_ref, sems):
    tile = own_ref.shape[0]
    width = w_ref.shape[0]
    rows = width // 16
    part = w_ref.shape[1] // 4
    step = width // 4
    copies = []
    for i in range(16):
        source = (mine_ref if i < 8 else theirs_ref).at[pl.ds(i % 8 * rows, rows), :]
        into = w_ref.at[pl.ds(pl.multiple_of(place_ref[i] * rows, 16), rows), :]
        copies.append(pltpu.make_async_copy(source, into, sems.at[i]))
    for copy in copies:
        copy.start()
    for copy in copies:
        copy.wait()
    for n in range(4):
        at = pl.ds(n * step, step)
        for k, w_cols in enumerate((pl.ds(3 * part, part), pl.ds(0, 3 * part))):
            product = across(grad_ref[:, w_cols], w_ref[at, w_cols])
            cols = pl.ds(k * width + n * step, step)
            own_ref[:, cols] = product[:tile]
            other_ref[:, cols] = product[tile:].astype(jnp.bfloat16)


def after(value, earlier):
    return lax.optimization_barrier((value, earlier))[0]


def kernel_call(body, outs, in_specs, out_specs, scratch, flops, moved, name, room=58):
    return pl.pallas_call(
        body,
        out_shape=outs,
        in_specs=in_specs,
        out_specs=out_specs,
        scratch_shapes=scratch,
        compiler_params=pltpu.CompilerParams(vmem_limit_bytes=room * 1024 * 1024),
        cost_estimate=pl.CostEstimate(flops=flops, bytes_accessed=moved, transcendentals=0),
        name=name,
    )


def on_device(tokens, land, surface, gain, weights, shifts, index_table, bias_table, cotangent):
    levels, side, _, width = tokens.shape
    area = side * side
    tile = levels * area
    heads = bias_table.shape[2]
    entries = bias_table.shape[1]
    own_rows = weights.shape[0]
    part = weights.shape[1] // 8
    head = weights.shape[1] // 4 // heads
    own_heads = heads // 2
    far, near, beside, core = (lax.axis_index(axis) for axis in LON)
    grp = lax.axis_index("grp")
    first = near == 0
    f32 = jnp.float32

    def place(f, n, s, c):
        return ((far ^ f) * 4 + (near ^ n) * 2 + (beside ^ s)) * 2 + (core ^ c)

    low = jnp.concatenate([weights[:, 2 * k * part : (2 * k + 1) * part] for k in range(4)], axis=1)
    high = jnp.concatenate([weights[:, (2 * k + 1) * part : (2 * k + 2) * part] for k in range(4)], axis=1)
    mine = jnp.where(first, low, high)
    came = swap(jnp.where(first, high, low), "near")
    flat_cot = cotangent.reshape(tile, width)
    surface_term = jnp.where(land[None, :, :, None] == 1, surface[1], surface[0])
    stream = (tokens.astype(f32) + surface_term).astype(jnp.bfloat16).reshape(tile, width)
    values = stream.astype(f32)
    center = values - jnp.mean(values, axis=-1, keepdims=True)
    spread = lax.rsqrt(jnp.mean(center * center, axis=-1, keepdims=True) + epsilon)

    held = near ^ grp
    half_piece = jnp.where(grp == 0, mine, came)
    across_far = swap(half_piece, "far")
    order = [(f, s, n) for f in (1, 0) for s in (1, 0) for n in (0, 1)]
    natural = [place(f, near ^ n, s, c) for c in (0, 1) for f, s, n in order]

    vmem = pl.BlockSpec(memory_space=pltpu.VMEM)
    smem = pl.BlockSpec(memory_space=pltpu.SMEM)
    anywhere = pl.BlockSpec(memory_space=pl.ANY)
    dma = pltpu.SemaphoreType.DMA

    rows, below, below_cot = shifts[:, 0], stream, flat_cot
    if lax.axis_size("lat") > 1:
        zeros = jnp.zeros_like(rows)
        onehot_rows = pick(rows, zeros, levels, side, True)
        below = picked(onehot_rows, stream, along_lat(stream, -1))
        below_cot = picked(onehot_rows, flat_cot, along_lat(flat_cot, -1))
        rows = zeros
    moved, moved_cot = along_lon(below, -1), along_lon(below_cot, -1)
    info = jnp.concatenate(
        [jnp.stack([rows, shifts[:, 1]], axis=1).reshape(-1), jnp.stack(natural)]
    ).astype(jnp.int32)
    half = width // 2
    turned = jax.ShapeDtypeStruct((2, half, tile), jnp.bfloat16)
    own_turned, sent_turned = kernel_call(
        turned_rolls,
        (turned, turned),
        [smem, vmem] + [anywhere] * 4,
        (vmem, vmem),
        [
            pltpu.VMEM((2, 2 * tile, width), jnp.bfloat16),
            pltpu.VMEM((width, tile), jnp.bfloat16),
            dma((4,)),
        ],
        2 * 2 * 2 * tile * tile * width,
        3_000_000,
        "turned_rolls",
        24,
    )(info, gain.reshape(1, -1), below, moved, below_cot, moved_cot)
    mine_side = swap(after(mine, (moved, moved_cot)), "side")
    across_far = after(across_far, mine_side)
    far_side, far_grp = swap(across_far, "side"), swap(across_far, "grp")
    came_side = swap(after(came, far_side), "side")
    pieces = [
        (mine, 0, 0, near),
        (came, 0, 0, 1 - near),
        (mine_side, 0, 1, near),
        (came_side, 0, 1, 1 - near),
        (across_far, 1, 0, held),
        (far_grp, 1, 0, 1 - held),
        (far_side, 1, 1, held),
        (swap(far_side, "grp"), 1, 1, 1 - held),
    ]
    places = jnp.stack([(1 - f) * 4 + (1 - s) * 2 + n for _, f, s, n in pieces]).astype(jnp.int32)
    own_near, sent_near = swap(own_turned, "near"), swap(sent_turned, "near")
    tiles = [own_turned, swap(after(sent_turned, (sent_near, far_grp)), "core"), own_near, swap(after(sent_near, far_grp), "core")]

    onehot = (index_table[:, :, None] == jnp.arange(entries, dtype=jnp.int32)).astype(f32)
    own_table = lax.dynamic_slice_in_dim(bias_table, near * own_heads, own_heads, 2)
    bias = jnp.einsum("qkr,lrh->lhqk", onehot, own_table, precision=lax.Precision.HIGHEST)
    row_number = lax.axis_index("lat") * side + jnp.arange(side, dtype=jnp.int32)
    group = row_number[None, :] >= (side * lax.axis_size("lat") - shifts[:, 0])[:, None]
    group = jnp.repeat(group, side, axis=1)
    allowed = group[:, :, None] == group[:, None, :]
    bias = jnp.where(allowed[:, None], bias, -1e30).reshape(levels, own_heads // 2, 2 * area, area)

    bf16 = jnp.bfloat16
    kept, sent, w_mine = kernel_call(
        products_kernel,
        (
            jax.ShapeDtypeStruct((2 * tile, 4 * part), f32),
            jax.ShapeDtypeStruct((2 * tile, 4 * part), bf16),
            jax.ShapeDtypeStruct((half, 4 * part), bf16),
        ),
        [smem] + [anywhere] * 12,
        (vmem, vmem, anywhere),
        [
            pltpu.VMEM((4, 2, half, tile), bf16),
            pltpu.VMEM((2, 4 * tile, half), bf16),
            pltpu.VMEM((half, 4 * part), bf16),
            dma((12,)),
            dma,
        ],
        1_200_000_000,
        9_000_000,
        "products",
    )(after(places, bias), *tiles, *[piece for piece, *_ in pieces])
    crossed = swap(sent, "core")
    grad = kernel_call(
        functools.partial(attention_kernel, area, head),
        jax.ShapeDtypeStruct((2 * tile, 4 * part), bf16),
        [vmem] * 3,
        vmem,
        [pltpu.VMEM((2 * tile, 4 * part), bf16)]
        + [pltpu.VMEM((2 * tile // area * own_heads // 2, 2 * area, area), kind) for kind in (f32, f32, bf16, bf16)],
        1_000_000_000,
        4_000_000,
        "attention",
    )(kept, crossed, bias)
    w_theirs = swap(after(w_mine, crossed), "core")
    grad_theirs = swap(grad, "core")
    attended_own, attended_other = kernel_call(
        outer_kernel,
        (
            jax.ShapeDtypeStruct((tile, 2 * width), f32),
            jax.ShapeDtypeStruct((tile, 2 * width), bf16),
        ),
        [smem, vmem, anywhere, anywhere],
        (vmem, vmem),
        [pltpu.VMEM((width, 4 * part), bf16), dma((16,))],
        1_200_000_000,
        8_000_000,
        "projections",
        24,
    )(jnp.stack(natural).astype(jnp.int32), grad, w_mine, w_theirs)
    blocks = kernel_call(
        weights_kernel,
        [jax.ShapeDtypeStruct((own_rows, 4 * part), bf16)] * 8,
        [smem] + [anywhere] * 4 + [vmem] * 2,
        [vmem] * 8,
        [
            pltpu.VMEM((4, 2, half, tile), bf16),
            pltpu.VMEM((half, 4 * part), bf16),
            dma((4,)),
        ],
        1_200_000_000,
        6_000_000,
        "weight_gradient",
        24,
    )(after(near.astype(jnp.int32).reshape(1), attended_other), *tiles, grad, grad_theirs)

    def block(f, s, n):
        return blocks[((1 - f) * 2 + 1 - s) * 2 + 1 - n]

    side_far_1 = swap(block(1, 1, 1), "side")
    arrived_back = swap(attended_other, "near")
    side_far_0 = swap(after(block(1, 1, 0), side_far_1), "side")
    side_far_0 = after(side_far_0, arrived_back)
    far_1 = swap((block(1, 0, 1).astype(f32) + side_far_1.astype(f32)).astype(bf16), "far")
    far_0 = swap(after((block(1, 0, 0).astype(f32) + side_far_0.astype(f32)).astype(bf16), far_1), "far")
    side_1 = swap(after(block(0, 1, 1), (side_far_0, arrived_back)), "side")
    side_0 = swap(after(block(0, 1, 0), side_1), "side")
    total_1 = (block(0, 0, 1).astype(f32) + side_1.astype(f32) + far_1.astype(f32)).astype(bf16)
    theirs = swap(total_1, "near").astype(f32)

    back = (attended_own + arrived_back.astype(f32)).astype(jnp.bfloat16)
    back = after(roll_back(back, shifts, levels, side, far_1), far_0)
    output = (values + back[:, :width].astype(f32)).astype(jnp.bfloat16)
    scaled = center * spread
    upstream = back[:, width:].astype(f32) * gain
    grad_stream = spread * (
        upstream
        - jnp.mean(upstream, axis=-1, keepdims=True)
        - scaled * jnp.mean(upstream * scaled, axis=-1, keepdims=True)
    )
    grad_tokens = (flat_cot.astype(f32) + grad_stream).astype(jnp.bfloat16)

    far_0 = after(far_0, (output, grad_tokens))
    total_0 = block(0, 0, 0).astype(f32) + side_0.astype(f32) + far_0.astype(f32)
    token_count = tile * lax.axis_size("lat") * math.prod(lax.axis_size(axis) for axis in LON)
    columns = []
    for k in range(4):
        cols = slice(k * part, (k + 1) * part)
        columns += [
            jnp.where(first, total_0[:, cols], theirs[:, cols]),
            jnp.where(first, theirs[:, cols], total_0[:, cols]),
        ]
    summed = jnp.concatenate(columns, axis=1)
    if lax.axis_size("lat") > 1:
        summed = lax.psum(summed.astype(jnp.bfloat16), "lat").astype(f32)
    grad_weights = summed * (1.0 / math.sqrt(token_count))
    return (output.reshape(tokens.shape), grad_tokens.reshape(tokens.shape), grad_weights)


def solution(mesh):
    sizes = dict(mesh.shape)
    devices = mesh.devices.reshape(sizes["grp"], sizes["lon"] // 8, 2, 2, 2, sizes["lat"])
    finer = Mesh(devices, ("grp",) + LON + ("lat",))
    return jax.shard_map(
        on_device,
        mesh=finer,
        in_specs=(
            P("grp", "lat", LON, None),
            P(("grp", "lat"), LON),
            P(),
            P(),
            P(LON, None),
            P(),
            P(),
            P("lat", None, None),
            P("grp", "lat", LON, None),
        ),
        out_specs=(
            P("grp", "lat", LON, None),
            P("grp", "lat", LON, None),
            P(("grp",) + LON, None),
        ),
        check_vma=False,
    )
```

```python
import functools
import math

import jax
import jax.numpy as jnp
from jax import lax
from jax.experimental import pallas as pl
from jax.experimental.pallas import tpu as pltpu
from jax.sharding import Mesh
from jax.sharding import PartitionSpec as P

epsilon = 1e-05
LON = ("far", "near", "side", "core")


def along_lon(shard, by):
    count = math.prod(lax.axis_size(axis) for axis in LON)
    return lax.ppermute(shard, LON, [(i, (i + by) % count) for i in range(count)])


def along_lat(shard, by):
    count = lax.axis_size("lat")
    return lax.ppermute(shard, "lat", [(i, (i + by) % count) for i in range(count)])


def swap(shard, axis):
    return lax.ppermute(shard, axis, [(0, 1), (1, 0)])


def pick(rows, cols, levels, side, over_rows):
    tile = levels * side * side
    shape = (tile, 2 * tile)
    target = lax.broadcasted_iota(jnp.int32, shape, 0)
    source = lax.broadcasted_iota(jnp.int32, shape, 1)
    level = target // (side * side)
    row = target // side % side
    col = target % side
    from_row = jnp.full_like(row, rows[levels - 1])
    from_col = jnp.full_like(col, cols[levels - 1])
    for l in range(levels - 1):
        from_row = jnp.where(level == l, rows[l], from_row)
        from_col = jnp.where(level == l, cols[l], from_col)
    from_row = row + from_row
    from_col = col + from_col
    which = (from_row if over_rows else from_col) // side
    wanted = which * tile + level * side * side + from_row % side * side + from_col % side
    return (source == wanted).astype(jnp.bfloat16)


def picked(onehot, first, second):
    both = jnp.concatenate([first, second], axis=0)
    return jnp.dot(onehot, both, preferred_element_type=jnp.float32).astype(jnp.bfloat16)


def roll_back(field, shifts, levels, side, wait):
    zeros = jnp.zeros_like(shifts[:, 0])
    rows = side - shifts[:, 0]
    more = lax.axis_size("lat") > 1
    field = picked(
        pick(zeros if more else rows, side - shifts[:, 1], levels, side, False),
        after(along_lon(field, 1), wait),
        field,
    )
    if more:
        field = picked(pick(rows, zeros, levels, side, True), along_lat(field, 1), field)
    return field


def turned_rolls(info_ref, gain_ref, *refs):
    fields, (kept_ref, sent_ref, both_ref, turned_ref, sems) = refs[:4], refs[4:]
    tile = fields[0].shape[0]
    rows = kept_ref.shape[1] // 8
    levels, side = 2, 8
    area = tile // levels
    copies = [
        pltpu.make_async_copy(field, both_ref.at[i // 2, pl.ds(i % 2 * tile, tile), :], sems.at[i])
        for i, field in enumerate(fields)
    ]
    for copy in copies:
        copy.start()
    target = lax.broadcasted_iota(jnp.int32, (tile, 2 * tile), 0)
    source = lax.broadcasted_iota(jnp.int32, (tile, 2 * tile), 1)
    upper = target < area
    row = ((target >> 3) & 7) + jnp.where(upper, info_ref[0], info_ref[2])
    col = (target & 7) + jnp.where(upper, info_ref[1], info_ref[3])
    wanted = jnp.where(col >= side, tile, 0) + jnp.where(upper, 0, area) + (row & 7) * side + (col & 7)
    onehot = jnp.where(source == wanted, 1.0, 0.0).astype(jnp.bfloat16)
    for k in (1, 0):
        copies[2 * k].wait()
        copies[2 * k + 1].wait()
        rolled = jnp.dot(onehot, both_ref[k], preferred_element_type=jnp.float32)
        if k == 0:
            center = rolled - jnp.mean(rolled, axis=-1, keepdims=True)
            spread = lax.rsqrt(jnp.mean(center * center, axis=-1, keepdims=True) + epsilon)
            rolled = center * spread * gain_ref[...]
        turned_ref[...] = rolled.astype(jnp.bfloat16).T
        for i in range(8):
            at = pl.ds(i * rows, rows)
            kept_ref[k, at, :] = turned_ref[pl.ds(pl.multiple_of(info_ref[4 + i] * rows, 16), rows), :]
            sent_ref[k, at, :] = turned_ref[pl.ds(pl.multiple_of(info_ref[12 + i] * rows, 16), rows), :]


def down(a, b):
    return lax.dot_general(a, b, (((0,), (0,)), ((), ())), preferred_element_type=jnp.float32)


def across(a, b):
    return lax.dot_general(a, b, (((1,), (1,)), ((), ())), preferred_element_type=jnp.float32)


def products_kernel(place_ref, *refs):
    tiles, pieces = refs[:4], refs[4:12]
    kept_ref, sent_ref, full_ref, tile_ref, x_ref, w_ref, sems, out_sem = refs[12:]
    tile = tiles[0].shape[2]
    part = w_ref.shape[1] // 4
    copies = []
    for i, piece in enumerate(pieces):
        rows = pl.ds(pl.multiple_of(place_ref[i] * piece.shape[0], 16), piece.shape[0])
        copies.append(pltpu.make_async_copy(piece, w_ref.at[rows, :], sems.at[i]))
    for j, source in enumerate(tiles):
        copies.append(pltpu.make_async_copy(source, tile_ref.at[j], sems.at[8 + j]))
    for copy in copies:
        copy.start()
    for j, at in enumerate((0, 2, 1, 3)):
        copies[8 + j].wait()
        for kind in range(2):
            x_ref[kind, pl.ds(at * tile, tile), :] = tile_ref[j, kind].T
    for copy in copies[:8]:
        copy.wait()
    out_copy = pltpu.make_async_copy(w_ref, full_ref, out_sem)
    out_copy.start()
    for n in range(4):
        cols = pl.ds(n * part, part)
        product = jnp.dot(x_ref[n // 3], w_ref[:, cols], preferred_element_type=jnp.float32)
        kept_ref[:, cols] = product[: 2 * tile].astype(jnp.bfloat16)
        sent_ref[:, cols] = product[2 * tile :].astype(jnp.bfloat16)
    out_copy.wait()


def attention_kernel(area, head, kept_ref, came_ref, bias_ref, grad_ref, qkv_ref, scores_ref, toward_ref, probs_ref, back_ref):
    part = grad_ref.shape[1] // 4
    levels, pairs = bias_ref.shape[:2]
    scale = 1.0 / math.sqrt(head)
    lane = lax.broadcasted_iota(jnp.int32, (area, 2 * head), 1)
    left = lane < head

    def stacked(pair):
        zero = jnp.zeros_like(pair)
        return jnp.concatenate([jnp.where(left, pair, zero), jnp.where(left, zero, pair)], axis=0)

    def unstacked(product):
        return jnp.where(left, product[:area], product[area:]).astype(jnp.bfloat16)

    windows = grad_ref.shape[0] // area
    groups = [(w * pairs + p, w, p) for w in range(windows) for p in range(pairs)]

    def view(w, p, n):
        return pl.ds(w * area, area), pl.ds(n * part + p * 2 * head, 2 * head)

    qkv_ref[...] = (kept_ref[...].astype(jnp.float32) + came_ref[...].astype(jnp.float32)).astype(jnp.bfloat16)
    for g, w, p in groups:
        scores_ref[g] = across(stacked(qkv_ref[view(w, p, 0)]), qkv_ref[view(w, p, 1)])
        toward_ref[g] = across(stacked(qkv_ref[view(w, p, 3)]), qkv_ref[view(w, p, 2)])
    for g, w, p in groups:
        scores = scores_ref[g] * scale + bias_ref[w % levels, p]
        expo = jnp.exp(scores - jnp.max(scores, axis=-1, keepdims=True))
        probs = expo / jnp.sum(expo, axis=-1, keepdims=True)
        grad_probs = toward_ref[g]
        inner = jnp.sum(probs * grad_probs, axis=-1, keepdims=True)
        probs_ref[g] = probs.astype(jnp.bfloat16)
        back_ref[g] = (probs * (grad_probs - inner) * scale).astype(jnp.bfloat16)
    for g, w, p in groups:
        probs_b, grad_scores = probs_ref[g], back_ref[g]
        grad_ref[view(w, p, 3)] = unstacked(
            jnp.dot(probs_b, qkv_ref[view(w, p, 2)], preferred_element_type=jnp.float32)
        )
        grad_ref[view(w, p, 0)] = unstacked(
            jnp.dot(grad_scores, qkv_ref[view(w, p, 1)], preferred_element_type=jnp.float32)
        )
        grad_ref[view(w, p, 2)] = down(probs_b, stacked(qkv_ref[view(w, p, 3)])).astype(jnp.bfloat16)
        grad_ref[view(w, p, 1)] = down(grad_scores, stacked(qkv_ref[view(w, p, 0)])).astype(jnp.bfloat16)


def weights_kernel(near_ref, *refs):
    tiles, (own_ref, other_ref), out_refs = refs[:4], refs[4:6], refs[6:14]
    tile_ref, sum_ref, sems = refs[14:]
    tile = tiles[0].shape[2]
    part = own_ref.shape[1] // 4
    rows = out_refs[0].shape[0]
    copies = [pltpu.make_async_copy(source, tile_ref.at[j], sems.at[j]) for j, source in enumerate(tiles)]
    for copy in copies:
        copy.start()
    for copy in copies:
        copy.wait()
    for n in range(4):
        cols = pl.ds(n * part, part)
        total = None
        for t in range(2):
            tokens = pl.ds(t * tile, tile)
            left = jnp.concatenate([tile_ref[2 * t, n // 3], tile_ref[2 * t + 1, n // 3]], axis=1)
            right = jnp.concatenate([own_ref[tokens, cols], other_ref[tokens, cols]], axis=0)
            product = jnp.dot(left, right, preferred_element_type=jnp.float32)
            total = product if total is None else total + product
        sum_ref[:, cols] = total.astype(jnp.bfloat16)
    near = near_ref[0]
    for i, out_ref in enumerate(out_refs):
        wanted = 1 - near if i % 2 == 0 else near
        out_ref[...] = sum_ref[pl.ds(pl.multiple_of((i // 2 * 2 + wanted) * rows, 16), rows), :]


def outer_kernel(place_ref, grad_ref, mine_ref, theirs_ref, own_ref, other_ref, w_ref, sems):
    tile = own_ref.shape[0]
    width = w_ref.shape[0]
    rows = width // 16
    part = w_ref.shape[1] // 4
    step = width // 4
    copies = []
    for i in range(16):
        source = (mine_ref if i < 8 else theirs_ref).at[pl.ds(i % 8 * rows, rows), :]
        into = w_ref.at[pl.ds(pl.multiple_of(place_ref[i] * rows, 16), rows), :]
        copies.append(pltpu.make_async_copy(source, into, sems.at[i]))
    for copy in copies:
        copy.start()
    for copy in copies:
        copy.wait()
    for n in range(4):
        at = pl.ds(n * step, step)
        for k, w_cols in enumerate((pl.ds(3 * part, part), pl.ds(0, 3 * part))):
            product = across(grad_ref[:, w_cols], w_ref[at, w_cols])
            cols = pl.ds(k * width + n * step, step)
            own_ref[:, cols] = product[:tile]
            other_ref[:, cols] = product[tile:].astype(jnp.bfloat16)


def after(value, earlier):
    return lax.optimization_barrier((value, earlier))[0]


def kernel_call(body, outs, in_specs, out_specs, scratch, flops, moved, name, room=58):
    return pl.pallas_call(
        body,
        out_shape=outs,
        in_specs=in_specs,
        out_specs=out_specs,
        scratch_shapes=scratch,
        compiler_params=pltpu.CompilerParams(vmem_limit_bytes=room * 1024 * 1024),
        cost_estimate=pl.CostEstimate(flops=flops, bytes_accessed=moved, transcendentals=0),
        name=name,
    )


def on_device(tokens, land, surface, gain, weights, shifts, index_table, bias_table, cotangent):
    levels, side, _, width = tokens.shape
    area = side * side
    tile = levels * area
    heads = bias_table.shape[2]
    entries = bias_table.shape[1]
    own_rows = weights.shape[0]
    part = weights.shape[1] // 8
    head = weights.shape[1] // 4 // heads
    own_heads = heads // 2
    far, near, beside, core = (lax.axis_index(axis) for axis in LON)
    grp = lax.axis_index("grp")
    first = near == 0
    f32 = jnp.float32

    def place(f, n, s, c):
        return ((far ^ f) * 4 + (near ^ n) * 2 + (beside ^ s)) * 2 + (core ^ c)

    low = jnp.concatenate([weights[:, 2 * k * part : (2 * k + 1) * part] for k in range(4)], axis=1)
    high = jnp.concatenate([weights[:, (2 * k + 1) * part : (2 * k + 2) * part] for k in range(4)], axis=1)
    mine = jnp.where(first, low, high)
    came = swap(jnp.where(first, high, low), "near")
    flat_cot = cotangent.reshape(tile, width)
    surface_term = jnp.where(land[None, :, :, None] == 1, surface[1], surface[0])
    stream = (tokens.astype(f32) + surface_term).astype(jnp.bfloat16).reshape(tile, width)
    values = stream.astype(f32)
    center = values - jnp.mean(values, axis=-1, keepdims=True)
    spread = lax.rsqrt(jnp.mean(center * center, axis=-1, keepdims=True) + epsilon)

    held = near ^ grp
    half_piece = jnp.where(grp == 0, mine, came)
    across_far = swap(half_piece, "far")
    order = [(f, s, n) for f in (1, 0) for s in (1, 0) for n in (0, 1)]
    natural = [place(f, near ^ n, s, c) for c in (0, 1) for f, s, n in order]

    vmem = pl.BlockSpec(memory_space=pltpu.VMEM)
    smem = pl.BlockSpec(memory_space=pltpu.SMEM)
    anywhere = pl.BlockSpec(memory_space=pl.ANY)
    dma = pltpu.SemaphoreType.DMA

    rows, below, below_cot = shifts[:, 0], stream, flat_cot
    if lax.axis_size("lat") > 1:
        zeros = jnp.zeros_like(rows)
        onehot_rows = pick(rows, zeros, levels, side, True)
        below = picked(onehot_rows, stream, along_lat(stream, -1))
        below_cot = picked(onehot_rows, flat_cot, along_lat(flat_cot, -1))
        rows = zeros
    moved, moved_cot = along_lon(below, -1), along_lon(below_cot, -1)
    info = jnp.concatenate(
        [jnp.stack([rows, shifts[:, 1]], axis=1).reshape(-1), jnp.stack(natural)]
    ).astype(jnp.int32)
    half = width // 2
    turned = jax.ShapeDtypeStruct((2, half, tile), jnp.bfloat16)
    own_turned, sent_turned = kernel_call(
        turned_rolls,
        (turned, turned),
        [smem, vmem] + [anywhere] * 4,
        (vmem, vmem),
        [
            pltpu.VMEM((2, 2 * tile, width), jnp.bfloat16),
            pltpu.VMEM((width, tile), jnp.bfloat16),
            dma((4,)),
        ],
        2 * 2 * 2 * tile * tile * width,
        3_000_000,
        "turned_rolls",
        24,
    )(info, gain.reshape(1, -1), below, moved, below_cot, moved_cot)
    mine_side = swap(after(mine, (moved, moved_cot)), "side")
    across_far = after(across_far, mine_side)
    far_side, far_grp = swap(across_far, "side"), swap(across_far, "grp")
    came_side = swap(after(came, far_grp), "side")
    pieces = [
        (mine, 0, 0, near),
        (came, 0, 0, 1 - near),
        (mine_side, 0, 1, near),
        (came_side, 0, 1, 1 - near),
        (across_far, 1, 0, held),
        (far_grp, 1, 0, 1 - held),
        (far_side, 1, 1, held),
        (swap(far_side, "grp"), 1, 1, 1 - held),
    ]
    places = jnp.stack([(1 - f) * 4 + (1 - s) * 2 + n for _, f, s, n in pieces]).astype(jnp.int32)
    own_near, sent_near = swap(own_turned, "near"), swap(sent_turned, "near")
    tiles = [own_turned, swap(after(sent_turned, (sent_near, far_grp)), "core"), own_near, swap(after(sent_near, far_grp), "core")]

    onehot = (index_table[:, :, None] == jnp.arange(entries, dtype=jnp.int32)).astype(f32)
    own_table = lax.dynamic_slice_in_dim(bias_table, near * own_heads, own_heads, 2)
    bias = jnp.einsum("qkr,lrh->lhqk", onehot, own_table, precision=lax.Precision.HIGHEST)
    row_number = lax.axis_index("lat") * side + jnp.arange(side, dtype=jnp.int32)
    group = row_number[None, :] >= (side * lax.axis_size("lat") - shifts[:, 0])[:, None]
    group = jnp.repeat(group, side, axis=1)
    allowed = group[:, :, None] == group[:, None, :]
    bias = jnp.where(allowed[:, None], bias, -1e30).reshape(levels, own_heads // 2, 2 * area, area)

    bf16 = jnp.bfloat16
    kept, sent, w_mine = kernel_call(
        products_kernel,
        (
            jax.ShapeDtypeStruct((2 * tile, 4 * part), bf16),
            jax.ShapeDtypeStruct((2 * tile, 4 * part), bf16),
            jax.ShapeDtypeStruct((half, 4 * part), bf16),
        ),
        [smem] + [anywhere] * 12,
        (vmem, vmem, anywhere),
        [
            pltpu.VMEM((4, 2, half, tile), bf16),
            pltpu.VMEM((2, 4 * tile, half), bf16),
            pltpu.VMEM((half, 4 * part), bf16),
            dma((12,)),
            dma,
        ],
        1_200_000_000,
        9_000_000,
        "products",
    )(after(places, bias), *tiles, *[piece for piece, *_ in pieces])
    crossed = swap(sent, "core")
    grad = kernel_call(
        functools.partial(attention_kernel, area, head),
        jax.ShapeDtypeStruct((2 * tile, 4 * part), bf16),
        [vmem] * 3,
        vmem,
        [pltpu.VMEM((2 * tile, 4 * part), bf16)]
        + [pltpu.VMEM((2 * tile // area * own_heads // 2, 2 * area, area), kind) for kind in (f32, f32, bf16, bf16)],
        1_000_000_000,
        4_000_000,
        "attention",
    )(kept, crossed, bias)
    w_theirs = swap(after(w_mine, crossed), "core")
    grad_theirs = swap(grad, "core")
    attended_own, attended_other = kernel_call(
        outer_kernel,
        (
            jax.ShapeDtypeStruct((tile, 2 * width), f32),
            jax.ShapeDtypeStruct((tile, 2 * width), bf16),
        ),
        [smem, vmem, anywhere, anywhere],
        (vmem, vmem),
        [pltpu.VMEM((width, 4 * part), bf16), dma((16,))],
        1_200_000_000,
        8_000_000,
        "projections",
        24,
    )(jnp.stack(natural).astype(jnp.int32), grad, w_mine, w_theirs)
    blocks = kernel_call(
        weights_kernel,
        [jax.ShapeDtypeStruct((own_rows, 4 * part), bf16)] * 8,
        [smem] + [anywhere] * 4 + [vmem] * 2,
        [vmem] * 8,
        [
            pltpu.VMEM((4, 2, half, tile), bf16),
            pltpu.VMEM((half, 4 * part), bf16),
            dma((4,)),
        ],
        1_200_000_000,
        6_000_000,
        "weight_gradient",
        24,
    )(after(near.astype(jnp.int32).reshape(1), attended_other), *tiles, grad, grad_theirs)

    def block(f, s, n):
        return blocks[((1 - f) * 2 + 1 - s) * 2 + 1 - n]

    side_far_1 = swap(block(1, 1, 1), "side")
    arrived_back = swap(attended_other, "near")
    side_far_0 = swap(after(block(1, 1, 0), side_far_1), "side")
    far_1 = swap((block(1, 0, 1).astype(f32) + side_far_1.astype(f32)).astype(bf16), "far")
    far_0 = swap(after((block(1, 0, 0).astype(f32) + side_far_0.astype(f32)).astype(bf16), (far_1, arrived_back)), "far")
    side_1 = swap(after(block(0, 1, 1), side_far_0), "side")
    side_0 = swap(after(block(0, 1, 0), side_1), "side")
    total_1 = (block(0, 0, 1).astype(f32) + side_1.astype(f32) + far_1.astype(f32)).astype(bf16)
    theirs = swap(total_1, "near").astype(f32)

    back = (attended_own + arrived_back.astype(f32)).astype(jnp.bfloat16)
    back = after(roll_back(back, shifts, levels, side, far_1), far_0)
    output = (values + back[:, :width].astype(f32)).astype(jnp.bfloat16)
    scaled = center * spread
    upstream = back[:, width:].astype(f32) * gain
    grad_stream = spread * (
        upstream
        - jnp.mean(upstream, axis=-1, keepdims=True)
        - scaled * jnp.mean(upstream * scaled, axis=-1, keepdims=True)
    )
    grad_tokens = (flat_cot.astype(f32) + grad_stream).astype(jnp.bfloat16)

    far_0 = after(far_0, (output, grad_tokens))
    total_0 = block(0, 0, 0).astype(f32) + side_0.astype(f32) + far_0.astype(f32)
    token_count = tile * lax.axis_size("lat") * math.prod(lax.axis_size(axis) for axis in LON)
    columns = []
    for k in range(4):
        cols = slice(k * part, (k + 1) * part)
        columns += [
            jnp.where(first, total_0[:, cols], theirs[:, cols]),
            jnp.where(first, theirs[:, cols], total_0[:, cols]),
        ]
    summed = jnp.concatenate(columns, axis=1)
    if lax.axis_size("lat") > 1:
        summed = lax.psum(summed.astype(jnp.bfloat16), "lat").astype(f32)
    grad_weights = summed * (1.0 / math.sqrt(token_count))
    return (output.reshape(tokens.shape), grad_tokens.reshape(tokens.shape), grad_weights)


def solution(mesh):
    sizes = dict(mesh.shape)
    devices = mesh.devices.reshape(sizes["grp"], sizes["lon"] // 8, 2, 2, 2, sizes["lat"])
    finer = Mesh(devices, ("grp",) + LON + ("lat",))
    return jax.shard_map(
        on_device,
        mesh=finer,
        in_specs=(
            P("grp", "lat", LON, None),
            P(("grp", "lat"), LON),
            P(),
            P(),
            P(LON, None),
            P(),
            P(),
            P("lat", None, None),
            P("grp", "lat", LON, None),
        ),
        out_specs=(
            P("grp", "lat", LON, None),
            P("grp", "lat", LON, None),
            P(("grp",) + LON, None),
        ),
        check_vma=False,
    )
```

```python
import functools
import math

import jax
import jax.numpy as jnp
from jax import lax
from jax.experimental import pallas as pl
from jax.experimental.pallas import tpu as pltpu
from jax.sharding import Mesh
from jax.sharding import PartitionSpec as P

epsilon = 1e-05
LON = ("far", "near", "side", "core")


def along_lon(shard, by):
    count = math.prod(lax.axis_size(axis) for axis in LON)
    return lax.ppermute(shard, LON, [(i, (i + by) % count) for i in range(count)])


def along_lat(shard, by):
    count = lax.axis_size("lat")
    return lax.ppermute(shard, "lat", [(i, (i + by) % count) for i in range(count)])


def swap(shard, axis):
    return lax.ppermute(shard, axis, [(0, 1), (1, 0)])


def pick(rows, cols, levels, side, over_rows):
    tile = levels * side * side
    shape = (tile, 2 * tile)
    target = lax.broadcasted_iota(jnp.int32, shape, 0)
    source = lax.broadcasted_iota(jnp.int32, shape, 1)
    level = target // (side * side)
    row = target // side % side
    col = target % side
    from_row = jnp.full_like(row, rows[levels - 1])
    from_col = jnp.full_like(col, cols[levels - 1])
    for l in range(levels - 1):
        from_row = jnp.where(level == l, rows[l], from_row)
        from_col = jnp.where(level == l, cols[l], from_col)
    from_row = row + from_row
    from_col = col + from_col
    which = (from_row if over_rows else from_col) // side
    wanted = which * tile + level * side * side + from_row % side * side + from_col % side
    return (source == wanted).astype(jnp.bfloat16)


def picked(onehot, first, second):
    both = jnp.concatenate([first, second], axis=0)
    return jnp.dot(onehot, both, preferred_element_type=jnp.float32).astype(jnp.bfloat16)


def roll_back(field, shifts, levels, side, wait):
    zeros = jnp.zeros_like(shifts[:, 0])
    rows = side - shifts[:, 0]
    more = lax.axis_size("lat") > 1
    field = picked(
        pick(zeros if more else rows, side - shifts[:, 1], levels, side, False),
        after(along_lon(field, 1), wait),
        field,
    )
    if more:
        field = picked(pick(rows, zeros, levels, side, True), along_lat(field, 1), field)
    return field


def turned_rolls(info_ref, gain_ref, *refs):
    fields, (kept_ref, sent_ref, both_ref, turned_ref, sems) = refs[:4], refs[4:]
    tile = fields[0].shape[0]
    rows = kept_ref.shape[1] // 8
    levels, side = 2, 8
    area = tile // levels
    copies = [
        pltpu.make_async_copy(field, both_ref.at[i // 2, pl.ds(i % 2 * tile, tile), :], sems.at[i])
        for i, field in enumerate(fields)
    ]
    for copy in copies:
        copy.start()
    target = lax.broadcasted_iota(jnp.int32, (tile, 2 * tile), 0)
    source = lax.broadcasted_iota(jnp.int32, (tile, 2 * tile), 1)
    upper = target < area
    row = ((target >> 3) & 7) + jnp.where(upper, info_ref[0], info_ref[2])
    col = (target & 7) + jnp.where(upper, info_ref[1], info_ref[3])
    wanted = jnp.where(col >= side, tile, 0) + jnp.where(upper, 0, area) + (row & 7) * side + (col & 7)
    onehot = jnp.where(source == wanted, 1.0, 0.0).astype(jnp.bfloat16)
    for k in (1, 0):
        copies[2 * k].wait()
        copies[2 * k + 1].wait()
        rolled = jnp.dot(onehot, both_ref[k], preferred_element_type=jnp.float32)
        if k == 0:
            center = rolled - jnp.mean(rolled, axis=-1, keepdims=True)
            spread = lax.rsqrt(jnp.mean(center * center, axis=-1, keepdims=True) + epsilon)
            rolled = center * spread * gain_ref[...]
        turned_ref[...] = rolled.astype(jnp.bfloat16).T
        for i in range(8):
            at = pl.ds(i * rows, rows)
            kept_ref[k, at, :] = turned_ref[pl.ds(pl.multiple_of(info_ref[4 + i] * rows, 16), rows), :]
            sent_ref[k, at, :] = turned_ref[pl.ds(pl.multiple_of(info_ref[12 + i] * rows, 16), rows), :]


def down(a, b):
    return lax.dot_general(a, b, (((0,), (0,)), ((), ())), preferred_element_type=jnp.float32)


def across(a, b):
    return lax.dot_general(a, b, (((1,), (1,)), ((), ())), preferred_element_type=jnp.float32)


def products_kernel(place_ref, *refs):
    tiles, pieces = refs[:4], refs[4:12]
    kept_ref, sent_ref, full_ref, tile_ref, x_ref, w_ref, sems, out_sem = refs[12:]
    tile = tiles[0].shape[2]
    part = w_ref.shape[1] // 4
    copies = []
    for i, piece in enumerate(pieces):
        rows = pl.ds(pl.multiple_of(place_ref[i] * piece.shape[0], 16), piece.shape[0])
        copies.append(pltpu.make_async_copy(piece, w_ref.at[rows, :], sems.at[i]))
    for j, source in enumerate(tiles):
        copies.append(pltpu.make_async_copy(source, tile_ref.at[j], sems.at[8 + j]))
    for copy in copies[8:] + copies[:8]:
        copy.start()
    for j, at in enumerate((0, 2, 1, 3)):
        copies[8 + j].wait()
        for kind in range(2):
            x_ref[kind, pl.ds(at * tile, tile), :] = tile_ref[j, kind].T
    for copy in copies[:8]:
        copy.wait()
    out_copy = pltpu.make_async_copy(w_ref, full_ref, out_sem)
    out_copy.start()
    for n in range(4):
        cols = pl.ds(n * part, part)
        product = jnp.dot(x_ref[n // 3], w_ref[:, cols], preferred_element_type=jnp.float32)
        kept_ref[:, cols] = product[: 2 * tile].astype(jnp.bfloat16)
        sent_ref[:, cols] = product[2 * tile :].astype(jnp.bfloat16)
    out_copy.wait()


def attention_kernel(area, head, kept_ref, came_ref, bias_ref, grad_ref, qkv_ref, scores_ref, toward_ref, probs_ref, back_ref):
    part = grad_ref.shape[1] // 4
    levels, pairs = bias_ref.shape[:2]
    scale = 1.0 / math.sqrt(head)
    lane = lax.broadcasted_iota(jnp.int32, (area, 2 * head), 1)
    left = lane < head

    def stacked(pair):
        zero = jnp.zeros_like(pair)
        return jnp.concatenate([jnp.where(left, pair, zero), jnp.where(left, zero, pair)], axis=0)

    def unstacked(product):
        return jnp.where(left, product[:area], product[area:]).astype(jnp.bfloat16)

    windows = grad_ref.shape[0] // area
    groups = [(w * pairs + p, w, p) for w in range(windows) for p in range(pairs)]

    def view(w, p, n):
        return pl.ds(w * area, area), pl.ds(n * part + p * 2 * head, 2 * head)

    qkv_ref[...] = (kept_ref[...].astype(jnp.float32) + came_ref[...].astype(jnp.float32)).astype(jnp.bfloat16)
    for g, w, p in groups:
        scores_ref[g] = across(stacked(qkv_ref[view(w, p, 0)]), qkv_ref[view(w, p, 1)])
        toward_ref[g] = across(stacked(qkv_ref[view(w, p, 3)]), qkv_ref[view(w, p, 2)])
    for g, w, p in groups:
        scores = scores_ref[g] * scale + bias_ref[w % levels, p]
        expo = jnp.exp(scores - jnp.max(scores, axis=-1, keepdims=True))
        probs = expo / jnp.sum(expo, axis=-1, keepdims=True)
        grad_probs = toward_ref[g]
        inner = jnp.sum(probs * grad_probs, axis=-1, keepdims=True)
        probs_ref[g] = probs.astype(jnp.bfloat16)
        back_ref[g] = (probs * (grad_probs - inner) * scale).astype(jnp.bfloat16)
    for g, w, p in groups:
        probs_b, grad_scores = probs_ref[g], back_ref[g]
        grad_ref[view(w, p, 3)] = unstacked(
            jnp.dot(probs_b, qkv_ref[view(w, p, 2)], preferred_element_type=jnp.float32)
        )
        grad_ref[view(w, p, 0)] = unstacked(
            jnp.dot(grad_scores, qkv_ref[view(w, p, 1)], preferred_element_type=jnp.float32)
        )
        grad_ref[view(w, p, 2)] = down(probs_b, stacked(qkv_ref[view(w, p, 3)])).astype(jnp.bfloat16)
        grad_ref[view(w, p, 1)] = down(grad_scores, stacked(qkv_ref[view(w, p, 0)])).astype(jnp.bfloat16)


def weights_kernel(near_ref, *refs):
    tiles, (own_ref, other_ref), out_refs = refs[:4], refs[4:6], refs[6:14]
    tile_ref, sum_ref, sems = refs[14:]
    tile = tiles[0].shape[2]
    part = own_ref.shape[1] // 4
    rows = out_refs[0].shape[0]
    copies = [pltpu.make_async_copy(source, tile_ref.at[j], sems.at[j]) for j, source in enumerate(tiles)]
    for copy in copies:
        copy.start()
    for copy in copies:
        copy.wait()
    for n in range(4):
        cols = pl.ds(n * part, part)
        total = None
        for t in range(2):
            tokens = pl.ds(t * tile, tile)
            left = jnp.concatenate([tile_ref[2 * t, n // 3], tile_ref[2 * t + 1, n // 3]], axis=1)
            right = jnp.concatenate([own_ref[tokens, cols], other_ref[tokens, cols]], axis=0)
            product = jnp.dot(left, right, preferred_element_type=jnp.float32)
            total = product if total is None else total + product
        sum_ref[:, cols] = total.astype(jnp.bfloat16)
    near = near_ref[0]
    for i, out_ref in enumerate(out_refs):
        wanted = 1 - near if i % 2 == 0 else near
        out_ref[...] = sum_ref[pl.ds(pl.multiple_of((i // 2 * 2 + wanted) * rows, 16), rows), :]


def outer_kernel(place_ref, grad_ref, mine_ref, theirs_ref, own_ref, other_ref, w_ref, sems):
    tile = own_ref.shape[0]
    width = w_ref.shape[0]
    rows = width // 16
    part = w_ref.shape[1] // 4
    step = width // 4
    copies = []
    for i in range(16):
        source = (mine_ref if i < 8 else theirs_ref).at[pl.ds(i % 8 * rows, rows), :]
        into = w_ref.at[pl.ds(pl.multiple_of(place_ref[i] * rows, 16), rows), :]
        copies.append(pltpu.make_async_copy(source, into, sems.at[i]))
    for copy in copies:
        copy.start()
    for copy in copies:
        copy.wait()
    for n in range(4):
        at = pl.ds(n * step, step)
        for k, w_cols in enumerate((pl.ds(3 * part, part), pl.ds(0, 3 * part))):
            product = across(grad_ref[:, w_cols], w_ref[at, w_cols])
            cols = pl.ds(k * width + n * step, step)
            own_ref[:, cols] = product[:tile]
            other_ref[:, cols] = product[tile:].astype(jnp.bfloat16)


def after(value, earlier):
    return lax.optimization_barrier((value, earlier))[0]


def kernel_call(body, outs, in_specs, out_specs, scratch, flops, moved, name, room=58):
    return pl.pallas_call(
        body,
        out_shape=outs,
        in_specs=in_specs,
        out_specs=out_specs,
        scratch_shapes=scratch,
        compiler_params=pltpu.CompilerParams(vmem_limit_bytes=room * 1024 * 1024),
        cost_estimate=pl.CostEstimate(flops=flops, bytes_accessed=moved, transcendentals=0),
        name=name,
    )


def on_device(tokens, land, surface, gain, weights, shifts, index_table, bias_table, cotangent):
    levels, side, _, width = tokens.shape
    area = side * side
    tile = levels * area
    heads = bias_table.shape[2]
    entries = bias_table.shape[1]
    own_rows = weights.shape[0]
    part = weights.shape[1] // 8
    head = weights.shape[1] // 4 // heads
    own_heads = heads // 2
    far, near, beside, core = (lax.axis_index(axis) for axis in LON)
    grp = lax.axis_index("grp")
    first = near == 0
    f32 = jnp.float32

    def place(f, n, s, c):
        return ((far ^ f) * 4 + (near ^ n) * 2 + (beside ^ s)) * 2 + (core ^ c)

    low = jnp.concatenate([weights[:, 2 * k * part : (2 * k + 1) * part] for k in range(4)], axis=1)
    high = jnp.concatenate([weights[:, (2 * k + 1) * part : (2 * k + 2) * part] for k in range(4)], axis=1)
    mine = jnp.where(first, low, high)
    came = swap(jnp.where(first, high, low), "near")
    flat_cot = cotangent.reshape(tile, width)
    surface_term = jnp.where(land[None, :, :, None] == 1, surface[1], surface[0])
    stream = (tokens.astype(f32) + surface_term).astype(jnp.bfloat16).reshape(tile, width)
    values = stream.astype(f32)
    center = values - jnp.mean(values, axis=-1, keepdims=True)
    spread = lax.rsqrt(jnp.mean(center * center, axis=-1, keepdims=True) + epsilon)

    held = near ^ grp
    half_piece = jnp.where(grp == 0, mine, came)
    across_far = swap(half_piece, "far")
    order = [(f, s, n) for f in (1, 0) for s in (1, 0) for n in (0, 1)]
    natural = [place(f, near ^ n, s, c) for c in (0, 1) for f, s, n in order]

    vmem = pl.BlockSpec(memory_space=pltpu.VMEM)
    smem = pl.BlockSpec(memory_space=pltpu.SMEM)
    anywhere = pl.BlockSpec(memory_space=pl.ANY)
    dma = pltpu.SemaphoreType.DMA

    rows, below, below_cot = shifts[:, 0], stream, flat_cot
    if lax.axis_size("lat") > 1:
        zeros = jnp.zeros_like(rows)
        onehot_rows = pick(rows, zeros, levels, side, True)
        below = picked(onehot_rows, stream, along_lat(stream, -1))
        below_cot = picked(onehot_rows, flat_cot, along_lat(flat_cot, -1))
        rows = zeros
    moved, moved_cot = along_lon(below, -1), along_lon(below_cot, -1)
    info = jnp.concatenate(
        [jnp.stack([rows, shifts[:, 1]], axis=1).reshape(-1), jnp.stack(natural)]
    ).astype(jnp.int32)
    half = width // 2
    turned = jax.ShapeDtypeStruct((2, half, tile), jnp.bfloat16)
    own_turned, sent_turned = kernel_call(
        turned_rolls,
        (turned, turned),
        [smem, vmem] + [anywhere] * 4,
        (vmem, vmem),
        [
            pltpu.VMEM((2, 2 * tile, width), jnp.bfloat16),
            pltpu.VMEM((width, tile), jnp.bfloat16),
            dma((4,)),
        ],
        2 * 2 * 2 * tile * tile * width,
        3_000_000,
        "turned_rolls",
        24,
    )(info, gain.reshape(1, -1), below, moved, below_cot, moved_cot)
    mine_side = swap(after(mine, (moved, moved_cot)), "side")
    across_far = after(across_far, mine_side)
    far_side, far_grp = swap(across_far, "side"), swap(across_far, "grp")
    came_side = swap(after(came, far_grp), "side")
    pieces = [
        (mine, 0, 0, near),
        (came, 0, 0, 1 - near),
        (mine_side, 0, 1, near),
        (came_side, 0, 1, 1 - near),
        (across_far, 1, 0, held),
        (far_grp, 1, 0, 1 - held),
        (far_side, 1, 1, held),
        (swap(far_side, "grp"), 1, 1, 1 - held),
    ]
    places = jnp.stack([(1 - f) * 4 + (1 - s) * 2 + n for _, f, s, n in pieces]).astype(jnp.int32)
    own_near, sent_near = swap(own_turned, "near"), swap(sent_turned, "near")
    tiles = [own_turned, swap(after(sent_turned, (sent_near, far_grp)), "core"), own_near, swap(after(sent_near, far_grp), "core")]

    onehot = (index_table[:, :, None] == jnp.arange(entries, dtype=jnp.int32)).astype(f32)
    own_table = lax.dynamic_slice_in_dim(bias_table, near * own_heads, own_heads, 2)
    bias = jnp.einsum("qkr,lrh->lhqk", onehot, own_table, precision=lax.Precision.HIGHEST)
    row_number = lax.axis_index("lat") * side + jnp.arange(side, dtype=jnp.int32)
    group = row_number[None, :] >= (side * lax.axis_size("lat") - shifts[:, 0])[:, None]
    group = jnp.repeat(group, side, axis=1)
    allowed = group[:, :, None] == group[:, None, :]
    bias = jnp.where(allowed[:, None], bias, -1e30).reshape(levels, own_heads // 2, 2 * area, area)

    bf16 = jnp.bfloat16
    kept, sent, w_mine = kernel_call(
        products_kernel,
        (
            jax.ShapeDtypeStruct((2 * tile, 4 * part), bf16),
            jax.ShapeDtypeStruct((2 * tile, 4 * part), bf16),
            jax.ShapeDtypeStruct((half, 4 * part), bf16),
        ),
        [smem] + [anywhere] * 12,
        (vmem, vmem, anywhere),
        [
            pltpu.VMEM((4, 2, half, tile), bf16),
            pltpu.VMEM((2, 4 * tile, half), bf16),
            pltpu.VMEM((half, 4 * part), bf16),
            dma((12,)),
            dma,
        ],
        1_200_000_000,
        9_000_000,
        "products",
    )(after(places, bias), *tiles, *[piece for piece, *_ in pieces])
    crossed = swap(sent, "core")
    grad = kernel_call(
        functools.partial(attention_kernel, area, head),
        jax.ShapeDtypeStruct((2 * tile, 4 * part), bf16),
        [vmem] * 3,
        vmem,
        [pltpu.VMEM((2 * tile, 4 * part), bf16)]
        + [pltpu.VMEM((2 * tile // area * own_heads // 2, 2 * area, area), kind) for kind in (f32, f32, bf16, bf16)],
        1_000_000_000,
        4_000_000,
        "attention",
    )(kept, crossed, bias)
    w_theirs = swap(after(w_mine, crossed), "core")
    grad_theirs = swap(grad, "core")
    blocks = kernel_call(
        weights_kernel,
        [jax.ShapeDtypeStruct((own_rows, 4 * part), bf16)] * 8,
        [smem] + [anywhere] * 4 + [vmem] * 2,
        [vmem] * 8,
        [
            pltpu.VMEM((4, 2, half, tile), bf16),
            pltpu.VMEM((half, 4 * part), bf16),
            dma((4,)),
        ],
        1_200_000_000,
        6_000_000,
        "weight_gradient",
        24,
    )(near.astype(jnp.int32).reshape(1), *tiles, grad, grad_theirs)

    def block(f, s, n):
        return blocks[((1 - f) * 2 + 1 - s) * 2 + 1 - n]

    attended_own, attended_other = kernel_call(
        outer_kernel,
        (
            jax.ShapeDtypeStruct((tile, 2 * width), f32),
            jax.ShapeDtypeStruct((tile, 2 * width), bf16),
        ),
        [smem, vmem, anywhere, anywhere],
        (vmem, vmem),
        [pltpu.VMEM((width, 4 * part), bf16), dma((16,))],
        1_200_000_000,
        8_000_000,
        "projections",
        24,
    )(after(jnp.stack(natural).astype(jnp.int32), blocks[0]), grad, w_mine, w_theirs)
    side_far_1 = after(swap(block(1, 1, 1), "side"), attended_other)
    arrived_back = swap(attended_other, "near")
    side_far_0 = swap(after(block(1, 1, 0), side_far_1), "side")
    far_1 = swap((block(1, 0, 1).astype(f32) + side_far_1.astype(f32)).astype(bf16), "far")
    far_0 = swap(after((block(1, 0, 0).astype(f32) + side_far_0.astype(f32)).astype(bf16), (far_1, arrived_back)), "far")
    side_1 = swap(after(block(0, 1, 1), side_far_0), "side")
    side_0 = swap(after(block(0, 1, 0), side_1), "side")
    total_1 = (block(0, 0, 1).astype(f32) + side_1.astype(f32) + far_1.astype(f32)).astype(bf16)
    theirs = swap(total_1, "near").astype(f32)

    back = (attended_own + arrived_back.astype(f32)).astype(jnp.bfloat16)
    back = after(roll_back(back, shifts, levels, side, far_1), far_0)
    output = (values + back[:, :width].astype(f32)).astype(jnp.bfloat16)
    scaled = center * spread
    upstream = back[:, width:].astype(f32) * gain
    grad_stream = spread * (
        upstream
        - jnp.mean(upstream, axis=-1, keepdims=True)
        - scaled * jnp.mean(upstream * scaled, axis=-1, keepdims=True)
    )
    grad_tokens = (flat_cot.astype(f32) + grad_stream).astype(jnp.bfloat16)

    far_0 = after(far_0, (output, grad_tokens))
    total_0 = block(0, 0, 0).astype(f32) + side_0.astype(f32) + far_0.astype(f32)
    token_count = tile * lax.axis_size("lat") * math.prod(lax.axis_size(axis) for axis in LON)
    columns = []
    for k in range(4):
        cols = slice(k * part, (k + 1) * part)
        columns += [
            jnp.where(first, total_0[:, cols], theirs[:, cols]),
            jnp.where(first, theirs[:, cols], total_0[:, cols]),
        ]
    summed = jnp.concatenate(columns, axis=1)
    if lax.axis_size("lat") > 1:
        summed = lax.psum(summed.astype(jnp.bfloat16), "lat").astype(f32)
    grad_weights = summed * (1.0 / math.sqrt(token_count))
    return (output.reshape(tokens.shape), grad_tokens.reshape(tokens.shape), grad_weights)


def solution(mesh):
    sizes = dict(mesh.shape)
    devices = mesh.devices.reshape(sizes["grp"], sizes["lon"] // 8, 2, 2, 2, sizes["lat"])
    finer = Mesh(devices, ("grp",) + LON + ("lat",))
    return jax.shard_map(
        on_device,
        mesh=finer,
        in_specs=(
            P("grp", "lat", LON, None),
            P(("grp", "lat"), LON),
            P(),
            P(),
            P(LON, None),
            P(),
            P(),
            P("lat", None, None),
            P("grp", "lat", LON, None),
        ),
        out_specs=(
            P("grp", "lat", LON, None),
            P("grp", "lat", LON, None),
            P(("grp",) + LON, None),
        ),
        check_vma=False,
    )
```

```python
import functools
import math

import jax
import jax.numpy as jnp
from jax import lax
from jax.experimental import pallas as pl
from jax.experimental.pallas import tpu as pltpu
from jax.sharding import Mesh
from jax.sharding import PartitionSpec as P

epsilon = 1e-05
LON = ("far", "near", "side", "core")


def along_lon(shard, by):
    count = math.prod(lax.axis_size(axis) for axis in LON)
    return lax.ppermute(shard, LON, [(i, (i + by) % count) for i in range(count)])


def along_lat(shard, by):
    count = lax.axis_size("lat")
    return lax.ppermute(shard, "lat", [(i, (i + by) % count) for i in range(count)])


def swap(shard, axis):
    return lax.ppermute(shard, axis, [(0, 1), (1, 0)])


def pick(rows, cols, levels, side, over_rows):
    tile = levels * side * side
    shape = (tile, 2 * tile)
    target = lax.broadcasted_iota(jnp.int32, shape, 0)
    source = lax.broadcasted_iota(jnp.int32, shape, 1)
    level = target // (side * side)
    row = target // side % side
    col = target % side
    from_row = jnp.full_like(row, rows[levels - 1])
    from_col = jnp.full_like(col, cols[levels - 1])
    for l in range(levels - 1):
        from_row = jnp.where(level == l, rows[l], from_row)
        from_col = jnp.where(level == l, cols[l], from_col)
    from_row = row + from_row
    from_col = col + from_col
    which = (from_row if over_rows else from_col) // side
    wanted = which * tile + level * side * side + from_row % side * side + from_col % side
    return (source == wanted).astype(jnp.bfloat16)


def picked(onehot, first, second):
    both = jnp.concatenate([first, second], axis=0)
    return jnp.dot(onehot, both, preferred_element_type=jnp.float32).astype(jnp.bfloat16)


def roll_back(field, shifts, levels, side, wait):
    zeros = jnp.zeros_like(shifts[:, 0])
    rows = side - shifts[:, 0]
    more = lax.axis_size("lat") > 1
    field = picked(
        pick(zeros if more else rows, side - shifts[:, 1], levels, side, False),
        after(along_lon(field, 1), wait),
        field,
    )
    if more:
        field = picked(pick(rows, zeros, levels, side, True), along_lat(field, 1), field)
    return field


def turned_rolls(info_ref, gain_ref, *refs):
    fields, (kept_ref, sent_ref, both_ref, turned_ref, sems) = refs[:4], refs[4:]
    tile = fields[0].shape[0]
    rows = kept_ref.shape[1] // 8
    levels, side = 2, 8
    area = tile // levels
    copies = [
        pltpu.make_async_copy(field, both_ref.at[i // 2, pl.ds(i % 2 * tile, tile), :], sems.at[i])
        for i, field in enumerate(fields)
    ]
    for copy in copies:
        copy.start()
    target = lax.broadcasted_iota(jnp.int32, (tile, 2 * tile), 0)
    source = lax.broadcasted_iota(jnp.int32, (tile, 2 * tile), 1)
    upper = target < area
    row = ((target >> 3) & 7) + jnp.where(upper, info_ref[0], info_ref[2])
    col = (target & 7) + jnp.where(upper, info_ref[1], info_ref[3])
    wanted = jnp.where(col >= side, tile, 0) + jnp.where(upper, 0, area) + (row & 7) * side + (col & 7)
    onehot = jnp.where(source == wanted, 1.0, 0.0).astype(jnp.bfloat16)
    for k in (1, 0):
        copies[2 * k].wait()
        copies[2 * k + 1].wait()
        rolled = jnp.dot(onehot, both_ref[k], preferred_element_type=jnp.float32)
        if k == 0:
            center = rolled - jnp.mean(rolled, axis=-1, keepdims=True)
            spread = lax.rsqrt(jnp.mean(center * center, axis=-1, keepdims=True) + epsilon)
            rolled = center * spread * gain_ref[...]
        turned_ref[...] = rolled.astype(jnp.bfloat16).T
        for i in range(8):
            at = pl.ds(i * rows, rows)
            kept_ref[k, at, :] = turned_ref[pl.ds(pl.multiple_of(info_ref[4 + i] * rows, 16), rows), :]
            sent_ref[k, at, :] = turned_ref[pl.ds(pl.multiple_of(info_ref[12 + i] * rows, 16), rows), :]


def down(a, b):
    return lax.dot_general(a, b, (((0,), (0,)), ((), ())), preferred_element_type=jnp.float32)


def across(a, b):
    return lax.dot_general(a, b, (((1,), (1,)), ((), ())), preferred_element_type=jnp.float32)


def products_kernel(place_ref, *refs):
    tiles, pieces = refs[:4], refs[4:12]
    kept_ref, sent_ref, full_ref, tile_ref, x_ref, w_ref, sems, out_sem = refs[12:]
    tile = tiles[0].shape[2]
    part = w_ref.shape[1] // 4
    copies = []
    for i, piece in enumerate(pieces):
        rows = pl.ds(pl.multiple_of(place_ref[i] * piece.shape[0], 16), piece.shape[0])
        copies.append(pltpu.make_async_copy(piece, w_ref.at[rows, :], sems.at[i]))
    for j, source in enumerate(tiles):
        copies.append(pltpu.make_async_copy(source, tile_ref.at[j], sems.at[8 + j]))
    for copy in copies[8:] + copies[:8]:
        copy.start()
    for j, at in enumerate((0, 2, 1, 3)):
        copies[8 + j].wait()
        for kind in range(2):
            x_ref[kind, pl.ds(at * tile, tile), :] = tile_ref[j, kind].T
    for copy in copies[:8]:
        copy.wait()
    out_copy = pltpu.make_async_copy(w_ref, full_ref, out_sem)
    out_copy.start()
    for n in range(4):
        cols = pl.ds(n * part, part)
        product = jnp.dot(x_ref[n // 3], w_ref[:, cols], preferred_element_type=jnp.float32)
        kept_ref[:, cols] = product[: 2 * tile].astype(jnp.bfloat16)
        sent_ref[:, cols] = product[2 * tile :].astype(jnp.bfloat16)
    out_copy.wait()


def attention_kernel(area, head, kept_ref, came_ref, bias_ref, grad_ref, qkv_ref, scores_ref, toward_ref, probs_ref, back_ref):
    part = grad_ref.shape[1] // 4
    levels, pairs = bias_ref.shape[:2]
    scale = 1.0 / math.sqrt(head)
    lane = lax.broadcasted_iota(jnp.int32, (area, 2 * head), 1)
    left = lane < head

    def stacked(pair):
        zero = jnp.zeros_like(pair)
        return jnp.concatenate([jnp.where(left, pair, zero), jnp.where(left, zero, pair)], axis=0)

    def unstacked(product):
        return jnp.where(left, product[:area], product[area:]).astype(jnp.bfloat16)

    windows = grad_ref.shape[0] // area
    groups = [(w * pairs + p, w, p) for w in range(windows) for p in range(pairs)]

    def view(w, p, n):
        return pl.ds(w * area, area), pl.ds(n * part + p * 2 * head, 2 * head)

    qkv_ref[...] = (kept_ref[...].astype(jnp.float32) + came_ref[...].astype(jnp.float32)).astype(jnp.bfloat16)
    for g, w, p in groups:
        scores_ref[g] = across(stacked(qkv_ref[view(w, p, 0)]), qkv_ref[view(w, p, 1)])
        toward_ref[g] = across(stacked(qkv_ref[view(w, p, 3)]), qkv_ref[view(w, p, 2)])
    for g, w, p in groups:
        scores = scores_ref[g] * scale + bias_ref[w % levels, p]
        expo = jnp.exp(scores - jnp.max(scores, axis=-1, keepdims=True))
        probs = expo / jnp.sum(expo, axis=-1, keepdims=True)
        grad_probs = toward_ref[g]
        inner = jnp.sum(probs * grad_probs, axis=-1, keepdims=True)
        probs_ref[g] = probs.astype(jnp.bfloat16)
        back_ref[g] = (probs * (grad_probs - inner) * scale).astype(jnp.bfloat16)
    for g, w, p in groups:
        probs_b, grad_scores = probs_ref[g], back_ref[g]
        grad_ref[view(w, p, 3)] = unstacked(
            jnp.dot(probs_b, qkv_ref[view(w, p, 2)], preferred_element_type=jnp.float32)
        )
        grad_ref[view(w, p, 0)] = unstacked(
            jnp.dot(grad_scores, qkv_ref[view(w, p, 1)], preferred_element_type=jnp.float32)
        )
        grad_ref[view(w, p, 2)] = down(probs_b, stacked(qkv_ref[view(w, p, 3)])).astype(jnp.bfloat16)
        grad_ref[view(w, p, 1)] = down(grad_scores, stacked(qkv_ref[view(w, p, 0)])).astype(jnp.bfloat16)


def weights_kernel(near_ref, *refs):
    tiles, (own_ref, other_ref), out_refs = refs[:4], refs[4:6], refs[6:14]
    tile_ref, sum_ref, sems = refs[14:]
    tile = tiles[0].shape[2]
    part = own_ref.shape[1] // 4
    rows = out_refs[0].shape[0]
    copies = [pltpu.make_async_copy(source, tile_ref.at[j], sems.at[j]) for j, source in enumerate(tiles)]
    for copy in copies:
        copy.start()
    for copy in copies:
        copy.wait()
    for n in range(4):
        cols = pl.ds(n * part, part)
        total = None
        for t in range(2):
            tokens = pl.ds(t * tile, tile)
            left = jnp.concatenate([tile_ref[2 * t, n // 3], tile_ref[2 * t + 1, n // 3]], axis=1)
            right = jnp.concatenate([own_ref[tokens, cols], other_ref[tokens, cols]], axis=0)
            product = jnp.dot(left, right, preferred_element_type=jnp.float32)
            total = product if total is None else total + product
        sum_ref[:, cols] = total.astype(jnp.bfloat16)
    near = near_ref[0]
    for i, out_ref in enumerate(out_refs):
        wanted = 1 - near if i % 2 == 0 else near
        out_ref[...] = sum_ref[pl.ds(pl.multiple_of((i // 2 * 2 + wanted) * rows, 16), rows), :]


def outer_kernel(place_ref, grad_ref, mine_ref, theirs_ref, *refs):
    own_refs, other_refs, (w_ref, sems) = refs[:2], refs[2:4], refs[4:]
    tile = own_refs[0].shape[0]
    width = w_ref.shape[0]
    rows = width // 16
    part = w_ref.shape[1] // 4
    step = width // 4
    copies = []
    for i in range(16):
        source = (mine_ref if i < 8 else theirs_ref).at[pl.ds(i % 8 * rows, rows), :]
        into = w_ref.at[pl.ds(pl.multiple_of(place_ref[i] * rows, 16), rows), :]
        copies.append(pltpu.make_async_copy(source, into, sems.at[i]))
    for copy in copies:
        copy.start()
    for copy in copies:
        copy.wait()
    for n in range(4):
        at = pl.ds(n * step, step)
        for k, w_cols in enumerate((pl.ds(3 * part, part), pl.ds(0, 3 * part))):
            product = across(grad_ref[:, w_cols], w_ref[at, w_cols])
            own_refs[k][:, at] = product[:tile]
            other_refs[k][:, at] = product[tile:].astype(jnp.bfloat16)


def after(value, earlier):
    return lax.optimization_barrier((value, earlier))[0]


def kernel_call(body, outs, in_specs, out_specs, scratch, flops, moved, name, room=58):
    return pl.pallas_call(
        body,
        out_shape=outs,
        in_specs=in_specs,
        out_specs=out_specs,
        scratch_shapes=scratch,
        compiler_params=pltpu.CompilerParams(vmem_limit_bytes=room * 1024 * 1024),
        cost_estimate=pl.CostEstimate(flops=flops, bytes_accessed=moved, transcendentals=0),
        name=name,
    )


def on_device(tokens, land, surface, gain, weights, shifts, index_table, bias_table, cotangent):
    levels, side, _, width = tokens.shape
    area = side * side
    tile = levels * area
    heads = bias_table.shape[2]
    entries = bias_table.shape[1]
    own_rows = weights.shape[0]
    part = weights.shape[1] // 8
    head = weights.shape[1] // 4 // heads
    own_heads = heads // 2
    far, near, beside, core = (lax.axis_index(axis) for axis in LON)
    grp = lax.axis_index("grp")
    first = near == 0
    f32 = jnp.float32

    def place(f, n, s, c):
        return ((far ^ f) * 4 + (near ^ n) * 2 + (beside ^ s)) * 2 + (core ^ c)

    low = jnp.concatenate([weights[:, 2 * k * part : (2 * k + 1) * part] for k in range(4)], axis=1)
    high = jnp.concatenate([weights[:, (2 * k + 1) * part : (2 * k + 2) * part] for k in range(4)], axis=1)
    mine = jnp.where(first, low, high)
    came = swap(jnp.where(first, high, low), "near")
    flat_cot = cotangent.reshape(tile, width)
    surface_term = jnp.where(land[None, :, :, None] == 1, surface[1], surface[0])
    stream = (tokens.astype(f32) + surface_term).astype(jnp.bfloat16).reshape(tile, width)
    values = stream.astype(f32)
    center = values - jnp.mean(values, axis=-1, keepdims=True)
    spread = lax.rsqrt(jnp.mean(center * center, axis=-1, keepdims=True) + epsilon)

    held = near ^ grp
    half_piece = jnp.where(grp == 0, mine, came)
    across_far = swap(half_piece, "far")
    order = [(f, s, n) for f in (1, 0) for s in (1, 0) for n in (0, 1)]
    natural = [place(f, near ^ n, s, c) for c in (0, 1) for f, s, n in order]

    vmem = pl.BlockSpec(memory_space=pltpu.VMEM)
    smem = pl.BlockSpec(memory_space=pltpu.SMEM)
    anywhere = pl.BlockSpec(memory_space=pl.ANY)
    dma = pltpu.SemaphoreType.DMA

    rows, below, below_cot = shifts[:, 0], stream, flat_cot
    if lax.axis_size("lat") > 1:
        zeros = jnp.zeros_like(rows)
        onehot_rows = pick(rows, zeros, levels, side, True)
        below = picked(onehot_rows, stream, along_lat(stream, -1))
        below_cot = picked(onehot_rows, flat_cot, along_lat(flat_cot, -1))
        rows = zeros
    moved, moved_cot = along_lon(below, -1), along_lon(below_cot, -1)
    info = jnp.concatenate(
        [jnp.stack([rows, shifts[:, 1]], axis=1).reshape(-1), jnp.stack(natural)]
    ).astype(jnp.int32)
    half = width // 2
    turned = jax.ShapeDtypeStruct((2, half, tile), jnp.bfloat16)
    own_turned, sent_turned = kernel_call(
        turned_rolls,
        (turned, turned),
        [smem, vmem] + [anywhere] * 4,
        (vmem, vmem),
        [
            pltpu.VMEM((2, 2 * tile, width), jnp.bfloat16),
            pltpu.VMEM((width, tile), jnp.bfloat16),
            dma((4,)),
        ],
        2 * 2 * 2 * tile * tile * width,
        3_000_000,
        "turned_rolls",
        24,
    )(info, gain.reshape(1, -1), below, moved, below_cot, moved_cot)
    mine_side = swap(after(mine, (moved, moved_cot)), "side")
    across_far = after(across_far, mine_side)
    far_side, far_grp = swap(across_far, "side"), swap(across_far, "grp")
    came_side = swap(after(came, far_grp), "side")
    pieces = [
        (mine, 0, 0, near),
        (came, 0, 0, 1 - near),
        (mine_side, 0, 1, near),
        (came_side, 0, 1, 1 - near),
        (across_far, 1, 0, held),
        (far_grp, 1, 0, 1 - held),
        (far_side, 1, 1, held),
        (swap(far_side, "grp"), 1, 1, 1 - held),
    ]
    places = jnp.stack([(1 - f) * 4 + (1 - s) * 2 + n for _, f, s, n in pieces]).astype(jnp.int32)
    own_near, sent_near = swap(own_turned, "near"), swap(sent_turned, "near")
    tiles = [own_turned, swap(after(sent_turned, (sent_near, far_grp)), "core"), own_near, swap(after(sent_near, far_grp), "core")]

    onehot = (index_table[:, :, None] == jnp.arange(entries, dtype=jnp.int32)).astype(f32)
    own_table = lax.dynamic_slice_in_dim(bias_table, near * own_heads, own_heads, 2)
    bias = jnp.einsum("qkr,lrh->lhqk", onehot, own_table, precision=lax.Precision.HIGHEST)
    row_number = lax.axis_index("lat") * side + jnp.arange(side, dtype=jnp.int32)
    group = row_number[None, :] >= (side * lax.axis_size("lat") - shifts[:, 0])[:, None]
    group = jnp.repeat(group, side, axis=1)
    allowed = group[:, :, None] == group[:, None, :]
    bias = jnp.where(allowed[:, None], bias, -1e30).reshape(levels, own_heads // 2, 2 * area, area)

    bf16 = jnp.bfloat16
    kept, sent, w_mine = kernel_call(
        products_kernel,
        (
            jax.ShapeDtypeStruct((2 * tile, 4 * part), bf16),
            jax.ShapeDtypeStruct((2 * tile, 4 * part), bf16),
            jax.ShapeDtypeStruct((half, 4 * part), bf16),
        ),
        [smem] + [anywhere] * 12,
        (vmem, vmem, anywhere),
        [
            pltpu.VMEM((4, 2, half, tile), bf16),
            pltpu.VMEM((2, 4 * tile, half), bf16),
            pltpu.VMEM((half, 4 * part), bf16),
            dma((12,)),
            dma,
        ],
        1_200_000_000,
        9_000_000,
        "products",
    )(after(places, bias), *tiles, *[piece for piece, *_ in pieces])
    crossed = swap(sent, "core")
    grad = kernel_call(
        functools.partial(attention_kernel, area, head),
        jax.ShapeDtypeStruct((2 * tile, 4 * part), bf16),
        [vmem] * 3,
        vmem,
        [pltpu.VMEM((2 * tile, 4 * part), bf16)]
        + [pltpu.VMEM((2 * tile // area * own_heads // 2, 2 * area, area), kind) for kind in (f32, f32, bf16, bf16)],
        1_000_000_000,
        4_000_000,
        "attention",
    )(kept, crossed, bias)
    w_theirs = swap(after(w_mine, crossed), "core")
    grad_theirs = swap(grad, "core")
    attended_own, grad_own, attended_other, grad_other = kernel_call(
        outer_kernel,
        (jax.ShapeDtypeStruct((tile, width), f32),) * 2 + (jax.ShapeDtypeStruct((tile, width), bf16),) * 2,
        [smem, vmem, anywhere, anywhere],
        (vmem,) * 4,
        [pltpu.VMEM((width, 4 * part), bf16), dma((16,))],
        1_200_000_000,
        8_000_000,
        "projections",
        24,
    )(jnp.stack(natural).astype(jnp.int32), grad, w_mine, w_theirs)
    blocks = kernel_call(
        weights_kernel,
        [jax.ShapeDtypeStruct((own_rows, 4 * part), bf16)] * 8,
        [smem] + [anywhere] * 4 + [vmem] * 2,
        [vmem] * 8,
        [
            pltpu.VMEM((4, 2, half, tile), bf16),
            pltpu.VMEM((half, 4 * part), bf16),
            dma((4,)),
        ],
        1_200_000_000,
        6_000_000,
        "weight_gradient",
        24,
    )(after(near.astype(jnp.int32).reshape(1), grad_other), *tiles, grad, grad_theirs)

    def block(f, s, n):
        return blocks[((1 - f) * 2 + 1 - s) * 2 + 1 - n]

    arrived_first = swap(attended_other, "near")
    side_far_1 = after(swap(block(1, 1, 1), "side"), arrived_first)
    arrived_back = swap(grad_other, "near")
    side_far_0 = swap(after(block(1, 1, 0), (side_far_1, arrived_first)), "side")
    far_1 = swap((block(1, 0, 1).astype(f32) + side_far_1.astype(f32)).astype(bf16), "far")
    far_0 = swap(after((block(1, 0, 0).astype(f32) + side_far_0.astype(f32)).astype(bf16), (far_1, arrived_back)), "far")
    side_1 = swap(after(block(0, 1, 1), side_far_0), "side")
    side_0 = swap(after(block(0, 1, 0), side_1), "side")
    total_1 = (block(0, 0, 1).astype(f32) + side_1.astype(f32) + far_1.astype(f32)).astype(bf16)
    theirs = swap(total_1, "near").astype(f32)

    first_back = roll_back((attended_own + arrived_first.astype(f32)).astype(bf16), shifts, levels, side, ())
    output = (values + first_back.astype(f32)).astype(bf16)
    back = roll_back((grad_own + arrived_back.astype(f32)).astype(bf16), shifts, levels, side, (theirs, output))
    back = after(back, far_0)
    scaled = center * spread
    upstream = back.astype(f32) * gain
    grad_stream = spread * (
        upstream
        - jnp.mean(upstream, axis=-1, keepdims=True)
        - scaled * jnp.mean(upstream * scaled, axis=-1, keepdims=True)
    )
    grad_tokens = (flat_cot.astype(f32) + grad_stream).astype(jnp.bfloat16)

    far_0 = after(far_0, (output, grad_tokens))
    total_0 = block(0, 0, 0).astype(f32) + side_0.astype(f32) + far_0.astype(f32)
    token_count = tile * lax.axis_size("lat") * math.prod(lax.axis_size(axis) for axis in LON)
    columns = []
    for k in range(4):
        cols = slice(k * part, (k + 1) * part)
        columns += [
            jnp.where(first, total_0[:, cols], theirs[:, cols]),
            jnp.where(first, theirs[:, cols], total_0[:, cols]),
        ]
    summed = jnp.concatenate(columns, axis=1)
    if lax.axis_size("lat") > 1:
        summed = lax.psum(summed.astype(jnp.bfloat16), "lat").astype(f32)
    grad_weights = summed * (1.0 / math.sqrt(token_count))
    return (output.reshape(tokens.shape), grad_tokens.reshape(tokens.shape), grad_weights)


def solution(mesh):
    sizes = dict(mesh.shape)
    devices = mesh.devices.reshape(sizes["grp"], sizes["lon"] // 8, 2, 2, 2, sizes["lat"])
    finer = Mesh(devices, ("grp",) + LON + ("lat",))
    return jax.shard_map(
        on_device,
        mesh=finer,
        in_specs=(
            P("grp", "lat", LON, None),
            P(("grp", "lat"), LON),
            P(),
            P(),
            P(LON, None),
            P(),
            P(),
            P("lat", None, None),
            P("grp", "lat", LON, None),
        ),
        out_specs=(
            P("grp", "lat", LON, None),
            P("grp", "lat", LON, None),
            P(("grp",) + LON, None),
        ),
        check_vma=False,
    )
```

```python
import functools
import math

import jax
import jax.numpy as jnp
from jax import lax
from jax.experimental import pallas as pl
from jax.experimental.pallas import tpu as pltpu
from jax.sharding import Mesh
from jax.sharding import PartitionSpec as P

epsilon = 1e-05
LON = ("far", "near", "side", "core")


def along_lon(shard, by):
    count = math.prod(lax.axis_size(axis) for axis in LON)
    return lax.ppermute(shard, LON, [(i, (i + by) % count) for i in range(count)])


def along_lat(shard, by):
    count = lax.axis_size("lat")
    return lax.ppermute(shard, "lat", [(i, (i + by) % count) for i in range(count)])


def swap(shard, axis):
    return lax.ppermute(shard, axis, [(0, 1), (1, 0)])


def pick(rows, cols, levels, side, over_rows):
    tile = levels * side * side
    shape = (tile, 2 * tile)
    target = lax.broadcasted_iota(jnp.int32, shape, 0)
    source = lax.broadcasted_iota(jnp.int32, shape, 1)
    level = target // (side * side)
    row = target // side % side
    col = target % side
    from_row = jnp.full_like(row, rows[levels - 1])
    from_col = jnp.full_like(col, cols[levels - 1])
    for l in range(levels - 1):
        from_row = jnp.where(level == l, rows[l], from_row)
        from_col = jnp.where(level == l, cols[l], from_col)
    from_row = row + from_row
    from_col = col + from_col
    which = (from_row if over_rows else from_col) // side
    wanted = which * tile + level * side * side + from_row % side * side + from_col % side
    return (source == wanted).astype(jnp.bfloat16)


def picked(onehot, first, second):
    both = jnp.concatenate([first, second], axis=0)
    return jnp.dot(onehot, both, preferred_element_type=jnp.float32).astype(jnp.bfloat16)


def roll_back(field, shifts, levels, side, wait):
    zeros = jnp.zeros_like(shifts[:, 0])
    rows = side - shifts[:, 0]
    more = lax.axis_size("lat") > 1
    field = picked(
        pick(zeros if more else rows, side - shifts[:, 1], levels, side, False),
        after(along_lon(field, 1), wait),
        field,
    )
    if more:
        field = picked(pick(rows, zeros, levels, side, True), along_lat(field, 1), field)
    return field


def turned_rolls(info_ref, gain_ref, *refs):
    fields, (kept_ref, sent_ref, both_ref, turned_ref, sems) = refs[:4], refs[4:]
    tile = fields[0].shape[0]
    rows = kept_ref.shape[1] // 8
    levels, side = 2, 8
    area = tile // levels
    copies = [
        pltpu.make_async_copy(field, both_ref.at[i // 2, pl.ds(i % 2 * tile, tile), :], sems.at[i])
        for i, field in enumerate(fields)
    ]
    for copy in copies:
        copy.start()
    target = lax.broadcasted_iota(jnp.int32, (tile, 2 * tile), 0)
    source = lax.broadcasted_iota(jnp.int32, (tile, 2 * tile), 1)
    upper = target < area
    row = ((target >> 3) & 7) + jnp.where(upper, info_ref[0], info_ref[2])
    col = (target & 7) + jnp.where(upper, info_ref[1], info_ref[3])
    wanted = jnp.where(col >= side, tile, 0) + jnp.where(upper, 0, area) + (row & 7) * side + (col & 7)
    onehot = jnp.where(source == wanted, 1.0, 0.0).astype(jnp.bfloat16)
    for k in (1, 0):
        copies[2 * k].wait()
        copies[2 * k + 1].wait()
        rolled = jnp.dot(onehot, both_ref[k], preferred_element_type=jnp.float32)
        if k == 0:
            center = rolled - jnp.mean(rolled, axis=-1, keepdims=True)
            spread = lax.rsqrt(jnp.mean(center * center, axis=-1, keepdims=True) + epsilon)
            rolled = center * spread * gain_ref[...]
        turned_ref[...] = rolled.astype(jnp.bfloat16).T
        for i in range(8):
            at = pl.ds(i * rows, rows)
            kept_ref[k, at, :] = turned_ref[pl.ds(pl.multiple_of(info_ref[4 + i] * rows, 16), rows), :]
            sent_ref[k, at, :] = turned_ref[pl.ds(pl.multiple_of(info_ref[12 + i] * rows, 16), rows), :]


def down(a, b):
    return lax.dot_general(a, b, (((0,), (0,)), ((), ())), preferred_element_type=jnp.float32)


def across(a, b):
    return lax.dot_general(a, b, (((1,), (1,)), ((), ())), preferred_element_type=jnp.float32)


def products_kernel(place_ref, *refs):
    tiles, pieces = refs[:4], refs[4:12]
    kept_ref, sent_ref, full_ref, tile_ref, x_ref, w_ref, sems, out_sem = refs[12:]
    tile = tiles[0].shape[2]
    part = w_ref.shape[1] // 4
    copies = []
    for i, piece in enumerate(pieces):
        rows = pl.ds(pl.multiple_of(place_ref[i] * piece.shape[0], 16), piece.shape[0])
        copies.append(pltpu.make_async_copy(piece, w_ref.at[rows, :], sems.at[i]))
    for j, source in enumerate(tiles):
        copies.append(pltpu.make_async_copy(source, tile_ref.at[j], sems.at[8 + j]))
    for copy in copies[8:] + copies[:8]:
        copy.start()
    for j, at in enumerate((0, 2, 1, 3)):
        copies[8 + j].wait()
        for kind in range(2):
            x_ref[kind, pl.ds(at * tile, tile), :] = tile_ref[j, kind].T
    for copy in copies[:8]:
        copy.wait()
    out_copy = pltpu.make_async_copy(w_ref, full_ref, out_sem)
    out_copy.start()
    for n in range(4):
        cols = pl.ds(n * part, part)
        product = jnp.dot(x_ref[n // 3], w_ref[:, cols], preferred_element_type=jnp.float32)
        kept_ref[:, cols] = product[: 2 * tile].astype(jnp.bfloat16)
        sent_ref[:, cols] = product[2 * tile :].astype(jnp.bfloat16)
    out_copy.wait()


def attention_kernel(area, head, kept_ref, came_ref, bias_ref, grad_ref, qkv_ref, scores_ref, toward_ref, probs_ref, back_ref):
    part = grad_ref.shape[1] // 4
    levels, pairs = bias_ref.shape[:2]
    scale = 1.0 / math.sqrt(head)
    lane = lax.broadcasted_iota(jnp.int32, (area, 2 * head), 1)
    left = lane < head

    def stacked(pair):
        zero = jnp.zeros_like(pair)
        return jnp.concatenate([jnp.where(left, pair, zero), jnp.where(left, zero, pair)], axis=0)

    def unstacked(product):
        return jnp.where(left, product[:area], product[area:]).astype(jnp.bfloat16)

    windows = grad_ref.shape[0] // area
    groups = [(w * pairs + p, w, p) for w in range(windows) for p in range(pairs)]

    def view(w, p, n):
        return pl.ds(w * area, area), pl.ds(n * part + p * 2 * head, 2 * head)

    qkv_ref[...] = (kept_ref[...].astype(jnp.float32) + came_ref[...].astype(jnp.float32)).astype(jnp.bfloat16)
    for g, w, p in groups:
        scores_ref[g] = across(stacked(qkv_ref[view(w, p, 0)]), qkv_ref[view(w, p, 1)])
        toward_ref[g] = across(stacked(qkv_ref[view(w, p, 3)]), qkv_ref[view(w, p, 2)])
    for g, w, p in groups:
        scores = scores_ref[g] * scale + bias_ref[w % levels, p]
        expo = jnp.exp(scores - jnp.max(scores, axis=-1, keepdims=True))
        probs = expo / jnp.sum(expo, axis=-1, keepdims=True)
        grad_probs = toward_ref[g]
        inner = jnp.sum(probs * grad_probs, axis=-1, keepdims=True)
        probs_ref[g] = probs.astype(jnp.bfloat16)
        back_ref[g] = (probs * (grad_probs - inner) * scale).astype(jnp.bfloat16)
    for g, w, p in groups:
        probs_b, grad_scores = probs_ref[g], back_ref[g]
        grad_ref[view(w, p, 3)] = unstacked(
            jnp.dot(probs_b, qkv_ref[view(w, p, 2)], preferred_element_type=jnp.float32)
        )
        grad_ref[view(w, p, 0)] = unstacked(
            jnp.dot(grad_scores, qkv_ref[view(w, p, 1)], preferred_element_type=jnp.float32)
        )
        grad_ref[view(w, p, 2)] = down(probs_b, stacked(qkv_ref[view(w, p, 3)])).astype(jnp.bfloat16)
        grad_ref[view(w, p, 1)] = down(grad_scores, stacked(qkv_ref[view(w, p, 0)])).astype(jnp.bfloat16)


def weights_kernel(near_ref, *refs):
    tiles, (own_ref, other_ref), out_refs = refs[:4], refs[4:6], refs[6:14]
    tile_ref, sum_ref, sems = refs[14:]
    tile = tiles[0].shape[2]
    part = own_ref.shape[1] // 4
    rows = out_refs[0].shape[0]
    copies = [pltpu.make_async_copy(source, tile_ref.at[j], sems.at[j]) for j, source in enumerate(tiles)]
    for copy in copies:
        copy.start()
    for copy in copies:
        copy.wait()
    for n in range(4):
        cols = pl.ds(n * part, part)
        total = None
        for t in range(2):
            tokens = pl.ds(t * tile, tile)
            left = jnp.concatenate([tile_ref[2 * t, n // 3], tile_ref[2 * t + 1, n // 3]], axis=1)
            right = jnp.concatenate([own_ref[tokens, cols], other_ref[tokens, cols]], axis=0)
            product = jnp.dot(left, right, preferred_element_type=jnp.float32)
            total = product if total is None else total + product
        sum_ref[:, cols] = total.astype(jnp.bfloat16)
    near = near_ref[0]
    for i, out_ref in enumerate(out_refs):
        wanted = 1 - near if i % 2 == 0 else near
        out_ref[...] = sum_ref[pl.ds(pl.multiple_of((i // 2 * 2 + wanted) * rows, 16), rows), :]


def outer_kernel(place_ref, grad_ref, mine_ref, theirs_ref, own_ref, other_ref, w_ref, sems):
    tile = own_ref.shape[0]
    width = w_ref.shape[0]
    rows = width // 16
    part = w_ref.shape[1] // 4
    step = width // 4
    copies = []
    for i in range(16):
        source = (mine_ref if i < 8 else theirs_ref).at[pl.ds(i % 8 * rows, rows), :]
        into = w_ref.at[pl.ds(pl.multiple_of(place_ref[i] * rows, 16), rows), :]
        copies.append(pltpu.make_async_copy(source, into, sems.at[i]))
    for copy in copies:
        copy.start()
    for copy in copies:
        copy.wait()
    for n in range(4):
        at = pl.ds(n * step, step)
        for k, w_cols in enumerate((pl.ds(3 * part, part), pl.ds(0, 3 * part))):
            product = across(grad_ref[:, w_cols], w_ref[at, w_cols])
            cols = pl.ds(k * width + n * step, step)
            own_ref[:, cols] = product[:tile]
            other_ref[:, cols] = product[tile:].astype(jnp.bfloat16)


def after(value, earlier):
    return lax.optimization_barrier((value, earlier))[0]


def kernel_call(body, outs, in_specs, out_specs, scratch, flops, moved, name, room=58):
    return pl.pallas_call(
        body,
        out_shape=outs,
        in_specs=in_specs,
        out_specs=out_specs,
        scratch_shapes=scratch,
        compiler_params=pltpu.CompilerParams(vmem_limit_bytes=room * 1024 * 1024),
        cost_estimate=pl.CostEstimate(flops=flops, bytes_accessed=moved, transcendentals=0),
        name=name,
    )


def on_device(tokens, land, surface, gain, weights, shifts, index_table, bias_table, cotangent):
    levels, side, _, width = tokens.shape
    area = side * side
    tile = levels * area
    heads = bias_table.shape[2]
    entries = bias_table.shape[1]
    own_rows = weights.shape[0]
    part = weights.shape[1] // 8
    head = weights.shape[1] // 4 // heads
    own_heads = heads // 2
    far, near, beside, core = (lax.axis_index(axis) for axis in LON)
    grp = lax.axis_index("grp")
    first = near == 0
    f32 = jnp.float32

    def place(f, n, s, c):
        return ((far ^ f) * 4 + (near ^ n) * 2 + (beside ^ s)) * 2 + (core ^ c)

    low = jnp.concatenate([weights[:, 2 * k * part : (2 * k + 1) * part] for k in range(4)], axis=1)
    high = jnp.concatenate([weights[:, (2 * k + 1) * part : (2 * k + 2) * part] for k in range(4)], axis=1)
    mine = jnp.where(first, low, high)
    came = swap(jnp.where(first, high, low), "near")
    flat_cot = cotangent.reshape(tile, width)
    surface_term = jnp.where(land[None, :, :, None] == 1, surface[1], surface[0])
    stream = (tokens.astype(f32) + surface_term).astype(jnp.bfloat16).reshape(tile, width)
    values = stream.astype(f32)
    center = values - jnp.mean(values, axis=-1, keepdims=True)
    spread = lax.rsqrt(jnp.mean(center * center, axis=-1, keepdims=True) + epsilon)

    held = near ^ grp
    half_piece = jnp.where(grp == 0, mine, came)
    across_far = swap(half_piece, "far")
    order = [(f, s, n) for f in (1, 0) for s in (1, 0) for n in (0, 1)]
    natural = [place(f, near ^ n, s, c) for c in (0, 1) for f, s, n in order]

    vmem = pl.BlockSpec(memory_space=pltpu.VMEM)
    smem = pl.BlockSpec(memory_space=pltpu.SMEM)
    anywhere = pl.BlockSpec(memory_space=pl.ANY)
    dma = pltpu.SemaphoreType.DMA

    rows, below, below_cot = shifts[:, 0], stream, flat_cot
    if lax.axis_size("lat") > 1:
        zeros = jnp.zeros_like(rows)
        onehot_rows = pick(rows, zeros, levels, side, True)
        below = picked(onehot_rows, stream, along_lat(stream, -1))
        below_cot = picked(onehot_rows, flat_cot, along_lat(flat_cot, -1))
        rows = zeros
    moved, moved_cot = along_lon(below, -1), along_lon(below_cot, -1)
    info = jnp.concatenate(
        [jnp.stack([rows, shifts[:, 1]], axis=1).reshape(-1), jnp.stack(natural)]
    ).astype(jnp.int32)
    half = width // 2
    turned = jax.ShapeDtypeStruct((2, half, tile), jnp.bfloat16)
    own_turned, sent_turned = kernel_call(
        turned_rolls,
        (turned, turned),
        [smem, vmem] + [anywhere] * 4,
        (vmem, vmem),
        [
            pltpu.VMEM((2, 2 * tile, width), jnp.bfloat16),
            pltpu.VMEM((width, tile), jnp.bfloat16),
            dma((4,)),
        ],
        2 * 2 * 2 * tile * tile * width,
        3_000_000,
        "turned_rolls",
        24,
    )(info, gain.reshape(1, -1), below, moved, below_cot, moved_cot)
    mine_side = swap(after(mine, (moved, moved_cot)), "side")
    across_far = after(across_far, mine_side)
    far_side, far_grp = swap(across_far, "side"), swap(across_far, "grp")
    came_side = swap(after(came, far_grp), "side")
    pieces = [
        (mine, 0, 0, near),
        (came, 0, 0, 1 - near),
        (mine_side, 0, 1, near),
        (came_side, 0, 1, 1 - near),
        (across_far, 1, 0, held),
        (far_grp, 1, 0, 1 - held),
        (far_side, 1, 1, held),
        (swap(far_side, "grp"), 1, 1, 1 - held),
    ]
    places = jnp.stack([(1 - f) * 4 + (1 - s) * 2 + n for _, f, s, n in pieces]).astype(jnp.int32)
    own_near, sent_near = swap(own_turned, "near"), swap(sent_turned, "near")
    tiles = [own_turned, swap(after(sent_turned, (sent_near, far_grp)), "core"), own_near, swap(after(sent_near, far_grp), "core")]

    onehot = (index_table[:, :, None] == jnp.arange(entries, dtype=jnp.int32)).astype(f32)
    own_table = lax.dynamic_slice_in_dim(bias_table, near * own_heads, own_heads, 2)
    bias = jnp.einsum("qkr,lrh->lhqk", onehot, own_table, precision=lax.Precision.HIGHEST)
    row_number = lax.axis_index("lat") * side + jnp.arange(side, dtype=jnp.int32)
    group = row_number[None, :] >= (side * lax.axis_size("lat") - shifts[:, 0])[:, None]
    group = jnp.repeat(group, side, axis=1)
    allowed = group[:, :, None] == group[:, None, :]
    bias = jnp.where(allowed[:, None], bias, -1e30).reshape(levels, own_heads // 2, 2 * area, area)

    bf16 = jnp.bfloat16
    kept, sent, w_mine = kernel_call(
        products_kernel,
        (
            jax.ShapeDtypeStruct((2 * tile, 4 * part), bf16),
            jax.ShapeDtypeStruct((2 * tile, 4 * part), bf16),
            jax.ShapeDtypeStruct((half, 4 * part), bf16),
        ),
        [smem] + [anywhere] * 12,
        (vmem, vmem, anywhere),
        [
            pltpu.VMEM((4, 2, half, tile), bf16),
            pltpu.VMEM((2, 4 * tile, half), bf16),
            pltpu.VMEM((half, 4 * part), bf16),
            dma((12,)),
            dma,
        ],
        1_200_000_000,
        9_000_000,
        "products",
    )(after(places, bias), *tiles, *[piece for piece, *_ in pieces])
    crossed = swap(sent, "core")
    grad = kernel_call(
        functools.partial(attention_kernel, area, head),
        jax.ShapeDtypeStruct((2 * tile, 4 * part), bf16),
        [vmem] * 3,
        vmem,
        [pltpu.VMEM((2 * tile, 4 * part), bf16)]
        + [pltpu.VMEM((2 * tile // area * own_heads // 2, 2 * area, area), kind) for kind in (f32, f32, bf16, bf16)],
        1_000_000_000,
        4_000_000,
        "attention",
    )(kept, crossed, bias)
    w_theirs = swap(after(w_mine, crossed), "core")
    grad_theirs = swap(grad, "core")
    attended_own, attended_other = kernel_call(
        outer_kernel,
        (
            jax.ShapeDtypeStruct((tile, 2 * width), f32),
            jax.ShapeDtypeStruct((tile, 2 * width), bf16),
        ),
        [smem, vmem, anywhere, anywhere],
        (vmem, vmem),
        [pltpu.VMEM((width, 4 * part), bf16), dma((16,))],
        1_200_000_000,
        8_000_000,
        "projections",
        24,
    )(jnp.stack(natural).astype(jnp.int32), grad, w_mine, w_theirs)
    blocks = kernel_call(
        weights_kernel,
        [jax.ShapeDtypeStruct((own_rows, 4 * part), bf16)] * 8,
        [smem] + [anywhere] * 4 + [vmem] * 2,
        [vmem] * 8,
        [
            pltpu.VMEM((4, 2, half, tile), bf16),
            pltpu.VMEM((half, 4 * part), bf16),
            dma((4,)),
        ],
        1_200_000_000,
        6_000_000,
        "weight_gradient",
        24,
    )(after(near.astype(jnp.int32).reshape(1), attended_other), *tiles, grad, grad_theirs)

    def block(f, s, n):
        return blocks[((1 - f) * 2 + 1 - s) * 2 + 1 - n]

    side_far_1 = swap(block(1, 1, 1), "side")
    arrived_back = swap(attended_other, "near")
    side_far_0 = swap(after(block(1, 1, 0), side_far_1), "side")
    far_1 = swap((block(1, 0, 1).astype(f32) + side_far_1.astype(f32)).astype(bf16), "far")
    far_0 = swap(after((block(1, 0, 0).astype(f32) + side_far_0.astype(f32)).astype(bf16), (far_1, arrived_back)), "far")
    side_1 = swap(after(block(0, 1, 1), side_far_0), "side")
    side_0 = swap(after(block(0, 1, 0), side_1), "side")
    total_1 = (block(0, 0, 1).astype(f32) + side_1.astype(f32) + far_1.astype(f32)).astype(bf16)
    theirs = swap(total_1, "near").astype(f32)

    back = (attended_own + arrived_back.astype(f32)).astype(jnp.bfloat16)
    back = after(roll_back(after(back, far_1), shifts, levels, side, ()), far_0)
    output = (values + back[:, :width].astype(f32)).astype(jnp.bfloat16)
    scaled = center * spread
    upstream = back[:, width:].astype(f32) * gain
    grad_stream = spread * (
        upstream
        - jnp.mean(upstream, axis=-1, keepdims=True)
        - scaled * jnp.mean(upstream * scaled, axis=-1, keepdims=True)
    )
    grad_tokens = (flat_cot.astype(f32) + grad_stream).astype(jnp.bfloat16)

    far_0 = after(far_0, (output, grad_tokens))
    total_0 = block(0, 0, 0).astype(f32) + side_0.astype(f32) + far_0.astype(f32)
    token_count = tile * lax.axis_size("lat") * math.prod(lax.axis_size(axis) for axis in LON)
    columns = []
    for k in range(4):
        cols = slice(k * part, (k + 1) * part)
        columns += [
            jnp.where(first, total_0[:, cols], theirs[:, cols]),
            jnp.where(first, theirs[:, cols], total_0[:, cols]),
        ]
    summed = jnp.concatenate(columns, axis=1)
    if lax.axis_size("lat") > 1:
        summed = lax.psum(summed.astype(jnp.bfloat16), "lat").astype(f32)
    grad_weights = summed * (1.0 / math.sqrt(token_count))
    return (output.reshape(tokens.shape), grad_tokens.reshape(tokens.shape), grad_weights)


def solution(mesh):
    sizes = dict(mesh.shape)
    devices = mesh.devices.reshape(sizes["grp"], sizes["lon"] // 8, 2, 2, 2, sizes["lat"])
    finer = Mesh(devices, ("grp",) + LON + ("lat",))
    return jax.shard_map(
        on_device,
        mesh=finer,
        in_specs=(
            P("grp", "lat", LON, None),
            P(("grp", "lat"), LON),
            P(),
            P(),
            P(LON, None),
            P(),
            P(),
            P("lat", None, None),
            P("grp", "lat", LON, None),
        ),
        out_specs=(
            P("grp", "lat", LON, None),
            P("grp", "lat", LON, None),
            P(("grp",) + LON, None),
        ),
        check_vma=False,
    )
```

```python
import functools
import math

import jax
import jax.numpy as jnp
from jax import lax
from jax.experimental import pallas as pl
from jax.experimental.pallas import tpu as pltpu
from jax.sharding import Mesh
from jax.sharding import PartitionSpec as P

epsilon = 1e-05
LON = ("far", "near", "side", "core")


def along_lon(shard, by):
    count = math.prod(lax.axis_size(axis) for axis in LON)
    return lax.ppermute(shard, LON, [(i, (i + by) % count) for i in range(count)])


def along_lat(shard, by):
    count = lax.axis_size("lat")
    return lax.ppermute(shard, "lat", [(i, (i + by) % count) for i in range(count)])


def swap(shard, axis):
    return lax.ppermute(shard, axis, [(0, 1), (1, 0)])


def pick(rows, cols, levels, side, over_rows):
    tile = levels * side * side
    shape = (tile, 2 * tile)
    target = lax.broadcasted_iota(jnp.int32, shape, 0)
    source = lax.broadcasted_iota(jnp.int32, shape, 1)
    level = target // (side * side)
    row = target // side % side
    col = target % side
    from_row = jnp.full_like(row, rows[levels - 1])
    from_col = jnp.full_like(col, cols[levels - 1])
    for l in range(levels - 1):
        from_row = jnp.where(level == l, rows[l], from_row)
        from_col = jnp.where(level == l, cols[l], from_col)
    from_row = row + from_row
    from_col = col + from_col
    which = (from_row if over_rows else from_col) // side
    wanted = which * tile + level * side * side + from_row % side * side + from_col % side
    return (source == wanted).astype(jnp.bfloat16)


def picked(onehot, first, second):
    both = jnp.concatenate([first, second], axis=0)
    return jnp.dot(onehot, both, preferred_element_type=jnp.float32).astype(jnp.bfloat16)


def roll_back(field, shifts, levels, side, wait):
    zeros = jnp.zeros_like(shifts[:, 0])
    rows = side - shifts[:, 0]
    more = lax.axis_size("lat") > 1
    field = picked(
        pick(zeros if more else rows, side - shifts[:, 1], levels, side, False),
        after(along_lon(field, 1), wait),
        field,
    )
    if more:
        field = picked(pick(rows, zeros, levels, side, True), along_lat(field, 1), field)
    return field


def turned_rolls(info_ref, gain_ref, *refs):
    fields, (kept_ref, sent_ref, both_ref, turned_ref, sems) = refs[:4], refs[4:]
    tile = fields[0].shape[0]
    rows = kept_ref.shape[1] // 8
    levels, side = 2, 8
    area = tile // levels
    copies = [
        pltpu.make_async_copy(field, both_ref.at[i // 2, pl.ds(i % 2 * tile, tile), :], sems.at[i])
        for i, field in enumerate(fields)
    ]
    for copy in copies:
        copy.start()
    target = lax.broadcasted_iota(jnp.int32, (tile, 2 * tile), 0)
    source = lax.broadcasted_iota(jnp.int32, (tile, 2 * tile), 1)
    upper = target < area
    row = ((target >> 3) & 7) + jnp.where(upper, info_ref[0], info_ref[2])
    col = (target & 7) + jnp.where(upper, info_ref[1], info_ref[3])
    wanted = jnp.where(col >= side, tile, 0) + jnp.where(upper, 0, area) + (row & 7) * side + (col & 7)
    onehot = jnp.where(source == wanted, 1.0, 0.0).astype(jnp.bfloat16)
    for k in (1, 0):
        copies[2 * k].wait()
        copies[2 * k + 1].wait()
        rolled = jnp.dot(onehot, both_ref[k], preferred_element_type=jnp.float32)
        if k == 0:
            center = rolled - jnp.mean(rolled, axis=-1, keepdims=True)
            spread = lax.rsqrt(jnp.mean(center * center, axis=-1, keepdims=True) + epsilon)
            rolled = center * spread * gain_ref[...]
        turned_ref[...] = rolled.astype(jnp.bfloat16).T
        for i in range(8):
            at = pl.ds(i * rows, rows)
            kept_ref[k, at, :] = turned_ref[pl.ds(pl.multiple_of(info_ref[4 + i] * rows, 16), rows), :]
            sent_ref[k, at, :] = turned_ref[pl.ds(pl.multiple_of(info_ref[12 + i] * rows, 16), rows), :]


def down(a, b):
    return lax.dot_general(a, b, (((0,), (0,)), ((), ())), preferred_element_type=jnp.float32)


def across(a, b):
    return lax.dot_general(a, b, (((1,), (1,)), ((), ())), preferred_element_type=jnp.float32)


def products_kernel(place_ref, *refs):
    tiles, pieces = refs[:4], refs[4:12]
    kept_ref, sent_ref, full_ref, tile_ref, x_ref, w_ref, sems, out_sem = refs[12:]
    tile = tiles[0].shape[2]
    part = w_ref.shape[1] // 4
    copies = []
    for i, piece in enumerate(pieces):
        rows = pl.ds(pl.multiple_of(place_ref[i] * piece.shape[0], 16), piece.shape[0])
        copies.append(pltpu.make_async_copy(piece, w_ref.at[rows, :], sems.at[i]))
    for j, source in enumerate(tiles):
        copies.append(pltpu.make_async_copy(source, tile_ref.at[j], sems.at[8 + j]))
    for copy in copies[8:] + copies[:8]:
        copy.start()
    for j, at in enumerate((0, 2, 1, 3)):
        copies[8 + j].wait()
        for kind in range(2):
            x_ref[kind, pl.ds(at * tile, tile), :] = tile_ref[j, kind].T
    for copy in copies[:8]:
        copy.wait()
    out_copy = pltpu.make_async_copy(w_ref, full_ref, out_sem)
    out_copy.start()
    for n in range(4):
        cols = pl.ds(n * part, part)
        product = jnp.dot(x_ref[n // 3], w_ref[:, cols], preferred_element_type=jnp.float32)
        kept_ref[:, cols] = product[: 2 * tile].astype(jnp.bfloat16)
        sent_ref[:, cols] = product[2 * tile :].astype(jnp.bfloat16)
    out_copy.wait()


def attention_kernel(area, head, kept_ref, came_ref, bias_ref, grad_ref, qkv_ref, scores_ref, toward_ref, probs_ref, back_ref):
    part = grad_ref.shape[1] // 4
    levels, pairs = bias_ref.shape[:2]
    scale = 1.0 / math.sqrt(head)
    lane = lax.broadcasted_iota(jnp.int32, (area, 2 * head), 1)
    left = lane < head

    def stacked(pair):
        zero = jnp.zeros_like(pair)
        return jnp.concatenate([jnp.where(left, pair, zero), jnp.where(left, zero, pair)], axis=0)

    def unstacked(product):
        return jnp.where(left, product[:area], product[area:]).astype(jnp.bfloat16)

    windows = grad_ref.shape[0] // area
    groups = [(w * pairs + p, w, p) for w in range(windows) for p in range(pairs)]

    def view(w, p, n):
        return pl.ds(w * area, area), pl.ds(n * part + p * 2 * head, 2 * head)

    qkv_ref[...] = (kept_ref[...].astype(jnp.float32) + came_ref[...].astype(jnp.float32)).astype(jnp.bfloat16)
    for g, w, p in groups:
        scores_ref[g] = across(stacked(qkv_ref[view(w, p, 0)]), qkv_ref[view(w, p, 1)])
        toward_ref[g] = across(stacked(qkv_ref[view(w, p, 3)]), qkv_ref[view(w, p, 2)])
    for g, w, p in groups:
        scores = scores_ref[g] * scale + bias_ref[w % levels, p]
        expo = jnp.exp(scores - jnp.max(scores, axis=-1, keepdims=True))
        probs = expo / jnp.sum(expo, axis=-1, keepdims=True)
        grad_probs = toward_ref[g]
        inner = jnp.sum(probs * grad_probs, axis=-1, keepdims=True)
        probs_ref[g] = probs.astype(jnp.bfloat16)
        back_ref[g] = (probs * (grad_probs - inner) * scale).astype(jnp.bfloat16)
    for g, w, p in groups:
        probs_b, grad_scores = probs_ref[g], back_ref[g]
        grad_ref[view(w, p, 3)] = unstacked(
            jnp.dot(probs_b, qkv_ref[view(w, p, 2)], preferred_element_type=jnp.float32)
        )
        grad_ref[view(w, p, 0)] = unstacked(
            jnp.dot(grad_scores, qkv_ref[view(w, p, 1)], preferred_element_type=jnp.float32)
        )
        grad_ref[view(w, p, 2)] = down(probs_b, stacked(qkv_ref[view(w, p, 3)])).astype(jnp.bfloat16)
        grad_ref[view(w, p, 1)] = down(grad_scores, stacked(qkv_ref[view(w, p, 0)])).astype(jnp.bfloat16)


def weights_kernel(near_ref, *refs):
    tiles, (own_ref, other_ref), out_refs = refs[:4], refs[4:6], refs[6:14]
    tile_ref, sum_ref, sems = refs[14:]
    tile = tiles[0].shape[2]
    part = own_ref.shape[1] // 4
    rows = out_refs[0].shape[0]
    copies = [pltpu.make_async_copy(source, tile_ref.at[j], sems.at[j]) for j, source in enumerate(tiles)]
    for copy in copies:
        copy.start()
    for copy in copies:
        copy.wait()
    for n in range(4):
        cols = pl.ds(n * part, part)
        total = None
        for t in range(2):
            tokens = pl.ds(t * tile, tile)
            left = jnp.concatenate([tile_ref[2 * t, n // 3], tile_ref[2 * t + 1, n // 3]], axis=1)
            right = jnp.concatenate([own_ref[tokens, cols], other_ref[tokens, cols]], axis=0)
            product = jnp.dot(left, right, preferred_element_type=jnp.float32)
            total = product if total is None else total + product
        sum_ref[:, cols] = total.astype(jnp.bfloat16)
    near = near_ref[0]
    for i, out_ref in enumerate(out_refs):
        wanted = 1 - near if i % 2 == 0 else near
        out_ref[...] = sum_ref[pl.ds(pl.multiple_of((i // 2 * 2 + wanted) * rows, 16), rows), :]


def outer_kernel(place_ref, grad_ref, mine_ref, theirs_ref, own_ref, other_ref, w_ref, sems):
    tile = own_ref.shape[0]
    width = w_ref.shape[0]
    rows = width // 16
    part = w_ref.shape[1] // 4
    step = width // 4
    copies = []
    for i in range(16):
        source = (mine_ref if i < 8 else theirs_ref).at[pl.ds(i % 8 * rows, rows), :]
        into = w_ref.at[pl.ds(pl.multiple_of(place_ref[i] * rows, 16), rows), :]
        copies.append(pltpu.make_async_copy(source, into, sems.at[i]))
    for copy in copies:
        copy.start()
    for copy in copies:
        copy.wait()
    for n in range(4):
        at = pl.ds(n * step, step)
        for k, w_cols in enumerate((pl.ds(3 * part, part), pl.ds(0, 3 * part))):
            product = across(grad_ref[:, w_cols], w_ref[at, w_cols])
            cols = pl.ds(k * width + n * step, step)
            own_ref[:, cols] = product[:tile]
            other_ref[:, cols] = product[tile:].astype(jnp.bfloat16)


def after(value, earlier):
    return lax.optimization_barrier((value, earlier))[0]


def kernel_call(body, outs, in_specs, out_specs, scratch, flops, moved, name, room=58):
    return pl.pallas_call(
        body,
        out_shape=outs,
        in_specs=in_specs,
        out_specs=out_specs,
        scratch_shapes=scratch,
        compiler_params=pltpu.CompilerParams(vmem_limit_bytes=room * 1024 * 1024),
        cost_estimate=pl.CostEstimate(flops=flops, bytes_accessed=moved, transcendentals=0),
        name=name,
    )


def on_device(tokens, land, surface, gain, weights, shifts, index_table, bias_table, cotangent):
    levels, side, _, width = tokens.shape
    area = side * side
    tile = levels * area
    heads = bias_table.shape[2]
    entries = bias_table.shape[1]
    own_rows = weights.shape[0]
    part = weights.shape[1] // 8
    head = weights.shape[1] // 4 // heads
    own_heads = heads // 2
    far, near, beside, core = (lax.axis_index(axis) for axis in LON)
    grp = lax.axis_index("grp")
    first = near == 0
    f32 = jnp.float32

    def place(f, n, s, c):
        return ((far ^ f) * 4 + (near ^ n) * 2 + (beside ^ s)) * 2 + (core ^ c)

    low = jnp.concatenate([weights[:, 2 * k * part : (2 * k + 1) * part] for k in range(4)], axis=1)
    high = jnp.concatenate([weights[:, (2 * k + 1) * part : (2 * k + 2) * part] for k in range(4)], axis=1)
    mine = jnp.where(first, low, high)
    came = swap(jnp.where(first, high, low), "near")
    flat_cot = cotangent.reshape(tile, width)
    surface_term = jnp.where(land[None, :, :, None] == 1, surface[1], surface[0])
    stream = (tokens.astype(f32) + surface_term).astype(jnp.bfloat16).reshape(tile, width)
    values = stream.astype(f32)
    center = values - jnp.mean(values, axis=-1, keepdims=True)
    spread = lax.rsqrt(jnp.mean(center * center, axis=-1, keepdims=True) + epsilon)

    held = near ^ grp
    half_piece = jnp.where(grp == 0, mine, came)
    across_far = swap(half_piece, "far")
    order = [(f, s, n) for f in (1, 0) for s in (1, 0) for n in (0, 1)]
    natural = [place(f, near ^ n, s, c) for c in (0, 1) for f, s, n in order]

    vmem = pl.BlockSpec(memory_space=pltpu.VMEM)
    smem = pl.BlockSpec(memory_space=pltpu.SMEM)
    anywhere = pl.BlockSpec(memory_space=pl.ANY)
    dma = pltpu.SemaphoreType.DMA

    rows, below, below_cot = shifts[:, 0], stream, flat_cot
    if lax.axis_size("lat") > 1:
        zeros = jnp.zeros_like(rows)
        onehot_rows = pick(rows, zeros, levels, side, True)
        below = picked(onehot_rows, stream, along_lat(stream, -1))
        below_cot = picked(onehot_rows, flat_cot, along_lat(flat_cot, -1))
        rows = zeros
    moved, moved_cot = along_lon(below, -1), along_lon(below_cot, -1)
    info = jnp.concatenate(
        [jnp.stack([rows, shifts[:, 1]], axis=1).reshape(-1), jnp.stack(natural)]
    ).astype(jnp.int32)
    half = width // 2
    turned = jax.ShapeDtypeStruct((2, half, tile), jnp.bfloat16)
    own_turned, sent_turned = kernel_call(
        turned_rolls,
        (turned, turned),
        [smem, vmem] + [anywhere] * 4,
        (vmem, vmem),
        [
            pltpu.VMEM((2, 2 * tile, width), jnp.bfloat16),
            pltpu.VMEM((width, tile), jnp.bfloat16),
            dma((4,)),
        ],
        2 * 2 * 2 * tile * tile * width,
        3_000_000,
        "turned_rolls",
        24,
    )(info, gain.reshape(1, -1), below, moved, below_cot, moved_cot)
    mine_side = swap(after(mine, (moved, moved_cot)), "side")
    across_far = after(across_far, mine_side)
    far_side, far_grp = swap(across_far, "side"), swap(across_far, "grp")
    came_side = swap(after(came, far_grp), "side")
    pieces = [
        (mine, 0, 0, near),
        (came, 0, 0, 1 - near),
        (mine_side, 0, 1, near),
        (came_side, 0, 1, 1 - near),
        (across_far, 1, 0, held),
        (far_grp, 1, 0, 1 - held),
        (far_side, 1, 1, held),
        (swap(far_side, "grp"), 1, 1, 1 - held),
    ]
    places = jnp.stack([(1 - f) * 4 + (1 - s) * 2 + n for _, f, s, n in pieces]).astype(jnp.int32)
    own_near, sent_near = swap(own_turned, "near"), swap(sent_turned, "near")
    tiles = [own_turned, swap(after(sent_turned, (sent_near, far_grp)), "core"), own_near, swap(after(sent_near, far_grp), "core")]

    onehot = (index_table[:, :, None] == jnp.arange(entries, dtype=jnp.int32)).astype(f32)
    own_table = lax.dynamic_slice_in_dim(bias_table, near * own_heads, own_heads, 2)
    bias = jnp.einsum("qkr,lrh->lhqk", onehot, own_table, precision=lax.Precision.HIGHEST)
    row_number = lax.axis_index("lat") * side + jnp.arange(side, dtype=jnp.int32)
    group = row_number[None, :] >= (side * lax.axis_size("lat") - shifts[:, 0])[:, None]
    group = jnp.repeat(group, side, axis=1)
    allowed = group[:, :, None] == group[:, None, :]
    bias = jnp.where(allowed[:, None], bias, -1e30).reshape(levels, own_heads // 2, 2 * area, area)

    bf16 = jnp.bfloat16
    kept, sent, w_mine = kernel_call(
        products_kernel,
        (
            jax.ShapeDtypeStruct((2 * tile, 4 * part), bf16),
            jax.ShapeDtypeStruct((2 * tile, 4 * part), bf16),
            jax.ShapeDtypeStruct((half, 4 * part), bf16),
        ),
        [smem] + [anywhere] * 12,
        (vmem, vmem, anywhere),
        [
            pltpu.VMEM((4, 2, half, tile), bf16),
            pltpu.VMEM((2, 4 * tile, half), bf16),
            pltpu.VMEM((half, 4 * part), bf16),
            dma((12,)),
            dma,
        ],
        1_200_000_000,
        9_000_000,
        "products",
    )(after(places, bias), *tiles, *[piece for piece, *_ in pieces])
    crossed = swap(sent, "core")
    grad = kernel_call(
        functools.partial(attention_kernel, area, head),
        jax.ShapeDtypeStruct((2 * tile, 4 * part), bf16),
        [vmem] * 3,
        vmem,
        [pltpu.VMEM((2 * tile, 4 * part), bf16)]
        + [pltpu.VMEM((2 * tile // area * own_heads // 2, 2 * area, area), kind) for kind in (f32, f32, bf16, bf16)],
        1_000_000_000,
        4_000_000,
        "attention",
    )(kept, crossed, bias)
    w_theirs = swap(after(w_mine, crossed), "core")
    grad_theirs = swap(grad, "core")
    attended_own, attended_other = kernel_call(
        outer_kernel,
        (
            jax.ShapeDtypeStruct((tile, 2 * width), f32),
            jax.ShapeDtypeStruct((tile, 2 * width), bf16),
        ),
        [smem, vmem, anywhere, anywhere],
        (vmem, vmem),
        [pltpu.VMEM((width, 4 * part), bf16), dma((16,))],
        1_200_000_000,
        8_000_000,
        "projections",
        24,
    )(jnp.stack(natural).astype(jnp.int32), grad, w_mine, w_theirs)
    blocks = kernel_call(
        weights_kernel,
        [jax.ShapeDtypeStruct((own_rows, 4 * part), bf16)] * 8,
        [smem] + [anywhere] * 4 + [vmem] * 2,
        [vmem] * 8,
        [
            pltpu.VMEM((4, 2, half, tile), bf16),
            pltpu.VMEM((half, 4 * part), bf16),
            dma((4,)),
        ],
        1_200_000_000,
        6_000_000,
        "weight_gradient",
        24,
    )(after(near.astype(jnp.int32).reshape(1), attended_other), *tiles, grad, grad_theirs)

    def block(f, s, n):
        return blocks[((1 - f) * 2 + 1 - s) * 2 + 1 - n]

    side_far_1 = swap(block(1, 1, 1), "side")
    arrived_back = swap(attended_other, "near")
    side_far_0 = swap(after(block(1, 1, 0), side_far_1), "side")
    far_1 = swap((block(1, 0, 1).astype(f32) + side_far_1.astype(f32)).astype(bf16), "far")
    far_0 = swap(after((block(1, 0, 0).astype(f32) + side_far_0.astype(f32)).astype(bf16), (far_1, arrived_back)), "far")
    side_1 = swap(after(block(0, 1, 1), side_far_0), "side")
    side_0 = swap(after(block(0, 1, 0), side_1), "side")
    total_1 = (block(0, 0, 1).astype(f32) + side_1.astype(f32) + far_1.astype(f32)).astype(bf16)
    theirs = swap(total_1, "near")

    back = (attended_own + arrived_back.astype(f32)).astype(jnp.bfloat16)
    back = roll_back(back, shifts, levels, side, far_1)
    theirs = after(theirs, back).astype(f32)
    back = after(back, (far_0, theirs))
    output = (values + back[:, :width].astype(f32)).astype(jnp.bfloat16)
    scaled = center * spread
    upstream = back[:, width:].astype(f32) * gain
    grad_stream = spread * (
        upstream
        - jnp.mean(upstream, axis=-1, keepdims=True)
        - scaled * jnp.mean(upstream * scaled, axis=-1, keepdims=True)
    )
    grad_tokens = (flat_cot.astype(f32) + grad_stream).astype(jnp.bfloat16)

    far_0 = after(far_0, (output, grad_tokens))
    total_0 = block(0, 0, 0).astype(f32) + side_0.astype(f32) + far_0.astype(f32)
    token_count = tile * lax.axis_size("lat") * math.prod(lax.axis_size(axis) for axis in LON)
    columns = []
    for k in range(4):
        cols = slice(k * part, (k + 1) * part)
        columns += [
            jnp.where(first, total_0[:, cols], theirs[:, cols]),
            jnp.where(first, theirs[:, cols], total_0[:, cols]),
        ]
    summed = jnp.concatenate(columns, axis=1)
    if lax.axis_size("lat") > 1:
        summed = lax.psum(summed.astype(jnp.bfloat16), "lat").astype(f32)
    grad_weights = summed * (1.0 / math.sqrt(token_count))
    return (output.reshape(tokens.shape), grad_tokens.reshape(tokens.shape), grad_weights)


def solution(mesh):
    sizes = dict(mesh.shape)
    devices = mesh.devices.reshape(sizes["grp"], sizes["lon"] // 8, 2, 2, 2, sizes["lat"])
    finer = Mesh(devices, ("grp",) + LON + ("lat",))
    return jax.shard_map(
        on_device,
        mesh=finer,
        in_specs=(
            P("grp", "lat", LON, None),
            P(("grp", "lat"), LON),
            P(),
            P(),
            P(LON, None),
            P(),
            P(),
            P("lat", None, None),
            P("grp", "lat", LON, None),
        ),
        out_specs=(
            P("grp", "lat", LON, None),
            P("grp", "lat", LON, None),
            P(("grp",) + LON, None),
        ),
        check_vma=False,
    )
```

```python
import functools
import math

import jax
import jax.numpy as jnp
from jax import lax
from jax.experimental import pallas as pl
from jax.experimental.pallas import tpu as pltpu
from jax.sharding import Mesh
from jax.sharding import PartitionSpec as P

epsilon = 1e-05
LON = ("far", "near", "side", "core")


def along_lon(shard, by):
    count = math.prod(lax.axis_size(axis) for axis in LON)
    return lax.ppermute(shard, LON, [(i, (i + by) % count) for i in range(count)])


def along_lat(shard, by):
    count = lax.axis_size("lat")
    return lax.ppermute(shard, "lat", [(i, (i + by) % count) for i in range(count)])


def swap(shard, axis):
    return lax.ppermute(shard, axis, [(0, 1), (1, 0)])


def pick(rows, cols, levels, side, over_rows):
    tile = levels * side * side
    shape = (tile, 2 * tile)
    target = lax.broadcasted_iota(jnp.int32, shape, 0)
    source = lax.broadcasted_iota(jnp.int32, shape, 1)
    level = target // (side * side)
    row = target // side % side
    col = target % side
    from_row = jnp.full_like(row, rows[levels - 1])
    from_col = jnp.full_like(col, cols[levels - 1])
    for l in range(levels - 1):
        from_row = jnp.where(level == l, rows[l], from_row)
        from_col = jnp.where(level == l, cols[l], from_col)
    from_row = row + from_row
    from_col = col + from_col
    which = (from_row if over_rows else from_col) // side
    wanted = which * tile + level * side * side + from_row % side * side + from_col % side
    return (source == wanted).astype(jnp.bfloat16)


def picked(onehot, first, second):
    both = jnp.concatenate([first, second], axis=0)
    return jnp.dot(onehot, both, preferred_element_type=jnp.float32).astype(jnp.bfloat16)


def roll_back(field, shifts, levels, side, wait):
    zeros = jnp.zeros_like(shifts[:, 0])
    rows = side - shifts[:, 0]
    more = lax.axis_size("lat") > 1
    field = picked(
        pick(zeros if more else rows, side - shifts[:, 1], levels, side, False),
        after(along_lon(field, 1), wait),
        field,
    )
    if more:
        field = picked(pick(rows, zeros, levels, side, True), along_lat(field, 1), field)
    return field


def turned_rolls(info_ref, gain_ref, *refs):
    fields, (kept_ref, sent_ref, both_ref, turned_ref, sems) = refs[:4], refs[4:]
    tile = fields[0].shape[0]
    rows = kept_ref.shape[1] // 8
    levels, side = 2, 8
    area = tile // levels
    copies = [
        pltpu.make_async_copy(field, both_ref.at[i // 2, pl.ds(i % 2 * tile, tile), :], sems.at[i])
        for i, field in enumerate(fields)
    ]
    for copy in copies:
        copy.start()
    target = lax.broadcasted_iota(jnp.int32, (tile, 2 * tile), 0)
    source = lax.broadcasted_iota(jnp.int32, (tile, 2 * tile), 1)
    upper = target < area
    row = ((target >> 3) & 7) + jnp.where(upper, info_ref[0], info_ref[2])
    col = (target & 7) + jnp.where(upper, info_ref[1], info_ref[3])
    wanted = jnp.where(col >= side, tile, 0) + jnp.where(upper, 0, area) + (row & 7) * side + (col & 7)
    onehot = jnp.where(source == wanted, 1.0, 0.0).astype(jnp.bfloat16)
    for k in (1, 0):
        copies[2 * k].wait()
        copies[2 * k + 1].wait()
        rolled = jnp.dot(onehot, both_ref[k], preferred_element_type=jnp.float32)
        if k == 0:
            center = rolled - jnp.mean(rolled, axis=-1, keepdims=True)
            spread = lax.rsqrt(jnp.mean(center * center, axis=-1, keepdims=True) + epsilon)
            rolled = center * spread * gain_ref[...]
        turned_ref[...] = rolled.astype(jnp.bfloat16).T
        for i in range(8):
            at = pl.ds(i * rows, rows)
            kept_ref[k, at, :] = turned_ref[pl.ds(pl.multiple_of(info_ref[4 + i] * rows, 16), rows), :]
            sent_ref[k, at, :] = turned_ref[pl.ds(pl.multiple_of(info_ref[12 + i] * rows, 16), rows), :]


def down(a, b):
    return lax.dot_general(a, b, (((0,), (0,)), ((), ())), preferred_element_type=jnp.float32)


def across(a, b):
    return lax.dot_general(a, b, (((1,), (1,)), ((), ())), preferred_element_type=jnp.float32)


def products_kernel(place_ref, *refs):
    tiles, pieces = refs[:4], refs[4:12]
    kept_ref, sent_ref, full_ref, tile_ref, x_ref, w_ref, sems, out_sem = refs[12:]
    tile = tiles[0].shape[2]
    part = w_ref.shape[1] // 4
    copies = []
    for i, piece in enumerate(pieces):
        rows = pl.ds(pl.multiple_of(place_ref[i] * piece.shape[0], 16), piece.shape[0])
        copies.append(pltpu.make_async_copy(piece, w_ref.at[rows, :], sems.at[i]))
    for j, source in enumerate(tiles):
        copies.append(pltpu.make_async_copy(source, tile_ref.at[j], sems.at[8 + j]))
    for copy in copies[8:] + copies[:8]:
        copy.start()
    for j, at in enumerate((0, 2, 1, 3)):
        copies[8 + j].wait()
        for kind in range(2):
            x_ref[kind, pl.ds(at * tile, tile), :] = tile_ref[j, kind].T
    for copy in copies[:8]:
        copy.wait()
    out_copy = pltpu.make_async_copy(w_ref, full_ref, out_sem)
    out_copy.start()
    for n in range(4):
        cols = pl.ds(n * part, part)
        product = jnp.dot(x_ref[n // 3], w_ref[:, cols], preferred_element_type=jnp.float32)
        kept_ref[:, cols] = product[: 2 * tile].astype(jnp.bfloat16)
        sent_ref[:, cols] = product[2 * tile :].astype(jnp.bfloat16)
    out_copy.wait()


def attention_kernel(area, head, kept_ref, came_ref, bias_ref, grad_ref, qkv_ref, scores_ref, toward_ref, probs_ref, back_ref):
    part = grad_ref.shape[1] // 4
    levels, pairs = bias_ref.shape[:2]
    scale = 1.0 / math.sqrt(head)
    lane = lax.broadcasted_iota(jnp.int32, (area, 2 * head), 1)
    left = lane < head

    def stacked(pair):
        zero = jnp.zeros_like(pair)
        return jnp.concatenate([jnp.where(left, pair, zero), jnp.where(left, zero, pair)], axis=0)

    def unstacked(product):
        return jnp.where(left, product[:area], product[area:]).astype(jnp.bfloat16)

    windows = grad_ref.shape[0] // area
    groups = [(w * pairs + p, w, p) for w in range(windows) for p in range(pairs)]

    def view(w, p, n):
        return pl.ds(w * area, area), pl.ds(n * part + p * 2 * head, 2 * head)

    qkv_ref[...] = (kept_ref[...].astype(jnp.float32) + came_ref[...].astype(jnp.float32)).astype(jnp.bfloat16)
    for g, w, p in groups:
        scores_ref[g] = across(stacked(qkv_ref[view(w, p, 0)]), qkv_ref[view(w, p, 1)])
        toward_ref[g] = across(stacked(qkv_ref[view(w, p, 3)]), qkv_ref[view(w, p, 2)])
    for g, w, p in groups:
        scores = scores_ref[g] * scale + bias_ref[w % levels, p]
        expo = jnp.exp(scores - jnp.max(scores, axis=-1, keepdims=True))
        probs = expo / jnp.sum(expo, axis=-1, keepdims=True)
        grad_probs = toward_ref[g]
        inner = jnp.sum(probs * grad_probs, axis=-1, keepdims=True)
        probs_ref[g] = probs.astype(jnp.bfloat16)
        back_ref[g] = (probs * (grad_probs - inner) * scale).astype(jnp.bfloat16)
    for g, w, p in groups:
        probs_b, grad_scores = probs_ref[g], back_ref[g]
        grad_ref[view(w, p, 3)] = unstacked(
            jnp.dot(probs_b, qkv_ref[view(w, p, 2)], preferred_element_type=jnp.float32)
        )
        grad_ref[view(w, p, 0)] = unstacked(
            jnp.dot(grad_scores, qkv_ref[view(w, p, 1)], preferred_element_type=jnp.float32)
        )
        grad_ref[view(w, p, 2)] = down(probs_b, stacked(qkv_ref[view(w, p, 3)])).astype(jnp.bfloat16)
        grad_ref[view(w, p, 1)] = down(grad_scores, stacked(qkv_ref[view(w, p, 0)])).astype(jnp.bfloat16)


def weights_kernel(near_ref, *refs):
    tiles, (own_ref, other_ref), out_refs = refs[:4], refs[4:6], refs[6:14]
    tile_ref, sum_ref, sems = refs[14:]
    tile = tiles[0].shape[2]
    part = own_ref.shape[1] // 4
    rows = out_refs[0].shape[0]
    copies = [pltpu.make_async_copy(source, tile_ref.at[j], sems.at[j]) for j, source in enumerate(tiles)]
    for copy in copies:
        copy.start()
    for copy in copies:
        copy.wait()
    for n in range(4):
        cols = pl.ds(n * part, part)
        total = None
        for t in range(2):
            tokens = pl.ds(t * tile, tile)
            left = jnp.concatenate([tile_ref[2 * t, n // 3], tile_ref[2 * t + 1, n // 3]], axis=1)
            right = jnp.concatenate([own_ref[tokens, cols], other_ref[tokens, cols]], axis=0)
            product = jnp.dot(left, right, preferred_element_type=jnp.float32)
            total = product if total is None else total + product
        sum_ref[:, cols] = total.astype(jnp.bfloat16)
    near = near_ref[0]
    for i, out_ref in enumerate(out_refs):
        wanted = 1 - near if i % 2 == 0 else near
        out_ref[...] = sum_ref[pl.ds(pl.multiple_of((i // 2 * 2 + wanted) * rows, 16), rows), :]


def outer_kernel(place_ref, grad_ref, mine_ref, theirs_ref, own_ref, other_ref, w_ref, sems):
    tile = own_ref.shape[0]
    width = w_ref.shape[0]
    rows = width // 16
    part = w_ref.shape[1] // 4
    step = width // 4
    copies = []
    for i in range(16):
        source = (mine_ref if i < 8 else theirs_ref).at[pl.ds(i % 8 * rows, rows), :]
        into = w_ref.at[pl.ds(pl.multiple_of(place_ref[i] * rows, 16), rows), :]
        copies.append(pltpu.make_async_copy(source, into, sems.at[i]))
    for copy in copies:
        copy.start()
    for copy in copies:
        copy.wait()
    for n in range(4):
        at = pl.ds(n * step, step)
        for k, w_cols in enumerate((pl.ds(3 * part, part), pl.ds(0, 3 * part))):
            product = across(grad_ref[:, w_cols], w_ref[at, w_cols])
            cols = pl.ds(k * width + n * step, step)
            own_ref[:, cols] = product[:tile]
            other_ref[:, cols] = product[tile:].astype(jnp.bfloat16)


def after(value, earlier):
    return lax.optimization_barrier((value, earlier))[0]


def kernel_call(body, outs, in_specs, out_specs, scratch, flops, moved, name, room=58):
    return pl.pallas_call(
        body,
        out_shape=outs,
        in_specs=in_specs,
        out_specs=out_specs,
        scratch_shapes=scratch,
        compiler_params=pltpu.CompilerParams(vmem_limit_bytes=room * 1024 * 1024),
        cost_estimate=pl.CostEstimate(flops=flops, bytes_accessed=moved, transcendentals=0),
        name=name,
    )


def on_device(tokens, land, surface, gain, weights, shifts, index_table, bias_table, cotangent):
    levels, side, _, width = tokens.shape
    area = side * side
    tile = levels * area
    heads = bias_table.shape[2]
    entries = bias_table.shape[1]
    own_rows = weights.shape[0]
    part = weights.shape[1] // 8
    head = weights.shape[1] // 4 // heads
    own_heads = heads // 2
    far, near, beside, core = (lax.axis_index(axis) for axis in LON)
    grp = lax.axis_index("grp")
    first = near == 0
    f32 = jnp.float32

    def place(f, n, s, c):
        return ((far ^ f) * 4 + (near ^ n) * 2 + (beside ^ s)) * 2 + (core ^ c)

    low = jnp.concatenate([weights[:, 2 * k * part : (2 * k + 1) * part] for k in range(4)], axis=1)
    high = jnp.concatenate([weights[:, (2 * k + 1) * part : (2 * k + 2) * part] for k in range(4)], axis=1)
    mine = jnp.where(first, low, high)
    came = swap(jnp.where(first, high, low), "near")
    flat_cot = cotangent.reshape(tile, width)
    surface_term = jnp.where(land[None, :, :, None] == 1, surface[1], surface[0])
    stream = (tokens.astype(f32) + surface_term).astype(jnp.bfloat16).reshape(tile, width)
    values = stream.astype(f32)
    center = values - jnp.mean(values, axis=-1, keepdims=True)
    spread = lax.rsqrt(jnp.mean(center * center, axis=-1, keepdims=True) + epsilon)

    held = near ^ grp
    half_piece = jnp.where(grp == 0, mine, came)
    across_far = swap(half_piece, "far")
    order = [(f, s, n) for f in (1, 0) for s in (1, 0) for n in (0, 1)]
    natural = [place(f, near ^ n, s, c) for c in (0, 1) for f, s, n in order]

    vmem = pl.BlockSpec(memory_space=pltpu.VMEM)
    smem = pl.BlockSpec(memory_space=pltpu.SMEM)
    anywhere = pl.BlockSpec(memory_space=pl.ANY)
    dma = pltpu.SemaphoreType.DMA

    rows, below, below_cot = shifts[:, 0], stream, flat_cot
    if lax.axis_size("lat") > 1:
        zeros = jnp.zeros_like(rows)
        onehot_rows = pick(rows, zeros, levels, side, True)
        below = picked(onehot_rows, stream, along_lat(stream, -1))
        below_cot = picked(onehot_rows, flat_cot, along_lat(flat_cot, -1))
        rows = zeros
    moved, moved_cot = along_lon(below, -1), along_lon(below_cot, -1)
    info = jnp.concatenate(
        [jnp.stack([rows, shifts[:, 1]], axis=1).reshape(-1), jnp.stack(natural)]
    ).astype(jnp.int32)
    half = width // 2
    turned = jax.ShapeDtypeStruct((2, half, tile), jnp.bfloat16)
    own_turned, sent_turned = kernel_call(
        turned_rolls,
        (turned, turned),
        [smem, vmem] + [anywhere] * 4,
        (vmem, vmem),
        [
            pltpu.VMEM((2, 2 * tile, width), jnp.bfloat16),
            pltpu.VMEM((width, tile), jnp.bfloat16),
            dma((4,)),
        ],
        2 * 2 * 2 * tile * tile * width,
        3_000_000,
        "turned_rolls",
        24,
    )(info, gain.reshape(1, -1), below, moved, below_cot, moved_cot)
    mine_side = swap(after(mine, (moved, moved_cot)), "side")
    across_far = after(across_far, mine_side)
    far_side, far_grp = swap(across_far, "side"), swap(across_far, "grp")
    came_side = swap(after(came, far_grp), "side")
    pieces = [
        (mine, 0, 0, near),
        (came, 0, 0, 1 - near),
        (mine_side, 0, 1, near),
        (came_side, 0, 1, 1 - near),
        (across_far, 1, 0, held),
        (far_grp, 1, 0, 1 - held),
        (far_side, 1, 1, held),
        (swap(far_side, "grp"), 1, 1, 1 - held),
    ]
    places = jnp.stack([(1 - f) * 4 + (1 - s) * 2 + n for _, f, s, n in pieces]).astype(jnp.int32)
    own_near, sent_near = swap(own_turned, "near"), swap(sent_turned, "near")
    tiles = [own_turned, swap(after(sent_turned, (sent_near, far_grp)), "core"), own_near, swap(after(sent_near, far_grp), "core")]

    onehot = (index_table[:, :, None] == jnp.arange(entries, dtype=jnp.int32)).astype(f32)
    own_table = lax.dynamic_slice_in_dim(bias_table, near * own_heads, own_heads, 2)
    bias = jnp.einsum("qkr,lrh->lhqk", onehot, own_table, precision=lax.Precision.HIGHEST)
    row_number = lax.axis_index("lat") * side + jnp.arange(side, dtype=jnp.int32)
    group = row_number[None, :] >= (side * lax.axis_size("lat") - shifts[:, 0])[:, None]
    group = jnp.repeat(group, side, axis=1)
    allowed = group[:, :, None] == group[:, None, :]
    bias = jnp.where(allowed[:, None], bias, -1e30).reshape(levels, own_heads // 2, 2 * area, area)

    bf16 = jnp.bfloat16
    kept, sent, w_mine = kernel_call(
        products_kernel,
        (
            jax.ShapeDtypeStruct((2 * tile, 4 * part), bf16),
            jax.ShapeDtypeStruct((2 * tile, 4 * part), bf16),
            jax.ShapeDtypeStruct((half, 4 * part), bf16),
        ),
        [smem] + [anywhere] * 12,
        (vmem, vmem, anywhere),
        [
            pltpu.VMEM((4, 2, half, tile), bf16),
            pltpu.VMEM((2, 4 * tile, half), bf16),
            pltpu.VMEM((half, 4 * part), bf16),
            dma((12,)),
            dma,
        ],
        1_200_000_000,
        9_000_000,
        "products",
    )(after(places, bias), *tiles, *[piece for piece, *_ in pieces])
    crossed = swap(sent, "core")
    grad = kernel_call(
        functools.partial(attention_kernel, area, head),
        jax.ShapeDtypeStruct((2 * tile, 4 * part), bf16),
        [vmem] * 3,
        vmem,
        [pltpu.VMEM((2 * tile, 4 * part), bf16)]
        + [pltpu.VMEM((2 * tile // area * own_heads // 2, 2 * area, area), kind) for kind in (f32, f32, bf16, bf16)],
        1_000_000_000,
        4_000_000,
        "attention",
    )(kept, crossed, bias)
    w_theirs = swap(after(w_mine, crossed), "core")
    grad_theirs = swap(grad, "core")
    attended_own, attended_other = kernel_call(
        outer_kernel,
        (
            jax.ShapeDtypeStruct((tile, 2 * width), f32),
            jax.ShapeDtypeStruct((tile, 2 * width), bf16),
        ),
        [smem, vmem, anywhere, anywhere],
        (vmem, vmem),
        [pltpu.VMEM((width, 4 * part), bf16), dma((16,))],
        1_200_000_000,
        8_000_000,
        "projections",
        24,
    )(jnp.stack(natural).astype(jnp.int32), grad, w_mine, w_theirs)
    blocks = kernel_call(
        weights_kernel,
        [jax.ShapeDtypeStruct((own_rows, 4 * part), bf16)] * 8,
        [smem] + [anywhere] * 4 + [vmem] * 2,
        [vmem] * 8,
        [
            pltpu.VMEM((4, 2, half, tile), bf16),
            pltpu.VMEM((half, 4 * part), bf16),
            dma((4,)),
        ],
        1_200_000_000,
        6_000_000,
        "weight_gradient",
        24,
    )(after(near.astype(jnp.int32).reshape(1), attended_other), *tiles, grad, grad_theirs)

    def block(f, s, n):
        return blocks[((1 - f) * 2 + 1 - s) * 2 + 1 - n]

    side_far_1 = swap(block(1, 1, 1), "side")
    arrived_back = swap(attended_other, "near")
    side_far_0 = swap(after(block(1, 1, 0), side_far_1), "side")
    far_1 = swap((block(1, 0, 1).astype(f32) + side_far_1.astype(f32)).astype(bf16), "far")
    far_0 = swap(after((block(1, 0, 0).astype(f32) + side_far_0.astype(f32)).astype(bf16), (far_1, arrived_back)), "far")
    side_1 = swap(after(block(0, 1, 1), side_far_0), "side")
    side_0 = swap(after(block(0, 1, 0), side_1), "side")
    total_1 = (block(0, 0, 1).astype(f32) + side_1.astype(f32) + far_1.astype(f32)).astype(bf16)
    theirs = swap(total_1, "near").astype(f32)

    back = (attended_own + arrived_back.astype(f32)).astype(jnp.bfloat16)
    back = after(roll_back(back, shifts, levels, side, far_1), far_0)
    output = (values + back[:, :width].astype(f32)).astype(jnp.bfloat16)
    scaled = center * spread
    upstream = back[:, width:].astype(f32) * gain
    grad_stream = spread * (
        upstream
        - jnp.mean(upstream, axis=-1, keepdims=True)
        - scaled * jnp.mean(upstream * scaled, axis=-1, keepdims=True)
    )
    grad_tokens = (flat_cot.astype(f32) + grad_stream).astype(jnp.bfloat16)

    far_0 = after(far_0, (output, grad_tokens))
    total_0 = block(0, 0, 0).astype(f32) + side_0.astype(f32) + far_0.astype(f32)
    token_count = tile * lax.axis_size("lat") * math.prod(lax.axis_size(axis) for axis in LON)
    columns = []
    for k in range(4):
        cols = slice(k * part, (k + 1) * part)
        columns += [
            jnp.where(first, total_0[:, cols], theirs[:, cols]),
            jnp.where(first, theirs[:, cols], total_0[:, cols]),
        ]
    summed = jnp.concatenate(columns, axis=1)
    if lax.axis_size("lat") > 1:
        summed = lax.psum(summed.astype(jnp.bfloat16), "lat").astype(f32)
    grad_weights = summed * (1.0 / math.sqrt(token_count))
    return (output.reshape(tokens.shape), grad_tokens.reshape(tokens.shape), grad_weights)


def solution(mesh):
    sizes = dict(mesh.shape)
    devices = mesh.devices.reshape(sizes["grp"], sizes["lon"] // 8, 2, 2, 2, sizes["lat"])
    finer = Mesh(devices, ("grp",) + LON + ("lat",))
    return jax.shard_map(
        on_device,
        mesh=finer,
        in_specs=(
            P("grp", "lat", LON, None),
            P(("grp", "lat"), LON),
            P(),
            P(),
            P(LON, None),
            P(),
            P(),
            P("lat", None, None),
            P("grp", "lat", LON, None),
        ),
        out_specs=(
            P("grp", "lat", LON, None),
            P("grp", "lat", LON, None),
            P(("grp",) + LON, None),
        ),
        check_vma=False,
    )
```
